32 devices in a mesh: groups: 2 (over y), ctx: 4 (over z), head: 4 (over x, core).
Axes of the slice: x: 2, y: 2, z: 4, core: 2. Of those that a mesh axis runs over, the one named last changes fastest.
Arguments:
- queries: bfloat16 [4096, 4096], P(('groups', 'ctx'), 'head'), parts along dimension 0, may hold values from -6 to 6
- keys: bfloat16 [4096, 2, 4096], P(('groups', 'ctx'), None, 'head'), parts along dimension 0, may hold values from -6 to 6
- values: bfloat16 [4096, 2, 4096], P(('groups', 'ctx'), None, 'head'), parts along dimension 0, may hold values from -6 to 6
- beta: float32 [2, 32, 4096], P(None, 'head', ('groups', 'ctx')), parts along dimension 2, may hold values from 0 to 2, as said below
- gain: float32 [4096], P('head'), may hold values from 0.5 to 1.5
- w_out: bfloat16 [4096, 4096], P('head', 'ctx'), may hold values from -0.09375 to 0.09375
Outputs:
- mixed: bfloat16 [4096, 4096], P(('groups', 'ctx'), 'head'), parts along dimension 0
The draws below stay inside these ranges and needn't reach their ends.
There are 2 independent parts, one for each index of `groups`. The reference program is written for one: setup_inputs(seed, part) draws one part's arguments, and reference() takes and returns one part's arrays. A program takes and returns all parts, laid end to end along the dimension named above; an argument that names none is the same for every part. Nothing has to cross between parts.
Inputs may be any that keep to these rules, and one draw needn't show every extreme that they name: `beta`: every strength lies in the closed range shown; each head either keeps strengths just under 2 at all tokens or spreads them well inside the range.
All inputs are finite; a program needn't handle non-finite values.
Results may differ from the reference program's by a relative error of at most 0.014.
Values may be sent and summed in bfloat16 or wider, within the bound.
No kernel may reach another device: no remote copies, remote signals or barrier semaphores. Data moves between devices by JAX's collectives and lax.ppermute only.
A program may use at most 128 MiB of HBM per device.

```python
import jax
import jax.numpy as jnp
from jax import lax

D = 4096
H = 32
DK = 128
REFL = 2
TOKENS = 2048
N_HEAD = 4


def draw_beta(key, part):
    first, second, third = jax.random.split(jax.random.fold_in(key, 11), 3)
    share = 0.5
    keeping = jax.random.uniform(first, (1, H, 1), jnp.float32) < share
    near_two = 2.0 - 0.0003 * jax.random.uniform(second, (REFL, H, TOKENS), jnp.float32)
    spread_out = jax.random.uniform(third, (REFL, H, TOKENS), jnp.float32, 0.3, 1.7)
    return jnp.where(keeping, near_two, spread_out)


def levels(key, dims, shards, least, largest):
    factor_of = 1.0
    for axis_at, blocks in shards:
        draws = jax.random.uniform(jax.random.fold_in(jax.random.fold_in(key, 6), axis_at), (blocks,), jnp.float32, least / len(shards), largest / len(shards))
        factor_of = factor_of * jnp.repeat(jnp.exp(draws), dims[axis_at] // blocks).reshape((-1,) + (1,) * (len(dims) - 1 - axis_at))
    return factor_of


def gaussian(stream_key, shape, deviation, bound, shards=(), kind=jnp.bfloat16):
    array = jax.random.normal(stream_key, shape, jnp.float32) * deviation
    if len(shards) > 0:
        array = levels(stream_key, shape, shards, -0.22, 0.18) * array
    return jnp.clip(array, min=-bound, max=bound).astype(kind)


def setup_inputs(seed: int = 0, part: int = 0) -> dict:
    streams_of = jax.random.split(jax.random.key(seed), 7)
    own_keys = jax.random.split(jax.random.fold_in(streams_of[6], part), 7)
    return {
        "queries": gaussian(own_keys[0], (TOKENS, H * DK), 1.0, 6.0, ((0, 4), (1, 4))),
        "keys": gaussian(own_keys[1], (TOKENS, REFL, H * DK), 1.0, 6.0, ((0, 4), (2, 4))),
        "values": gaussian(own_keys[2], (TOKENS, REFL, H * DK), 1.0, 6.0, ((0, 4), (2, 4))),
        "beta": draw_beta(jax.random.fold_in(jax.random.fold_in(streams_of[6], part), 71), part),
        "gain": jnp.clip(1.0 + 0.1 * jax.random.normal(streams_of[4], (H * DK,), jnp.float32), 0.5, 1.5),
        "w_out": gaussian(streams_of[5], (H * DK, D), (H * DK) ** -0.5, 0.09375, ((0, 4), (1, 4))),
    }


def unit_rows(matrix):
    return matrix * lax.rsqrt(lax.optimization_barrier(jnp.sum(matrix * matrix, axis=-1, keepdims=True)) + 1e-06)

def reference(queries, keys, values, beta, gain, w_out):
    highest = lax.Precision.HIGHEST
    query_unit = unit_rows(queries.astype(jnp.float32).reshape(TOKENS, H, DK))
    key_unit = unit_rows(keys.astype(jnp.float32).reshape(TOKENS, REFL, H, DK))
    value_full = values.astype(jnp.float32).reshape(TOKENS, REFL, H, DK)
    rates = jnp.transpose(beta, (2, 0, 1))

    def advance(memory, inputs):
        query_row, key_rows, value_rows, rate_rows = inputs
        for refl_index in range(REFL):
            key_now = key_rows[refl_index]
            recall = jnp.einsum('hd,hde->he', key_now, memory, precision=highest)
            delta_row = value_rows[refl_index] - recall
            memory = memory + rate_rows[refl_index][:, None, None] * key_now[:, :, None] * delta_row[:, None, :]
        return (memory, jnp.einsum('hd,hde->he', query_row, memory, precision=highest))
    start_state = jnp.zeros((H, DK, DK), jnp.float32)
    _, readout = lax.scan(advance, start_state, (query_unit, key_unit, value_full, rates))
    normed = readout * lax.rsqrt(lax.optimization_barrier(jnp.mean(readout * readout, axis=-1, keepdims=True)) + 1e-06) * gain.reshape(H, DK)
    flat = normed.reshape(TOKENS, H * DK).astype(jnp.bfloat16)
    group_width = H * DK // N_HEAD
    summed = jnp.zeros((TOKENS, D), jnp.float32)
    for group in range(N_HEAD):
        lower_edge = group * group_width
        partial_value = jnp.dot(flat[:, lower_edge:lower_edge + group_width], w_out[lower_edge:lower_edge + group_width], preferred_element_type=jnp.float32)
        rounded = lax.optimization_barrier(partial_value.astype(jnp.bfloat16))
        summed = summed + rounded.astype(jnp.float32)
    return summed.astype(jnp.bfloat16)
```

```python
import functools

import jax
import jax.numpy as jnp
from jax import lax
from jax.experimental import pallas as pl
from jax.experimental.pallas import tpu as pltpu
from jax.sharding import PartitionSpec as P

DK = 128
REFL = 2
TINY = 1e-06
CHUNK = 128
BASE = 8
F32 = jnp.float32
BF16 = jnp.bfloat16


def shifted(value, axis, steps):
    count = lax.axis_size(axis)
    return lax.ppermute(value, axis, [(source, source + steps) for source in range(count - steps)])


def mxu(left, right):
    return jnp.dot(left, right, preferred_element_type=F32)


def mxu_nt(left, right):
    return lax.dot_general(left, right, (((1,), (1,)), ((), ())), preferred_element_type=F32)


def split(value):
    high = value.astype(BF16)
    return high, (value - high.astype(F32)).astype(BF16)


def mxu3(left, right):
    (left_high, left_low), (right_high, right_low) = left, right
    wide = jnp.concatenate([left_high, left_high], axis=1)
    tall = jnp.concatenate([right_high, right_low], axis=0)
    return mxu(wide, tall) + mxu(left_low, right_high)


def unit_lower_inverse(lower):
    size = lower.shape[0]
    lane = lax.broadcasted_iota(jnp.int32, (BASE, size), 1)
    sub = lax.broadcasted_iota(jnp.int32, (BASE, size), 0)
    block_of = lane // BASE
    compact = jnp.zeros((BASE, size), F32)
    for block in range(size // BASE):
        rows = lower[block * BASE : (block + 1) * BASE, :]
        compact = jnp.where(block_of == block, rows, compact)
    inverse = jnp.where(lane % BASE == sub, 1.0, 0.0).astype(F32)
    for step in range(BASE - 1):
        factor = jnp.take_along_axis(compact, block_of * BASE + step, axis=1)
        inverse = inverse - factor * inverse[step : step + 1, :]
    rows = [jnp.where(block_of == block, inverse, 0.0) for block in range(size // BASE)]
    width = BASE
    while width < size:
        pairs = size // (2 * width)
        per = width // BASE
        whole = jnp.concatenate(rows, axis=0)
        halves = split(whole)
        lane_w = lax.broadcasted_iota(jnp.int32, (width, size), 1) // width
        picked = jnp.concatenate(
            [
                jnp.where(lane_w == 2 * p, lower[(2 * p + 1) * width : (2 * p + 2) * width, :], 0.0)
                for p in range(pairs)
            ],
            axis=0,
        )
        inner = mxu3(split(picked), halves)
        empty = jnp.zeros((width, size), F32)
        spread = jnp.concatenate(
            [x for p in range(pairs) for x in (empty, inner[p * width : (p + 1) * width, :])], axis=0
        )
        below = jnp.concatenate(
            [rows[(2 * p + 1) * per + i] for p in range(pairs) for i in range(per)], axis=0
        )
        joined = below - mxu3(split(below), split(spread))
        for p in range(pairs):
            for i in range(per):
                at = (p * per + i) * BASE
                rows[(2 * p + 1) * per + i] = joined[at : at + BASE, :]
        width *= 2
    return split(jnp.concatenate(rows, axis=0))


def chunk_kernel(group, q_ref, k_ref, v_ref, b_ref, o_ref, e_ref, s_ref, p_ref, state):
    chunk = pl.program_id(1)
    tokens = CHUNK // REFL

    @pl.when(chunk == 0)
    def _():
        lane = lax.broadcasted_iota(jnp.int32, (DK, 2 * DK), 1)
        sub = lax.broadcasted_iota(jnp.int32, (DK, 2 * DK), 0)
        start = jnp.where(lane == sub + DK, 1.0, 0.0).astype(F32)
        for head in range(group):
            state[head] = start

    below = lax.broadcasted_iota(jnp.int32, (CHUNK, CHUNK), 0) > lax.broadcasted_iota(
        jnp.int32, (CHUNK, CHUNK), 1
    )
    reach = REFL * lax.broadcasted_iota(jnp.int32, (tokens, CHUNK), 0) + (
        REFL - 1
    ) >= lax.broadcasted_iota(jnp.int32, (tokens, CHUNK), 1)
    for head in range(group):
        cols = slice(head * DK, (head + 1) * DK)
        k = k_ref[:, cols]
        q = q_ref[:, cols]
        kf = k.astype(F32)
        qf = q.astype(F32)
        k_scale = lax.rsqrt(jnp.sum(kf * kf, axis=-1, keepdims=True) + TINY)
        q_scale = lax.rsqrt(jnp.sum(qf * qf, axis=-1, keepdims=True) + TINY)
        rate = b_ref[0, :, head : head + 1] * k_scale
        rate2 = rate * k_scale
        kq = jnp.concatenate([k, q], axis=0)
        gram = mxu_nt(kq, k)
        inv_high, inv_low = unit_lower_inverse(jnp.where(below, rate2 * gram[:CHUNK], 0.0))
        scores = jnp.where(reach, gram[CHUNK:], 0.0).astype(BF16)
        now = state[head]
        seen = mxu(jnp.concatenate([kq, kq], axis=1), jnp.concatenate(split(now), axis=0))
        scaled = rate2 * seen[:CHUNK]
        right = jnp.concatenate(
            [rate * v_ref[:, cols].astype(F32) - scaled[:, :DK], -scaled[:, DK:]], axis=1
        )
        delta = mxu3((inv_high, inv_low), split(right))
        delta_high, delta_low = split(delta)
        k_t = kf.T.astype(BF16)
        state[head] = now + mxu(
            jnp.concatenate([k_t, k_t], axis=1), jnp.concatenate([delta_high, delta_low], axis=0)
        )
        out = q_scale * (seen[CHUNK:] + mxu(scores, delta_high))
        o_ref[:, cols] = out[:, :DK]
        e_ref[:, cols] = out[:, DK:].astype(BF16)

    @pl.when(chunk == pl.num_programs(1) - 1)
    def _():
        for head in range(group):
            s_ref[head] = state[head, :, :DK]
            p_ref[head] = state[head, :, DK:].astype(BF16)


def local_pass(queries, keys, values, beta, group):
    tokens, width = queries.shape
    heads = width // DK
    tile = CHUNK // REFL
    refl = pl.BlockSpec((CHUNK, group * DK), lambda g, c: (c, g))
    token = pl.BlockSpec((tile, group * DK), lambda g, c: (c, g))
    per_head = pl.BlockSpec((group, DK, DK), lambda g, c: (g, 0, 0))
    return pl.pallas_call(
        functools.partial(chunk_kernel, group),
        grid=(heads // group, tokens // tile),
        in_specs=[
            token,
            refl,
            refl,
            pl.BlockSpec((1, CHUNK, group), lambda g, c: (g, c, 0)),
        ],
        out_specs=[token, token, per_head, per_head],
        out_shape=[
            jax.ShapeDtypeStruct((tokens, width), F32),
            jax.ShapeDtypeStruct((tokens, width), BF16),
            jax.ShapeDtypeStruct((heads, DK, DK), F32),
            jax.ShapeDtypeStruct((heads, DK, DK), BF16),
        ],
        scratch_shapes=[pltpu.VMEM((group, DK, 2 * DK), F32)],
        compiler_params=pltpu.CompilerParams(vmem_limit_bytes=32 * 1024 * 1024),
        name="local_pass",
    )(queries, keys, values, beta)


def norm_kernel(o_ref, e_ref, s_ref, g_ref, out_ref):
    for head in range(s_ref.shape[0]):
        cols = slice(head * DK, (head + 1) * DK)
        readout = o_ref[:, cols] + mxu(e_ref[:, cols], s_ref[head])
        mean = jnp.mean(readout * readout, axis=-1, keepdims=True)
        out_ref[:, cols] = (readout * lax.rsqrt(mean + TINY) * g_ref[:, cols]).astype(BF16)


def normed_rows(local, exposure, incoming, gain):
    tokens, width = local.shape
    tile = 128
    rows = pl.BlockSpec((tile, width), lambda i: (i, 0))
    return pl.pallas_call(
        norm_kernel,
        grid=(tokens // tile,),
        in_specs=[
            rows,
            rows,
            pl.BlockSpec(incoming.shape, lambda i: (0, 0, 0)),
            pl.BlockSpec((1, width), lambda i: (0, 0)),
        ],
        out_specs=rows,
        out_shape=jax.ShapeDtypeStruct((tokens, width), BF16),
        name="normed_rows",
    )(local, exposure, incoming, gain.reshape(1, width))


def per_device(queries, keys, values, beta, gain, w_out):
    tokens, width = queries.shape
    heads = width // DK
    group = min(4, heads)
    keys2 = keys.reshape(tokens * REFL, width)
    values2 = values.reshape(tokens * REFL, width)
    beta_rows = (
        beta.transpose(2, 0, 1)
        .reshape(tokens * REFL, heads // group, group)
        .transpose(1, 0, 2)
    )
    w_full = lax.all_gather(w_out, "ctx", axis=1, tiled=True)
    local, exposure, state_end, total_end = local_pass(queries, keys2, values2, beta_rows, group)

    incoming = jnp.zeros((heads, DK, DK), BF16)
    for _ in range(lax.axis_size("ctx") - 1):
        outgoing = (
            jnp.einsum("hde,hef->hdf", total_end, incoming, preferred_element_type=F32) + state_end
        )
        incoming = shifted(outgoing.astype(BF16), "ctx", 1)
    flat = normed_rows(local, exposure, incoming, gain)
    partial_value = jnp.dot(flat, w_full, preferred_element_type=F32)
    return lax.psum_scatter(
        partial_value.astype(BF16), "head", scatter_dimension=1, tiled=True
    )


def solution(mesh):
    in_specs = (
        P(("groups", "ctx"), "head"),
        P(("groups", "ctx"), None, "head"),
        P(("groups", "ctx"), None, "head"),
        P(None, "head", ("groups", "ctx")),
        P("head"),
        P("head", "ctx"),
    )
    out_specs = P(("groups", "ctx"), "head")
    return jax.shard_map(
        per_device, mesh=mesh, in_specs=in_specs, out_specs=out_specs, check_vma=False
    )
```

```python
import functools

import jax
import jax.numpy as jnp
from jax import lax
from jax.experimental import pallas as pl
from jax.experimental.pallas import tpu as pltpu
from jax.sharding import PartitionSpec as P

DK = 128
REFL = 2
TINY = 1e-06
CHUNK = 128
BASE = 8
F32 = jnp.float32
BF16 = jnp.bfloat16


def shifted(value, axis, steps):
    count = lax.axis_size(axis)
    return lax.ppermute(value, axis, [(source, source + steps) for source in range(count - steps)])


def mxu(left, right):
    return jnp.dot(left, right, preferred_element_type=F32)


def mxu_nt(left, right):
    return lax.dot_general(left, right, (((1,), (1,)), ((), ())), preferred_element_type=F32)


def split(value):
    high = value.astype(BF16)
    return high, (value - high.astype(F32)).astype(BF16)


def mxu3(left, right):
    (left_high, left_low), (right_high, right_low) = left, right
    wide = jnp.concatenate([left_high, left_high], axis=1)
    tall = jnp.concatenate([right_high, right_low], axis=0)
    return mxu(wide, tall) + mxu(left_low, right_high)


def each(function, *columns):
    return [function(*row) for row in zip(*columns)]


def unit_lower_inverse(lowers):
    size = lowers[0].shape[0]
    lane = lax.broadcasted_iota(jnp.int32, (BASE, size), 1)
    sub = lax.broadcasted_iota(jnp.int32, (BASE, size), 0)
    block_of = lane // BASE
    blocks = range(size // BASE)

    def compacted(lower):
        compact = jnp.zeros((BASE, size), F32)
        for block in blocks:
            rows = lower[block * BASE : (block + 1) * BASE, :]
            compact = jnp.where(block_of == block, rows, compact)
        return compact

    compacts = each(compacted, lowers)
    inverses = [jnp.where(lane % BASE == sub, 1.0, 0.0).astype(F32) for _ in lowers]
    for step in range(BASE - 1):
        factors = each(
            lambda compact: jnp.take_along_axis(compact, block_of * BASE + step, axis=1), compacts
        )
        inverses = each(lambda inv, factor: inv - factor * inv[step : step + 1, :], inverses, factors)
    rows_of = each(lambda inv: [jnp.where(block_of == block, inv, 0.0) for block in blocks], inverses)
    width = BASE
    while width < size:
        pairs = range(size // (2 * width))
        per = width // BASE
        lane_w = lax.broadcasted_iota(jnp.int32, (width, size), 1) // width
        empty = jnp.zeros((width, size), F32)

        def picked(lower):
            return jnp.concatenate(
                [
                    jnp.where(
                        lane_w == 2 * p, lower[(2 * p + 1) * width : (2 * p + 2) * width, :], 0.0
                    )
                    for p in pairs
                ],
                axis=0,
            )

        def spread(inner):
            return jnp.concatenate(
                [x for p in pairs for x in (empty, inner[p * width : (p + 1) * width, :])], axis=0
            )

        halves = each(lambda rows: split(jnp.concatenate(rows, axis=0)), rows_of)
        picks = each(lambda lower: split(picked(lower)), lowers)
        inners = each(mxu3, picks, halves)
        belows = each(
            lambda rows: jnp.concatenate(
                [rows[(2 * p + 1) * per + i] for p in pairs for i in range(per)], axis=0
            ),
            rows_of,
        )
        joins = each(
            lambda below, inner: below - mxu3(split(below), split(spread(inner))), belows, inners
        )

        def placed(rows, joined):
            rows = list(rows)
            for p in pairs:
                for i in range(per):
                    at = (p * per + i) * BASE
                    rows[(2 * p + 1) * per + i] = joined[at : at + BASE, :]
            return rows

        rows_of = each(placed, rows_of, joins)
        width *= 2
    return each(lambda rows: split(jnp.concatenate(rows, axis=0)), rows_of)


def chunk_kernel(group, q_ref, k_ref, v_ref, b_ref, o_ref, e_ref, s_ref, p_ref, state):
    chunk = pl.program_id(1)
    tokens = CHUNK // REFL

    @pl.when(chunk == 0)
    def _():
        lane = lax.broadcasted_iota(jnp.int32, (DK, 2 * DK), 1)
        sub = lax.broadcasted_iota(jnp.int32, (DK, 2 * DK), 0)
        start = jnp.where(lane == sub + DK, 1.0, 0.0).astype(F32)
        for head in range(group):
            state[head] = start

    below = lax.broadcasted_iota(jnp.int32, (CHUNK, CHUNK), 0) > lax.broadcasted_iota(
        jnp.int32, (CHUNK, CHUNK), 1
    )
    reach = REFL * lax.broadcasted_iota(jnp.int32, (tokens, CHUNK), 0) + (
        REFL - 1
    ) >= lax.broadcasted_iota(jnp.int32, (tokens, CHUNK), 1)
    heads = range(group)
    cols = [slice(head * DK, (head + 1) * DK) for head in heads]
    ks = [k_ref[:, c] for c in cols]
    qs = [q_ref[:, c] for c in cols]

    def inverse_norm(rows):
        rows = rows.astype(F32)
        return lax.rsqrt(jnp.sum(rows * rows, axis=-1, keepdims=True) + TINY)

    k_scales = each(inverse_norm, ks)
    q_scales = each(inverse_norm, qs)
    rates = [b_ref[0, :, head : head + 1] * k_scales[head] for head in heads]
    rates2 = each(lambda rate, scale: rate * scale, rates, k_scales)
    kqs = each(lambda k, q: jnp.concatenate([k, q], axis=0), ks, qs)
    grams = each(mxu_nt, kqs, ks)
    lowers = each(lambda rate, gram: jnp.where(below, rate * gram[:CHUNK], 0.0), rates2, grams)
    scores = each(lambda gram: jnp.where(reach, gram[CHUNK:], 0.0).astype(BF16), grams)
    inverses = unit_lower_inverse(lowers)
    nows = [state[head] for head in heads]
    seens = each(
        lambda kq, now: mxu(
            jnp.concatenate([kq, kq], axis=1), jnp.concatenate(split(now), axis=0)
        ),
        kqs,
        nows,
    )

    def right_side(head):
        scaled = rates2[head] * seens[head][:CHUNK]
        own = rates[head] * v_ref[:, cols[head]].astype(F32)
        return split(jnp.concatenate([own - scaled[:, :DK], -scaled[:, DK:]], axis=1))

    rights = each(right_side, heads)
    deltas = each(lambda inverse, right: split(mxu3(inverse, right)), inverses, rights)

    def stepped(k, now, delta):
        k_t = k.astype(F32).T.astype(BF16)
        return now + mxu(jnp.concatenate([k_t, k_t], axis=1), jnp.concatenate(delta, axis=0))

    nexts = each(stepped, ks, nows, deltas)
    outs = each(
        lambda scale, seen, score, delta: scale * (seen[CHUNK:] + mxu(score, delta[0])),
        q_scales,
        seens,
        scores,
        deltas,
    )
    for head in heads:
        state[head] = nexts[head]
        o_ref[:, cols[head]] = outs[head][:, :DK]
        e_ref[:, cols[head]] = outs[head][:, DK:].astype(BF16)

    @pl.when(chunk == pl.num_programs(1) - 1)
    def _():
        for head in heads:
            s_ref[head] = nexts[head][:, :DK]
            p_ref[head] = nexts[head][:, DK:].astype(BF16)


def local_pass(queries, keys, values, beta, group):
    tokens, width = queries.shape
    heads = width // DK
    tile = CHUNK // REFL
    refl = pl.BlockSpec((CHUNK, group * DK), lambda g, c: (c, g))
    token = pl.BlockSpec((tile, group * DK), lambda g, c: (c, g))
    per_head = pl.BlockSpec((group, DK, DK), lambda g, c: (g, 0, 0))
    return pl.pallas_call(
        functools.partial(chunk_kernel, group),
        grid=(heads // group, tokens // tile),
        in_specs=[
            token,
            refl,
            refl,
            pl.BlockSpec((1, CHUNK, group), lambda g, c: (g, c, 0)),
        ],
        out_specs=[token, token, per_head, per_head],
        out_shape=[
            jax.ShapeDtypeStruct((tokens, width), F32),
            jax.ShapeDtypeStruct((tokens, width), BF16),
            jax.ShapeDtypeStruct((heads, DK, DK), F32),
            jax.ShapeDtypeStruct((heads, DK, DK), BF16),
        ],
        scratch_shapes=[pltpu.VMEM((group, DK, 2 * DK), F32)],
        compiler_params=pltpu.CompilerParams(vmem_limit_bytes=32 * 1024 * 1024),
        name="local_pass",
    )(queries, keys, values, beta)


def norm_kernel(o_ref, e_ref, s_ref, g_ref, out_ref):
    for head in range(s_ref.shape[0]):
        cols = slice(head * DK, (head + 1) * DK)
        readout = o_ref[:, cols] + mxu(e_ref[:, cols], s_ref[head])
        mean = jnp.mean(readout * readout, axis=-1, keepdims=True)
        out_ref[:, cols] = (readout * lax.rsqrt(mean + TINY) * g_ref[:, cols]).astype(BF16)


def normed_rows(local, exposure, incoming, gain):
    tokens, width = local.shape
    tile = 128
    rows = pl.BlockSpec((tile, width), lambda i: (i, 0))
    return pl.pallas_call(
        norm_kernel,
        grid=(tokens // tile,),
        in_specs=[
            rows,
            rows,
            pl.BlockSpec(incoming.shape, lambda i: (0, 0, 0)),
            pl.BlockSpec((1, width), lambda i: (0, 0)),
        ],
        out_specs=rows,
        out_shape=jax.ShapeDtypeStruct((tokens, width), BF16),
        name="normed_rows",
    )(local, exposure, incoming, gain.reshape(1, width))


def per_device(queries, keys, values, beta, gain, w_out):
    tokens, width = queries.shape
    heads = width // DK
    group = min(8, heads)
    keys2 = keys.reshape(tokens * REFL, width)
    values2 = values.reshape(tokens * REFL, width)
    beta_rows = (
        beta.transpose(2, 0, 1)
        .reshape(tokens * REFL, heads // group, group)
        .transpose(1, 0, 2)
    )
    w_full = lax.all_gather(w_out, "ctx", axis=1, tiled=True)
    local, exposure, state_end, total_end = local_pass(queries, keys2, values2, beta_rows, group)

    incoming = jnp.zeros((heads, DK, DK), BF16)
    for _ in range(lax.axis_size("ctx") - 1):
        outgoing = (
            jnp.einsum("hde,hef->hdf", total_end, incoming, preferred_element_type=F32) + state_end
        )
        incoming = shifted(outgoing.astype(BF16), "ctx", 1)
    flat = normed_rows(local, exposure, incoming, gain)
    partial_value = jnp.dot(flat, w_full, preferred_element_type=F32)
    return lax.psum_scatter(
        partial_value.astype(BF16), "head", scatter_dimension=1, tiled=True
    )


def solution(mesh):
    in_specs = (
        P(("groups", "ctx"), "head"),
        P(("groups", "ctx"), None, "head"),
        P(("groups", "ctx"), None, "head"),
        P(None, "head", ("groups", "ctx")),
        P("head"),
        P("head", "ctx"),
    )
    out_specs = P(("groups", "ctx"), "head")
    return jax.shard_map(
        per_device, mesh=mesh, in_specs=in_specs, out_specs=out_specs, check_vma=False
    )
```

```python
import functools

import jax
import jax.numpy as jnp
from jax import lax
from jax.experimental import pallas as pl
from jax.experimental.pallas import tpu as pltpu
from jax.sharding import PartitionSpec as P

DK = 128
REFL = 2
TINY = 1e-06
CHUNK = 128
BASE = 8
F32 = jnp.float32
BF16 = jnp.bfloat16


def mxu(left, right):
    return jnp.dot(left, right, preferred_element_type=F32)


def mxu_nt(left, right):
    return lax.dot_general(left, right, (((1,), (1,)), ((), ())), preferred_element_type=F32)


def split(value):
    high = value.astype(BF16)
    return high, (value - high.astype(F32)).astype(BF16)


def mxu3(left, right):
    (left_high, left_low), (right_high, right_low) = left, right
    wide = jnp.concatenate([left_high, left_high], axis=1)
    tall = jnp.concatenate([right_high, right_low], axis=0)
    return mxu(wide, tall) + mxu(left_low, right_high)


def each(function, *columns):
    return [function(*row) for row in zip(*columns)]


def unit_lower_inverse(lowers):
    size = lowers[0].shape[0]
    lane = lax.broadcasted_iota(jnp.int32, (BASE, size), 1)
    sub = lax.broadcasted_iota(jnp.int32, (BASE, size), 0)
    block_of = lane // BASE
    blocks = range(size // BASE)

    def compacted(lower):
        compact = jnp.zeros((BASE, size), F32)
        for block in blocks:
            rows = lower[block * BASE : (block + 1) * BASE, :]
            compact = jnp.where(block_of == block, rows, compact)
        return compact

    compacts = each(compacted, lowers)
    inverses = [jnp.where(lane % BASE == sub, 1.0, 0.0).astype(F32) for _ in lowers]
    for step in range(BASE - 1):
        factors = each(
            lambda compact: jnp.take_along_axis(compact, block_of * BASE + step, axis=1), compacts
        )
        inverses = each(lambda inv, factor: inv - factor * inv[step : step + 1, :], inverses, factors)
    rows_of = each(lambda inv: [jnp.where(block_of == block, inv, 0.0) for block in blocks], inverses)
    width = BASE
    while width < size:
        pairs = range(size // (2 * width))
        per = width // BASE
        lane_w = lax.broadcasted_iota(jnp.int32, (width, size), 1) // width
        empty = jnp.zeros((width, size), F32)

        def picked(lower):
            return jnp.concatenate(
                [
                    jnp.where(
                        lane_w == 2 * p, lower[(2 * p + 1) * width : (2 * p + 2) * width, :], 0.0
                    )
                    for p in pairs
                ],
                axis=0,
            )

        def spread(inner):
            return jnp.concatenate(
                [x for p in pairs for x in (empty, inner[p * width : (p + 1) * width, :])], axis=0
            )

        halves = each(lambda rows: split(jnp.concatenate(rows, axis=0)), rows_of)
        picks = each(lambda lower: split(picked(lower)), lowers)
        inners = each(mxu3, picks, halves)
        belows = each(
            lambda rows: jnp.concatenate(
                [rows[(2 * p + 1) * per + i] for p in pairs for i in range(per)], axis=0
            ),
            rows_of,
        )
        joins = each(
            lambda below, inner: below - mxu3(split(below), split(spread(inner))), belows, inners
        )

        def placed(rows, joined):
            rows = list(rows)
            for p in pairs:
                for i in range(per):
                    at = (p * per + i) * BASE
                    rows[(2 * p + 1) * per + i] = joined[at : at + BASE, :]
            return rows

        rows_of = each(placed, rows_of, joins)
        width *= 2
    return each(lambda rows: split(jnp.concatenate(rows, axis=0)), rows_of)


def chunk_kernel(group, q_ref, k_ref, v_ref, b_ref, o_ref, e_ref, s_ref, p_ref, state):
    chunk = pl.program_id(1)
    tokens = CHUNK // REFL

    @pl.when(chunk == 0)
    def _():
        lane = lax.broadcasted_iota(jnp.int32, (DK, 2 * DK), 1)
        sub = lax.broadcasted_iota(jnp.int32, (DK, 2 * DK), 0)
        start = jnp.where(lane == sub + DK, 1.0, 0.0).astype(F32)
        for head in range(group):
            state[head] = start

    below = lax.broadcasted_iota(jnp.int32, (CHUNK, CHUNK), 0) > lax.broadcasted_iota(
        jnp.int32, (CHUNK, CHUNK), 1
    )
    reach = REFL * lax.broadcasted_iota(jnp.int32, (tokens, CHUNK), 0) + (
        REFL - 1
    ) >= lax.broadcasted_iota(jnp.int32, (tokens, CHUNK), 1)
    heads = range(group)
    cols = [slice(head * DK, (head + 1) * DK) for head in heads]
    ks = [k_ref[:, c] for c in cols]
    qs = [q_ref[:, c] for c in cols]

    def inverse_norm(rows):
        rows = rows.astype(F32)
        return lax.rsqrt(jnp.sum(rows * rows, axis=-1, keepdims=True) + TINY)

    k_scales = each(inverse_norm, ks)
    q_scales = each(inverse_norm, qs)
    rates = [b_ref[0, :, head : head + 1] * k_scales[head] for head in heads]
    rates2 = each(lambda rate, scale: rate * scale, rates, k_scales)
    kqs = each(lambda k, q: jnp.concatenate([k, q], axis=0), ks, qs)
    grams = each(mxu_nt, kqs, ks)
    lowers = each(lambda rate, gram: jnp.where(below, rate * gram[:CHUNK], 0.0), rates2, grams)
    scores = each(lambda gram: jnp.where(reach, gram[CHUNK:], 0.0).astype(BF16), grams)
    inverses = unit_lower_inverse(lowers)
    nows = [state[head] for head in heads]
    seens = each(
        lambda kq, now: mxu(
            jnp.concatenate([kq, kq], axis=1), jnp.concatenate(split(now), axis=0)
        ),
        kqs,
        nows,
    )

    def right_side(head):
        scaled = rates2[head] * seens[head][:CHUNK]
        own = rates[head] * v_ref[:, cols[head]].astype(F32)
        return split(jnp.concatenate([own - scaled[:, :DK], -scaled[:, DK:]], axis=1))

    rights = each(right_side, heads)
    deltas = each(lambda inverse, right: split(mxu3(inverse, right)), inverses, rights)

    def stepped(k, now, delta):
        k_t = k.astype(F32).T.astype(BF16)
        return now + mxu(jnp.concatenate([k_t, k_t], axis=1), jnp.concatenate(delta, axis=0))

    nexts = each(stepped, ks, nows, deltas)
    outs = each(
        lambda scale, seen, score, delta: scale * (seen[CHUNK:] + mxu(score, delta[0])),
        q_scales,
        seens,
        scores,
        deltas,
    )
    for head in heads:
        state[head] = nexts[head]
        o_ref[:, cols[head]] = outs[head][:, :DK]
        e_ref[:, cols[head]] = outs[head][:, DK:].astype(BF16)

    @pl.when(chunk == pl.num_programs(1) - 1)
    def _():
        for head in heads:
            s_ref[head] = nexts[head][:, :DK]
            p_ref[head] = nexts[head][:, DK:].astype(BF16)


def local_pass(queries, keys, values, beta, group):
    tokens, width = queries.shape
    heads = width // DK
    tile = CHUNK // REFL
    refl = pl.BlockSpec((CHUNK, group * DK), lambda g, c: (c, g))
    token = pl.BlockSpec((tile, group * DK), lambda g, c: (c, g))
    per_head = pl.BlockSpec((group, DK, DK), lambda g, c: (g, 0, 0))
    return pl.pallas_call(
        functools.partial(chunk_kernel, group),
        grid=(heads // group, tokens // tile),
        in_specs=[
            token,
            refl,
            refl,
            pl.BlockSpec((1, CHUNK, group), lambda g, c: (g, c, 0)),
        ],
        out_specs=[token, token, per_head, per_head],
        out_shape=[
            jax.ShapeDtypeStruct((tokens, width), F32),
            jax.ShapeDtypeStruct((tokens, width), BF16),
            jax.ShapeDtypeStruct((heads, DK, DK), F32),
            jax.ShapeDtypeStruct((heads, DK, DK), BF16),
        ],
        scratch_shapes=[pltpu.VMEM((group, DK, 2 * DK), F32)],
        compiler_params=pltpu.CompilerParams(vmem_limit_bytes=32 * 1024 * 1024),
        name="local_pass",
    )(queries, keys, values, beta)


def norm_kernel(o_ref, e_ref, s_ref, g_ref, out_ref):
    heads = range(s_ref.shape[0])
    cols = [slice(head * DK, (head + 1) * DK) for head in heads]
    readouts = [o_ref[:, cols[head]] + mxu(e_ref[:, cols[head]], s_ref[head]) for head in heads]
    scales = each(
        lambda rows: lax.rsqrt(jnp.mean(rows * rows, axis=-1, keepdims=True) + TINY), readouts
    )
    for head in heads:
        out_ref[:, cols[head]] = (readouts[head] * scales[head] * g_ref[:, cols[head]]).astype(BF16)


def normed_rows(local, exposure, incoming, gain):
    tokens, width = local.shape
    tile = 128
    rows = pl.BlockSpec((tile, width), lambda i: (i, 0))
    return pl.pallas_call(
        norm_kernel,
        grid=(tokens // tile,),
        in_specs=[
            rows,
            rows,
            pl.BlockSpec(incoming.shape, lambda i: (0, 0, 0)),
            pl.BlockSpec((1, width), lambda i: (0, 0)),
        ],
        out_specs=rows,
        out_shape=jax.ShapeDtypeStruct((tokens, width), BF16),
        name="normed_rows",
    )(local, exposure, incoming, gain.reshape(1, width))


def project_kernel(order_ref, a_ref, w_ref, give_ref, keep_ref):
    step = pl.program_id(0)
    half = pl.num_programs(0) // 2
    product = mxu(a_ref[...], w_ref[...]).astype(BF16)

    @pl.when(step < half)
    def _():
        give_ref[...] = product

    @pl.when(step >= half)
    def _():
        keep_ref[...] = product


def project(order, rows, weights):
    tokens, depth = rows.shape
    count = order.shape[0]
    half = count // 2
    block = weights.shape[1] // count
    shape = jax.ShapeDtypeStruct((tokens, half * block), BF16)
    return pl.pallas_call(
        project_kernel,
        grid_spec=pltpu.PrefetchScalarGridSpec(
            num_scalar_prefetch=1,
            grid=(count,),
            in_specs=[
                pl.BlockSpec((tokens, depth), lambda i, order: (0, 0)),
                pl.BlockSpec((depth, block), lambda i, order: (0, order[i])),
            ],
            out_specs=[
                pl.BlockSpec((tokens, block), lambda i, order: (0, jnp.minimum(i, half - 1))),
                pl.BlockSpec((tokens, block), lambda i, order: (0, jnp.maximum(i - half, 0))),
            ],
        ),
        out_shape=[shape, shape],
        compiler_params=pltpu.CompilerParams(vmem_limit_bytes=32 * 1024 * 1024),
        name="project",
    )(order, rows, weights)


def halving_order(count):
    order = [0]
    bit = count // 2
    while bit >= 1:
        order = [m | bit for m in order] + order
        bit //= 2
    return order


def head_sum(give, keep):
    count = lax.axis_size("head")
    bit = 1
    while bit < count:
        pairs = [(i, i ^ bit) for i in range(count)]
        got = lax.ppermute(give, "head", pairs)
        total = keep.astype(F32) + got.astype(F32)
        bit *= 2
        half = total.shape[1] // 2
        give, keep = total[:, :half].astype(BF16), total[:, half:]
        if bit >= count:
            return total.astype(BF16)
    return keep


def per_device(queries, keys, values, beta, gain, w_out):
    tokens, width = queries.shape
    heads = width // DK
    group = min(8, heads)
    keys2 = keys.reshape(tokens * REFL, width)
    values2 = values.reshape(tokens * REFL, width)
    beta_rows = (
        beta.transpose(2, 0, 1)
        .reshape(tokens * REFL, heads // group, group)
        .transpose(1, 0, 2)
    )
    side = lax.axis_index("groups")
    half_cols = w_out.shape[1] // 2
    w_half = lax.dynamic_slice_in_dim(w_out, side * half_cols, half_cols, 1)
    w_mine = lax.all_gather(w_half, "ctx", axis=1, tiled=True)
    local, exposure, state_end, total_end = local_pass(queries, keys2, values2, beta_rows, group)

    incoming = jnp.zeros((heads, DK, DK), BF16)
    outgoing = state_end.astype(BF16)
    for hop in range(lax.axis_size("ctx") - 1):
        incoming = incoming + lax.ppermute(outgoing, "ctx", [(hop, hop + 1)])
        outgoing = (
            jnp.einsum("hde,hef->hdf", total_end, incoming, preferred_element_type=F32) + state_end
        ).astype(BF16)
    mine = normed_rows(local, exposure, incoming, gain)
    swap = [(0, 1), (1, 0)]
    other = lax.ppermute(mine, "groups", swap)
    head_count = lax.axis_size("head")
    order = lax.axis_index("head") ^ jnp.asarray(halving_order(head_count), jnp.int32)
    mine_sum = head_sum(*project(order, mine, w_mine))
    other_sum = head_sum(*project(order, other, w_mine))
    back = lax.ppermute(other_sum, "groups", swap)
    blocks = mine_sum.shape[1] // half_cols
    mine_sum = mine_sum.reshape(tokens, blocks, 1, half_cols)
    back = back.reshape(tokens, blocks, 1, half_cols)
    mixed = jnp.where(
        side == 0,
        jnp.concatenate([mine_sum, back], axis=2),
        jnp.concatenate([back, mine_sum], axis=2),
    )
    return mixed.reshape(tokens, blocks * 2 * half_cols)


def solution(mesh):
    in_specs = (
        P(("groups", "ctx"), "head"),
        P(("groups", "ctx"), None, "head"),
        P(("groups", "ctx"), None, "head"),
        P(None, "head", ("groups", "ctx")),
        P("head"),
        P("head", "ctx"),
    )
    out_specs = P(("groups", "ctx"), "head")
    return jax.shard_map(
        per_device, mesh=mesh, in_specs=in_specs, out_specs=out_specs, check_vma=False
    )
```

```python
import functools

import jax
import jax.numpy as jnp
from jax import lax
from jax.experimental import pallas as pl
from jax.experimental.pallas import tpu as pltpu
from jax.sharding import PartitionSpec as P

DK = 128
REFL = 2
TINY = 1e-06
CHUNK = 128
BASE = 8
F32 = jnp.float32
BF16 = jnp.bfloat16


def mxu(left, right):
    return jnp.dot(left, right, preferred_element_type=F32)


def mxu_nt(left, right):
    return lax.dot_general(left, right, (((1,), (1,)), ((), ())), preferred_element_type=F32)


def split(value):
    high = value.astype(BF16)
    return high, (value - high.astype(F32)).astype(BF16)


def mxu3(left, right):
    (left_high, left_low), (right_high, right_low) = left, right
    wide = jnp.concatenate([left_high, left_high], axis=1)
    tall = jnp.concatenate([right_high, right_low], axis=0)
    return mxu(wide, tall) + mxu(left_low, right_high)


def each(function, *columns):
    return [function(*row) for row in zip(*columns)]


def unit_lower_inverse(lowers):
    size = lowers[0].shape[0]
    lane = lax.broadcasted_iota(jnp.int32, (BASE, size), 1)
    sub = lax.broadcasted_iota(jnp.int32, (BASE, size), 0)
    block_of = lane // BASE
    blocks = range(size // BASE)

    def compacted(lower):
        compact = jnp.zeros((BASE, size), F32)
        for block in blocks:
            rows = lower[block * BASE : (block + 1) * BASE, :]
            compact = jnp.where(block_of == block, rows, compact)
        return compact

    compacts = each(compacted, lowers)
    inverses = [jnp.where(lane % BASE == sub, 1.0, 0.0).astype(F32) for _ in lowers]
    for step in range(BASE - 1):
        factors = each(
            lambda compact: jnp.take_along_axis(compact, block_of * BASE + step, axis=1), compacts
        )
        inverses = each(lambda inv, factor: inv - factor * inv[step : step + 1, :], inverses, factors)
    rows_of = each(lambda inv: [jnp.where(block_of == block, inv, 0.0) for block in blocks], inverses)
    width = BASE
    while width < size:
        pairs = range(size // (2 * width))
        per = width // BASE
        lane_w = lax.broadcasted_iota(jnp.int32, (width, size), 1) // width
        empty = jnp.zeros((width, size), F32)

        def picked(lower):
            return jnp.concatenate(
                [
                    jnp.where(
                        lane_w == 2 * p, lower[(2 * p + 1) * width : (2 * p + 2) * width, :], 0.0
                    )
                    for p in pairs
                ],
                axis=0,
            )

        def spread(inner):
            return jnp.concatenate(
                [x for p in pairs for x in (empty, inner[p * width : (p + 1) * width, :])], axis=0
            )

        halves = each(lambda rows: split(jnp.concatenate(rows, axis=0)), rows_of)
        picks = each(lambda lower: split(picked(lower)), lowers)
        inners = each(mxu3, picks, halves)
        belows = each(
            lambda rows: jnp.concatenate(
                [rows[(2 * p + 1) * per + i] for p in pairs for i in range(per)], axis=0
            ),
            rows_of,
        )
        joins = each(
            lambda below, inner: below - mxu3(split(below), split(spread(inner))), belows, inners
        )

        def placed(rows, joined):
            rows = list(rows)
            for p in pairs:
                for i in range(per):
                    at = (p * per + i) * BASE
                    rows[(2 * p + 1) * per + i] = joined[at : at + BASE, :]
            return rows

        rows_of = each(placed, rows_of, joins)
        width *= 2
    return each(lambda rows: split(jnp.concatenate(rows, axis=0)), rows_of)


def chunk_kernel(group, q_ref, k_ref, v_ref, b_ref, o_ref, e_ref, s_ref, p_ref, state):
    chunk = pl.program_id(1)
    tokens = CHUNK // REFL

    @pl.when(chunk == 0)
    def _():
        lane = lax.broadcasted_iota(jnp.int32, (DK, 2 * DK), 1)
        sub = lax.broadcasted_iota(jnp.int32, (DK, 2 * DK), 0)
        start = jnp.where(lane == sub + DK, 1.0, 0.0).astype(F32)
        for head in range(group):
            state[head] = start

    below = lax.broadcasted_iota(jnp.int32, (CHUNK, CHUNK), 0) > lax.broadcasted_iota(
        jnp.int32, (CHUNK, CHUNK), 1
    )
    reach = REFL * lax.broadcasted_iota(jnp.int32, (tokens, CHUNK), 0) + (
        REFL - 1
    ) >= lax.broadcasted_iota(jnp.int32, (tokens, CHUNK), 1)
    heads = range(group)
    cols = [slice(head * DK, (head + 1) * DK) for head in heads]
    ks = [k_ref[:, :, c].reshape(CHUNK, DK) for c in cols]
    qs = [q_ref[:, c] for c in cols]

    def inverse_norm(rows):
        rows = rows.astype(F32)
        return lax.rsqrt(jnp.sum(rows * rows, axis=-1, keepdims=True) + TINY)

    k_scales = each(inverse_norm, ks)
    q_scales = each(inverse_norm, qs)
    rates = [b_ref[0, :, head : head + 1] * k_scales[head] for head in heads]
    rates2 = each(lambda rate, scale: rate * scale, rates, k_scales)
    kqs = each(lambda k, q: jnp.concatenate([k, q], axis=0), ks, qs)
    grams = each(mxu_nt, kqs, ks)
    lowers = each(lambda rate, gram: jnp.where(below, rate * gram[:CHUNK], 0.0), rates2, grams)
    scores = each(lambda gram: jnp.where(reach, gram[CHUNK:], 0.0).astype(BF16), grams)
    inverses = unit_lower_inverse(lowers)
    nows = [state[head] for head in heads]
    seens = each(
        lambda kq, now: mxu(
            jnp.concatenate([kq, kq], axis=1), jnp.concatenate(split(now), axis=0)
        ),
        kqs,
        nows,
    )

    def right_side(head):
        scaled = rates2[head] * seens[head][:CHUNK]
        own = rates[head] * v_ref[:, :, cols[head]].reshape(CHUNK, DK).astype(F32)
        return split(jnp.concatenate([own - scaled[:, :DK], -scaled[:, DK:]], axis=1))

    rights = each(right_side, heads)
    deltas = each(lambda inverse, right: split(mxu3(inverse, right)), inverses, rights)

    def stepped(k, now, delta):
        k_t = k.astype(F32).T.astype(BF16)
        return now + mxu(jnp.concatenate([k_t, k_t], axis=1), jnp.concatenate(delta, axis=0))

    nexts = each(stepped, ks, nows, deltas)
    outs = each(
        lambda scale, seen, score, delta: scale * (seen[CHUNK:] + mxu(score, delta[0])),
        q_scales,
        seens,
        scores,
        deltas,
    )
    for head in heads:
        state[head] = nexts[head]
        o_ref[:, cols[head]] = outs[head][:, :DK]
        e_ref[:, cols[head]] = outs[head][:, DK:].astype(BF16)

    @pl.when(chunk == pl.num_programs(1) - 1)
    def _():
        for head in heads:
            s_ref[head] = nexts[head][:, :DK]
            p_ref[head] = nexts[head][:, DK:].astype(BF16)


def local_pass(queries, keys, values, beta, group):
    tokens, width = queries.shape
    heads = width // DK
    tile = CHUNK // REFL
    refl = pl.BlockSpec((tile, REFL, group * DK), lambda g, c: (c, 0, g))
    token = pl.BlockSpec((tile, group * DK), lambda g, c: (c, g))
    per_head = pl.BlockSpec((group, DK, DK), lambda g, c: (g, 0, 0))
    return pl.pallas_call(
        functools.partial(chunk_kernel, group),
        grid=(heads // group, tokens // tile),
        in_specs=[
            token,
            refl,
            refl,
            pl.BlockSpec((1, CHUNK, group), lambda g, c: (g, c, 0)),
        ],
        out_specs=[token, token, per_head, per_head],
        out_shape=[
            jax.ShapeDtypeStruct((tokens, width), F32),
            jax.ShapeDtypeStruct((tokens, width), BF16),
            jax.ShapeDtypeStruct((heads, DK, DK), F32),
            jax.ShapeDtypeStruct((heads, DK, DK), BF16),
        ],
        scratch_shapes=[pltpu.VMEM((group, DK, 2 * DK), F32)],
        compiler_params=pltpu.CompilerParams(vmem_limit_bytes=32 * 1024 * 1024),
        cost_estimate=pl.CostEstimate(
            flops=80 * tokens * width * DK, bytes_accessed=16 * tokens * width, transcendentals=0
        ),
        name="local_pass",
    )(queries, keys, values, beta)


def norm_kernel(o_ref, e_ref, s_ref, g_ref, out_ref):
    heads = range(s_ref.shape[0])
    cols = [slice(head * DK, (head + 1) * DK) for head in heads]
    readouts = [o_ref[:, cols[head]] + mxu(e_ref[:, cols[head]], s_ref[head]) for head in heads]
    scales = each(
        lambda rows: lax.rsqrt(jnp.mean(rows * rows, axis=-1, keepdims=True) + TINY), readouts
    )
    for head in heads:
        out_ref[:, cols[head]] = (readouts[head] * scales[head] * g_ref[:, cols[head]]).astype(BF16)


def normed_rows(local, exposure, incoming, gain):
    tokens, width = local.shape
    tile = 128
    rows = pl.BlockSpec((tile, width), lambda i: (i, 0))
    return pl.pallas_call(
        norm_kernel,
        grid=(tokens // tile,),
        in_specs=[
            rows,
            rows,
            pl.BlockSpec(incoming.shape, lambda i: (0, 0, 0)),
            pl.BlockSpec((1, width), lambda i: (0, 0)),
        ],
        out_specs=rows,
        out_shape=jax.ShapeDtypeStruct((tokens, width), BF16),
        name="normed_rows",
    )(local, exposure, incoming, gain.reshape(1, width))


def project_kernel(place_ref, a_ref, *refs):
    weights, (give_ref, keep_ref) = refs[:-2], refs[-2:]
    half, block = len(weights) // 2, weights[0].shape[1]
    for slot, weight in enumerate(weights):
        product = mxu(a_ref[...], weight[...]).astype(BF16)
        place = place_ref[slot]

        @pl.when(place < half)
        def _():
            give_ref[:, pl.ds(pl.multiple_of(place * block, block), block)] = product

        @pl.when(place >= half)
        def _():
            keep_ref[:, pl.ds(pl.multiple_of((place - half) * block, block), block)] = product


def project(places, rows, weights):
    tokens, depth = rows.shape
    count = len(weights)
    block = weights[0].shape[1]
    tile = 128
    half = pl.BlockSpec((tile, count // 2 * block), lambda i, places: (i, 0))
    shape = jax.ShapeDtypeStruct((tokens, count // 2 * block), BF16)
    return pl.pallas_call(
        project_kernel,
        grid_spec=pltpu.PrefetchScalarGridSpec(
            num_scalar_prefetch=1,
            grid=(tokens // tile,),
            in_specs=[pl.BlockSpec((tile, depth), lambda i, places: (i, 0))]
            + [pl.BlockSpec((depth, block), lambda i, places: (0, 0))] * count,
            out_specs=[half, half],
        ),
        out_shape=[shape, shape],
        compiler_params=pltpu.CompilerParams(vmem_limit_bytes=32 * 1024 * 1024),
        cost_estimate=pl.CostEstimate(
            flops=2 * tokens * depth * block * count,
            bytes_accessed=2 * (tokens * depth + (tokens + depth) * block * count),
            transcendentals=0,
        ),
        name="project",
    )(places, rows, *weights)


def halving_order(count):
    order = [0]
    bit = count // 2
    while bit >= 1:
        order = [m | bit for m in order] + order
        bit //= 2
    return order


def head_sum(give, keep):
    count = lax.axis_size("head")
    bit = 1
    while bit < count:
        pairs = [(i, i ^ bit) for i in range(count)]
        got = lax.ppermute(give, "head", pairs)
        total = keep.astype(F32) + got.astype(F32)
        bit *= 2
        half = total.shape[1] // 2
        give, keep = total[:, :half].astype(BF16), total[:, half:]
        if bit >= count:
            return total.astype(BF16)
    return keep


def ring_slots(own, axis):
    count = lax.axis_size(axis)
    up, down = {0: own}, {0: own}
    for step in range(1, count):
        up[step] = lax.ppermute(up[step - 1], axis, [(i, i + 1) for i in range(step - 1, count - 1)])
        down[step] = lax.ppermute(
            down[step - 1], axis, [(i + 1, i) for i in range(count - step)]
        )
    return [own] + [up[k] + down[count - k] for k in range(1, count)]


def slots_by_head(w_half):
    ctx, head = lax.axis_size("ctx"), lax.axis_size("head")
    if ctx == head:
        slots = ring_slots(w_half, "ctx")
        return slots, lax.rem(lax.axis_index("ctx") + ctx - jnp.arange(ctx), ctx)
    whole = lax.all_gather(w_half, "ctx", axis=1, tiled=True)
    return jnp.split(whole, head, axis=1), jnp.arange(head)


def per_device(queries, keys, values, beta, gain, w_out):
    tokens, width = queries.shape
    heads = width // DK
    group = min(8, heads)
    beta_rows = (
        beta.transpose(2, 0, 1)
        .reshape(tokens * REFL, heads // group, group)
        .transpose(1, 0, 2)
    )
    side = lax.axis_index("groups")
    half_cols = w_out.shape[1] // 2
    w_half = lax.dynamic_slice_in_dim(w_out, side * half_cols, half_cols, 1)
    weights, targets = slots_by_head(w_half)
    local, exposure, state_end, total_end = local_pass(queries, keys, values, beta_rows, group)

    incoming = jnp.zeros((heads, DK, DK), BF16)
    outgoing = state_end.astype(BF16)
    for hop in range(lax.axis_size("ctx") - 1):
        incoming = incoming + lax.ppermute(outgoing, "ctx", [(hop, hop + 1)])
        outgoing = (
            jnp.einsum("hde,hef->hdf", total_end, incoming, preferred_element_type=F32) + state_end
        ).astype(BF16)
    mine = normed_rows(local, exposure, incoming, gain)
    swap = [(0, 1), (1, 0)]
    other = lax.ppermute(mine, "groups", swap)
    distance = targets ^ lax.axis_index("head")
    order = jnp.asarray(halving_order(lax.axis_size("head")), jnp.int32)
    places = jnp.argmax(distance[:, None] == order[None, :], axis=1).astype(jnp.int32)
    mine_sum = head_sum(*project(places, mine, weights))
    other_sum = head_sum(*project(places, other, weights))
    back = lax.ppermute(other_sum, "groups", swap)
    blocks = mine_sum.shape[1] // half_cols
    mine_sum = mine_sum.reshape(tokens, blocks, 1, half_cols)
    back = back.reshape(tokens, blocks, 1, half_cols)
    mixed = jnp.where(
        side == 0,
        jnp.concatenate([mine_sum, back], axis=2),
        jnp.concatenate([back, mine_sum], axis=2),
    )
    return mixed.reshape(tokens, blocks * 2 * half_cols)


def solution(mesh):
    in_specs = (
        P(("groups", "ctx"), "head"),
        P(("groups", "ctx"), None, "head"),
        P(("groups", "ctx"), None, "head"),
        P(None, "head", ("groups", "ctx")),
        P("head"),
        P("head", "ctx"),
    )
    out_specs = P(("groups", "ctx"), "head")
    return jax.shard_map(
        per_device, mesh=mesh, in_specs=in_specs, out_specs=out_specs, check_vma=False
    )
```

```python
import functools

import jax
import jax.numpy as jnp
from jax import lax
from jax.experimental import pallas as pl
from jax.experimental.pallas import tpu as pltpu
from jax.sharding import PartitionSpec as P

DK = 128
REFL = 2
TINY = 1e-06
CHUNK = 128
BASE = 8
F32 = jnp.float32
BF16 = jnp.bfloat16


def mxu(left, right):
    return jnp.dot(left, right, preferred_element_type=F32)


def mxu_nt(left, right):
    return lax.dot_general(left, right, (((1,), (1,)), ((), ())), preferred_element_type=F32)


def split(value):
    high = value.astype(BF16)
    return high, (value - high.astype(F32)).astype(BF16)


def mxu3(left, right):
    (left_high, left_low), (right_high, right_low) = left, right
    wide = jnp.concatenate([left_high, left_high], axis=1)
    tall = jnp.concatenate([right_high, right_low], axis=0)
    return mxu(wide, tall) + mxu(left_low, right_high)


def each(function, *columns):
    return [function(*row) for row in zip(*columns)]


def unit_lower_inverse(lowers):
    size = lowers[0].shape[0]
    lane = lax.broadcasted_iota(jnp.int32, (BASE, size), 1)
    sub = lax.broadcasted_iota(jnp.int32, (BASE, size), 0)
    block_of = lane // BASE
    blocks = range(size // BASE)

    def compacted(lower):
        compact = jnp.zeros((BASE, size), F32)
        for block in blocks:
            rows = lower[block * BASE : (block + 1) * BASE, :]
            compact = jnp.where(block_of == block, rows, compact)
        return compact

    compacts = each(compacted, lowers)
    inverses = [jnp.where(lane % BASE == sub, 1.0, 0.0).astype(F32) for _ in lowers]
    for step in range(BASE - 1):
        factors = each(
            lambda compact: jnp.take_along_axis(compact, block_of * BASE + step, axis=1), compacts
        )
        inverses = each(lambda inv, factor: inv - factor * inv[step : step + 1, :], inverses, factors)
    rows_of = each(lambda inv: [jnp.where(block_of == block, inv, 0.0) for block in blocks], inverses)
    width = BASE
    while width < size:
        pairs = range(size // (2 * width))
        per = width // BASE
        lane_w = lax.broadcasted_iota(jnp.int32, (width, size), 1) // width
        empty = jnp.zeros((width, size), F32)

        def picked(lower):
            return jnp.concatenate(
                [
                    jnp.where(
                        lane_w == 2 * p, lower[(2 * p + 1) * width : (2 * p + 2) * width, :], 0.0
                    )
                    for p in pairs
                ],
                axis=0,
            )

        def spread(inner):
            return jnp.concatenate(
                [x for p in pairs for x in (empty, inner[p * width : (p + 1) * width, :])], axis=0
            )

        halves = each(lambda rows: split(jnp.concatenate(rows, axis=0)), rows_of)
        picks = each(lambda lower: split(picked(lower)), lowers)
        inners = each(mxu3, picks, halves)
        belows = each(
            lambda rows: jnp.concatenate(
                [rows[(2 * p + 1) * per + i] for p in pairs for i in range(per)], axis=0
            ),
            rows_of,
        )
        joins = each(
            lambda below, inner: below - mxu3(split(below), split(spread(inner))), belows, inners
        )

        def placed(rows, joined):
            rows = list(rows)
            for p in pairs:
                for i in range(per):
                    at = (p * per + i) * BASE
                    rows[(2 * p + 1) * per + i] = joined[at : at + BASE, :]
            return rows

        rows_of = each(placed, rows_of, joins)
        width *= 2
    return each(lambda rows: split(jnp.concatenate(rows, axis=0)), rows_of)


def chunk_kernel(group, first, q_ref, k_ref, v_ref, b_ref, *refs):
    if first:
        oe_ref, end_ref, state = refs
    else:
        start_ref, oe_ref, s_ref, p_ref, state = refs
    chunk = pl.program_id(0)
    tokens = CHUNK // REFL

    @pl.when(chunk == 0)
    def _():
        lane = lax.broadcasted_iota(jnp.int32, (DK, 2 * DK), 1)
        sub = lax.broadcasted_iota(jnp.int32, (DK, 2 * DK), 0)
        start = jnp.where(lane == sub + DK, 1.0, 0.0).astype(F32)
        for head in range(group):
            state[head] = start if first else start_ref[head]

    below = lax.broadcasted_iota(jnp.int32, (CHUNK, CHUNK), 0) > lax.broadcasted_iota(
        jnp.int32, (CHUNK, CHUNK), 1
    )
    reach = REFL * lax.broadcasted_iota(jnp.int32, (tokens, CHUNK), 0) + (
        REFL - 1
    ) >= lax.broadcasted_iota(jnp.int32, (tokens, CHUNK), 1)
    heads = range(group)
    cols = [slice(head * DK, (head + 1) * DK) for head in heads]
    ks = [k_ref[:, :, c].reshape(CHUNK, DK) for c in cols]
    qs = [q_ref[:, c] for c in cols]

    def inverse_norm(rows):
        rows = rows.astype(F32)
        return lax.rsqrt(jnp.sum(rows * rows, axis=-1, keepdims=True) + TINY)

    k_scales = each(inverse_norm, ks)
    q_scales = each(inverse_norm, qs)
    rates = [b_ref[:, head : head + 1] * k_scales[head] for head in heads]
    rates2 = each(lambda rate, scale: rate * scale, rates, k_scales)
    kqs = each(lambda k, q: jnp.concatenate([k, q], axis=0), ks, qs)
    grams = each(mxu_nt, kqs, ks)
    lowers = each(lambda rate, gram: jnp.where(below, rate * gram[:CHUNK], 0.0), rates2, grams)
    scores = each(lambda gram: jnp.where(reach, gram[CHUNK:], 0.0).astype(BF16), grams)
    inverses = unit_lower_inverse(lowers)
    nows = [state[head] for head in heads]
    seens = each(
        lambda kq, now: mxu(
            jnp.concatenate([kq, kq], axis=1), jnp.concatenate(split(now), axis=0)
        ),
        kqs,
        nows,
    )

    def right_side(head):
        scaled = rates2[head] * seens[head][:CHUNK]
        own = rates[head] * v_ref[:, :, cols[head]].reshape(CHUNK, DK).astype(F32)
        return split(jnp.concatenate([own - scaled[:, :DK], -scaled[:, DK:]], axis=1))

    rights = each(right_side, heads)
    deltas = each(lambda inverse, right: split(mxu3(inverse, right)), inverses, rights)

    def stepped(k, now, delta):
        k_t = k.astype(F32).T.astype(BF16)
        return now + mxu(jnp.concatenate([k_t, k_t], axis=1), jnp.concatenate(delta, axis=0))

    nexts = each(stepped, ks, nows, deltas)
    outs = each(
        lambda scale, seen, score, delta: scale * (seen[CHUNK:] + mxu(score, delta[0])),
        q_scales,
        seens,
        scores,
        deltas,
    )
    for head in heads:
        state[head] = nexts[head]
        oe_ref[:, cols[head]] = outs[head][:, :DK].astype(BF16)
        oe_ref[:, slice((group + head) * DK, (group + head + 1) * DK)] = outs[head][:, DK:].astype(
            BF16
        )

    @pl.when(chunk == pl.num_programs(0) - 1)
    def _():
        for head in heads:
            if first:
                end_ref[head] = nexts[head]
            else:
                s_ref[head] = nexts[head][:, :DK]
                p_ref[head] = nexts[head][:, DK:].astype(BF16)


def local_half(queries, keys, values, beta, start=None):
    tokens, width = queries.shape
    group = width // DK
    tile = CHUNK // REFL
    steps = tokens // tile // 2
    first = start is None
    skip = 0 if first else steps
    refl = pl.BlockSpec((tile, REFL, width), lambda c: (c + skip, 0, 0))
    whole = pl.BlockSpec((group, DK, 2 * DK), lambda c: (0, 0, 0))
    square = pl.BlockSpec((group, DK, DK), lambda c: (0, 0, 0))
    rows = jax.ShapeDtypeStruct((steps * tile, 2 * width), BF16)
    return pl.pallas_call(
        functools.partial(chunk_kernel, group, first),
        grid=(steps,),
        in_specs=[
            pl.BlockSpec((tile, width), lambda c: (c + skip, 0)),
            refl,
            refl,
            pl.BlockSpec((CHUNK, group), lambda c: (c + skip, 0)),
        ]
        + ([] if first else [whole]),
        out_specs=[pl.BlockSpec((tile, 2 * width), lambda c: (c, 0))]
        + ([whole] if first else [square, square]),
        out_shape=[rows]
        + (
            [jax.ShapeDtypeStruct((group, DK, 2 * DK), F32)]
            if first
            else [
                jax.ShapeDtypeStruct((group, DK, DK), F32),
                jax.ShapeDtypeStruct((group, DK, DK), BF16),
            ]
        ),
        scratch_shapes=[pltpu.VMEM((group, DK, 2 * DK), F32)],
        compiler_params=pltpu.CompilerParams(vmem_limit_bytes=56 * 1024 * 1024),
        cost_estimate=pl.CostEstimate(
            flops=200 * tokens * width * DK, bytes_accessed=8 * tokens * width, transcendentals=0
        ),
        name="local_half",
    )(queries, keys, values, beta, *([] if first else [start]))


def norm_kernel(first_ref, second_ref, s_ref, g_ref, out_ref):
    group = s_ref.shape[0]
    heads = range(group)
    cols = [slice(head * DK, (head + 1) * DK) for head in heads]
    tile = min(128, first_ref.shape[0])
    for half, oe_ref in enumerate((first_ref, second_ref)):
        for at in range(0, oe_ref.shape[0], tile):
            rows = slice(at, at + tile)
            to = slice(half * oe_ref.shape[0] + at, half * oe_ref.shape[0] + at + tile)
            seen = [
                mxu(oe_ref[rows, (group + head) * DK : (group + head + 1) * DK], s_ref[head])
                for head in heads
            ]
            readouts = [oe_ref[rows, cols[head]].astype(F32) + seen[head] for head in heads]
            scales = each(
                lambda x: lax.rsqrt(jnp.mean(x * x, axis=-1, keepdims=True) + TINY), readouts
            )
            for head in heads:
                out_ref[to, cols[head]] = (
                    readouts[head] * scales[head] * g_ref[:, cols[head]]
                ).astype(BF16)


def normed_rows(first, second, incoming, gain):
    width = gain.shape[0]
    tokens = 2 * first.shape[0]
    return pl.pallas_call(
        norm_kernel,
        in_specs=[pl.BlockSpec(memory_space=pltpu.VMEM)] * 4,
        out_specs=pl.BlockSpec(memory_space=pltpu.VMEM),
        out_shape=jax.ShapeDtypeStruct((tokens, width), BF16),
        cost_estimate=pl.CostEstimate(
            flops=2 * tokens * width * DK, bytes_accessed=6 * tokens * width, transcendentals=0
        ),
        name="normed_rows",
    )(first, second, incoming, gain.reshape(1, width))


def project_kernel(choices, place_ref, first_ref, a_ref, *refs):
    weights = refs[: sum(choices)]
    give_ref, keep_ref, held, sems = refs[sum(choices) :]
    half, block = len(choices) // 2, held.shape[2]
    at = 0
    for slot, options in enumerate(choices):
        here = weights[at : at + options]
        at += options
        if options == 1:
            pltpu.make_async_copy(here[0], held.at[slot], sems.at[slot]).start()
            continue
        for option in range(2):

            @pl.when(first_ref[slot] == 1 - option)
            def _():
                pltpu.make_async_copy(here[option], held.at[slot], sems.at[slot]).start()

    at = 0
    for slot, options in enumerate(choices):
        pltpu.make_async_copy(weights[at], held.at[slot], sems.at[slot]).wait()
        at += options
        product = mxu(a_ref[...], held[slot]).astype(BF16)
        place = place_ref[slot]

        @pl.when(place < half)
        def _():
            give_ref[:, pl.ds(pl.multiple_of(place * block, block), block)] = product

        @pl.when(place >= half)
        def _():
            keep_ref[:, pl.ds(pl.multiple_of((place - half) * block, block), block)] = product


def project(places, first, rows, weights):
    tokens, depth = rows.shape
    count = len(weights)
    block = weights[0][0].shape[1]
    choices = tuple(len(options) for options in weights)
    half = pl.BlockSpec(memory_space=pltpu.VMEM)
    shape = jax.ShapeDtypeStruct((tokens, count // 2 * block), BF16)
    return pl.pallas_call(
        functools.partial(project_kernel, choices),
        in_specs=[pl.BlockSpec(memory_space=pltpu.SMEM)] * 2
        + [half]
        + [pl.BlockSpec(memory_space=pl.ANY)] * sum(choices),
        out_specs=[half, half],
        out_shape=[shape, shape],
        scratch_shapes=[
            pltpu.VMEM((count, depth, block), BF16),
            pltpu.SemaphoreType.DMA((count,)),
        ],
        compiler_params=pltpu.CompilerParams(vmem_limit_bytes=48 * 1024 * 1024),
        cost_estimate=pl.CostEstimate(
            flops=2 * tokens * depth * block * count,
            bytes_accessed=2 * (tokens * depth + (tokens + depth) * block * count),
            transcendentals=0,
        ),
        name="project",
    )(places, first, rows, *[w for options in weights for w in options])


def halving_order(count):
    order = [0]
    bit = count // 2
    while bit >= 1:
        order = [m | bit for m in order] + order
        bit //= 2
    return order


def head_sum(give, keep):
    count = lax.axis_size("head")
    bit = 1
    while bit < count:
        pairs = [(i, i ^ bit) for i in range(count)]
        got = lax.ppermute(give, "head", pairs)
        total = keep.astype(F32) + got.astype(F32)
        bit *= 2
        half = total.shape[1] // 2
        give, keep = total[:, :half].astype(BF16), total[:, half:]
        if bit >= count:
            return total.astype(BF16)
    return keep


def tied(*values):
    return lax.optimization_barrier(values)


def send(value, axis, pairs):
    return lax.ppermute(value, axis, pairs)


def per_device(queries, keys, values, beta, gain, w_out):
    tokens, width = queries.shape
    heads = width // DK
    ctx, head = lax.axis_size("ctx"), lax.axis_size("head")
    here, side = lax.axis_index("ctx"), lax.axis_index("groups")
    beta_rows = beta.transpose(2, 0, 1).reshape(tokens * REFL, heads)
    half_cols = w_out.shape[1] // 2
    own = lax.dynamic_slice_in_dim(w_out, side * half_cols, half_cols, 1)
    ring = ctx == head and ctx >= 4
    up, down = {0: own}, {0: own}

    def pass_up(step):
        up[step] = send(up[step - 1], "ctx", [(i, i + 1) for i in range(step - 1, ctx - 1)])

    def pass_down(step):
        down[step] = send(down[step - 1], "ctx", [(i + 1, i) for i in range(ctx - step)])

    if ring:
        pass_up(1)
        pass_down(1)
    swap = [(0, 1), (1, 0)]
    near, middle = local_half(queries, keys, values, beta_rows)
    if ring:
        up[1], down[1], middle = tied(up[1], down[1], middle)
        pass_up(2)
        pass_down(2)
    near_other = send(near, "groups", swap)
    far, state_end, total_end = local_half(queries, keys, values, beta_rows, middle)
    far_other = send(far, "groups", swap)

    incoming = jnp.zeros((heads, DK, DK), BF16)
    outgoing = state_end.astype(BF16)
    for hop in range(ctx - 1):
        if hop == 1 and ring:
            up[2], down[2], near_other, outgoing = tied(up[2], down[2], near_other, outgoing)
        incoming = incoming + send(outgoing, "ctx", [(hop, hop + 1)])
        outgoing = (
            jnp.einsum("hde,hef->hdf", total_end, incoming, preferred_element_type=F32) + state_end
        ).astype(BF16)
    if ring:
        for step in range(3, ctx):
            pass_down(step)
        up[2], incoming = tied(up[2], incoming)
        for step in range(3, ctx):
            pass_up(step)
        weights = [(own,)] + [(up[k], down[ctx - k]) for k in range(1, ctx)]
        targets = lax.rem(here + ctx - jnp.arange(ctx), ctx)
        first = (here >= jnp.arange(ctx)).astype(jnp.int32)
    else:
        whole = lax.all_gather(own, "ctx", axis=1, tiled=True)
        weights = [(w,) for w in jnp.split(whole, head, axis=1)]
        targets = jnp.arange(head)
        first = jnp.ones((head,), jnp.int32)
    incoming_other = send(incoming, "groups", swap)
    mine = normed_rows(near, far, incoming, gain)
    other = normed_rows(near_other, far_other, incoming_other, gain)
    distance = targets ^ lax.axis_index("head")
    order = jnp.asarray(halving_order(head), jnp.int32)
    places = jnp.argmax(distance[:, None] == order[None, :], axis=1).astype(jnp.int32)
    other_sum = head_sum(*project(places, first, other, weights))
    mine_sum = head_sum(*project(places, first, mine, weights))
    back = send(other_sum, "groups", swap)
    blocks = mine_sum.shape[1] // half_cols
    if blocks == 1:
        return jnp.where(
            side == 0,
            jnp.concatenate([mine_sum, back], axis=1),
            jnp.concatenate([back, mine_sum], axis=1),
        )
    mine_sum = mine_sum.reshape(tokens, blocks, 1, half_cols)
    back = back.reshape(tokens, blocks, 1, half_cols)
    mixed = jnp.where(
        side == 0,
        jnp.concatenate([mine_sum, back], axis=2),
        jnp.concatenate([back, mine_sum], axis=2),
    )
    return mixed.reshape(tokens, blocks * 2 * half_cols)


def solution(mesh):
    in_specs = (
        P(("groups", "ctx"), "head"),
        P(("groups", "ctx"), None, "head"),
        P(("groups", "ctx"), None, "head"),
        P(None, "head", ("groups", "ctx")),
        P("head"),
        P("head", "ctx"),
    )
    out_specs = P(("groups", "ctx"), "head")
    return jax.shard_map(
        per_device, mesh=mesh, in_specs=in_specs, out_specs=out_specs, check_vma=False
    )
```

```python
import functools

import jax
import jax.numpy as jnp
from jax import lax
from jax.experimental import pallas as pl
from jax.experimental.pallas import tpu as pltpu
from jax.sharding import PartitionSpec as P

DK = 128
REFL = 2
TINY = 1e-06
CHUNK = 128
BASE = 8
F32 = jnp.float32
BF16 = jnp.bfloat16


def tied(*values):
    return lax.optimization_barrier(values)


def mxu(left, right):
    return jnp.dot(left, right, preferred_element_type=F32)


def mxu_nt(left, right):
    return lax.dot_general(left, right, (((1,), (1,)), ((), ())), preferred_element_type=F32)


def split(value):
    high = value.astype(BF16)
    return high, (value - high.astype(F32)).astype(BF16)


def mxu3(left, right):
    (left_high, left_low), (right_high, right_low) = left, right
    wide = jnp.concatenate([left_high, left_high], axis=1)
    tall = jnp.concatenate([right_high, right_low], axis=0)
    return mxu(wide, tall) + mxu(left_low, right_high)


def each(function, *columns):
    return [function(*row) for row in zip(*columns)]


def unit_lower_inverse(lowers):
    size = lowers[0].shape[0]
    lane = lax.broadcasted_iota(jnp.int32, (BASE, size), 1)
    sub = lax.broadcasted_iota(jnp.int32, (BASE, size), 0)
    block_of = lane // BASE
    blocks = range(size // BASE)

    def compacted(lower):
        compact = jnp.zeros((BASE, size), F32)
        for block in blocks:
            rows = lower[block * BASE : (block + 1) * BASE, :]
            compact = jnp.where(block_of == block, rows, compact)
        return compact

    compacts = each(compacted, lowers)
    inverses = [jnp.where(lane % BASE == sub, 1.0, 0.0).astype(F32) for _ in lowers]
    for step in range(BASE - 1):
        factors = each(
            lambda compact: jnp.take_along_axis(compact, block_of * BASE + step, axis=1), compacts
        )
        inverses = each(lambda inv, factor: inv - factor * inv[step : step + 1, :], inverses, factors)
    rows_of = each(lambda inv: [jnp.where(block_of == block, inv, 0.0) for block in blocks], inverses)
    width = BASE
    while width < size:
        pairs = range(size // (2 * width))
        per = width // BASE
        lane_w = lax.broadcasted_iota(jnp.int32, (width, size), 1) // width
        empty = jnp.zeros((width, size), F32)

        def picked(lower):
            return jnp.concatenate(
                [
                    jnp.where(
                        lane_w == 2 * p, lower[(2 * p + 1) * width : (2 * p + 2) * width, :], 0.0
                    )
                    for p in pairs
                ],
                axis=0,
            )

        def spread(inner):
            return jnp.concatenate(
                [x for p in pairs for x in (empty, inner[p * width : (p + 1) * width, :])], axis=0
            )

        halves = each(lambda rows: split(jnp.concatenate(rows, axis=0)), rows_of)
        picks = each(lambda lower: split(picked(lower)), lowers)
        inners = each(mxu3, picks, halves)
        belows = each(
            lambda rows: jnp.concatenate(
                [rows[(2 * p + 1) * per + i] for p in pairs for i in range(per)], axis=0
            ),
            rows_of,
        )
        joins = each(
            lambda below, inner: below - mxu3(split(below), split(spread(inner))), belows, inners
        )

        def placed(rows, joined):
            rows = list(rows)
            for p in pairs:
                for i in range(per):
                    at = (p * per + i) * BASE
                    rows[(2 * p + 1) * per + i] = joined[at : at + BASE, :]
            return rows

        rows_of = each(placed, rows_of, joins)
        width *= 2
    return each(lambda rows: split(jnp.concatenate(rows, axis=0)), rows_of)


def chunk_kernel(group, first, q_ref, k_ref, v_ref, b_ref, *refs):
    if first:
        oe_ref, end_ref, state = refs
    else:
        start_ref, oe_ref, s_ref, p_ref, state = refs
    chunk = pl.program_id(0)
    tokens = CHUNK // REFL

    @pl.when(chunk == 0)
    def _():
        lane = lax.broadcasted_iota(jnp.int32, (DK, 2 * DK), 1)
        sub = lax.broadcasted_iota(jnp.int32, (DK, 2 * DK), 0)
        start = jnp.where(lane == sub + DK, 1.0, 0.0).astype(F32)
        for head in range(group):
            state[head] = start if first else start_ref[head]

    below = lax.broadcasted_iota(jnp.int32, (CHUNK, CHUNK), 0) > lax.broadcasted_iota(
        jnp.int32, (CHUNK, CHUNK), 1
    )
    reach = REFL * lax.broadcasted_iota(jnp.int32, (tokens, CHUNK), 0) + (
        REFL - 1
    ) >= lax.broadcasted_iota(jnp.int32, (tokens, CHUNK), 1)
    heads = range(group)
    cols = [slice(head * DK, (head + 1) * DK) for head in heads]
    ks = [k_ref[:, :, c].reshape(CHUNK, DK) for c in cols]
    qs = [q_ref[:, c] for c in cols]

    def inverse_norm(rows):
        rows = rows.astype(F32)
        return lax.rsqrt(jnp.sum(rows * rows, axis=-1, keepdims=True) + TINY)

    k_scales = each(inverse_norm, ks)
    q_scales = each(inverse_norm, qs)
    rates = [b_ref[:, head : head + 1] * k_scales[head] for head in heads]
    rates2 = each(lambda rate, scale: rate * scale, rates, k_scales)
    kqs = each(lambda k, q: jnp.concatenate([k, q], axis=0), ks, qs)
    grams = each(mxu_nt, kqs, ks)
    lowers = each(lambda rate, gram: jnp.where(below, rate * gram[:CHUNK], 0.0), rates2, grams)
    scores = each(lambda gram: jnp.where(reach, gram[CHUNK:], 0.0).astype(BF16), grams)
    inverses = unit_lower_inverse(lowers)
    nows = [state[head] for head in heads]
    seens = each(
        lambda kq, now: mxu(
            jnp.concatenate([kq, kq], axis=1), jnp.concatenate(split(now), axis=0)
        ),
        kqs,
        nows,
    )

    def right_side(head):
        scaled = rates2[head] * seens[head][:CHUNK]
        own = rates[head] * v_ref[:, :, cols[head]].reshape(CHUNK, DK).astype(F32)
        return split(jnp.concatenate([own - scaled[:, :DK], -scaled[:, DK:]], axis=1))

    rights = each(right_side, heads)
    deltas = each(lambda inverse, right: split(mxu3(inverse, right)), inverses, rights)

    def stepped(k, now, delta):
        k_t = k.astype(F32).T.astype(BF16)
        return now + mxu(jnp.concatenate([k_t, k_t], axis=1), jnp.concatenate(delta, axis=0))

    nexts = each(stepped, ks, nows, deltas)
    outs = each(
        lambda scale, seen, score, delta: scale * (seen[CHUNK:] + mxu(score, delta[0])),
        q_scales,
        seens,
        scores,
        deltas,
    )
    for head in heads:
        state[head] = nexts[head]
        oe_ref[:, cols[head]] = outs[head][:, :DK].astype(BF16)
        oe_ref[:, slice((group + head) * DK, (group + head + 1) * DK)] = outs[head][:, DK:].astype(
            BF16
        )

    @pl.when(chunk == pl.num_programs(0) - 1)
    def _():
        for head in heads:
            if first:
                end_ref[head] = nexts[head]
            else:
                s_ref[head] = nexts[head][:, :DK]
                p_ref[head] = nexts[head][:, DK:].astype(BF16)


def local_part(queries, keys, values, beta, skip, steps, start=None):
    tokens, width = queries.shape
    group = width // DK
    tile = CHUNK // REFL
    first = start is None
    refl = pl.BlockSpec((tile, REFL, width), lambda c: (c + skip, 0, 0))
    whole = pl.BlockSpec((group, DK, 2 * DK), lambda c: (0, 0, 0))
    square = pl.BlockSpec((group, DK, DK), lambda c: (0, 0, 0))
    rows = jax.ShapeDtypeStruct((steps * tile, 2 * width), BF16)
    return pl.pallas_call(
        functools.partial(chunk_kernel, group, first),
        grid=(steps,),
        in_specs=[
            pl.BlockSpec((tile, width), lambda c: (c + skip, 0)),
            refl,
            refl,
            pl.BlockSpec((CHUNK, group), lambda c: (c + skip, 0)),
        ]
        + ([] if first else [whole]),
        out_specs=[pl.BlockSpec((tile, 2 * width), lambda c: (c, 0))]
        + ([whole] if first else [square, square]),
        out_shape=[rows]
        + (
            [jax.ShapeDtypeStruct((group, DK, 2 * DK), F32)]
            if first
            else [
                jax.ShapeDtypeStruct((group, DK, DK), F32),
                jax.ShapeDtypeStruct((group, DK, DK), BF16),
            ]
        ),
        scratch_shapes=[pltpu.VMEM((group, DK, 2 * DK), F32)],
        compiler_params=pltpu.CompilerParams(vmem_limit_bytes=56 * 1024 * 1024),
        cost_estimate=pl.CostEstimate(
            flops=400 * steps * tile * width * DK, bytes_accessed=16 * steps * tile * width, transcendentals=0
        ),
        name="local_part",
    )(queries, keys, values, beta, *([] if first else [start]))


def norm_kernel(first_ref, second_ref, s_ref, g_ref, out_ref):
    group = s_ref.shape[0]
    heads = range(group)
    cols = [slice(head * DK, (head + 1) * DK) for head in heads]
    tile = min(128, second_ref.shape[0])
    for half, oe_ref in enumerate((first_ref, second_ref)):
        for at in range(0, oe_ref.shape[0], tile):
            rows = slice(at, at + tile)
            to = slice(half * first_ref.shape[0] + at, half * first_ref.shape[0] + at + tile)
            seen = [
                mxu(oe_ref[rows, (group + head) * DK : (group + head + 1) * DK], s_ref[head])
                for head in heads
            ]
            readouts = [oe_ref[rows, cols[head]].astype(F32) + seen[head] for head in heads]
            scales = each(
                lambda x: lax.rsqrt(jnp.mean(x * x, axis=-1, keepdims=True) + TINY), readouts
            )
            for head in heads:
                out_ref[to, cols[head]] = (
                    readouts[head] * scales[head] * g_ref[:, cols[head]]
                ).astype(BF16)


def normed_rows(first, second, incoming, gain):
    width = gain.shape[0]
    tokens = first.shape[0] + second.shape[0]
    return pl.pallas_call(
        norm_kernel,
        in_specs=[pl.BlockSpec(memory_space=pltpu.VMEM)] * 4,
        out_specs=pl.BlockSpec(memory_space=pltpu.VMEM),
        out_shape=jax.ShapeDtypeStruct((tokens, width), BF16),
        cost_estimate=pl.CostEstimate(
            flops=2 * tokens * width * DK, bytes_accessed=6 * tokens * width, transcendentals=0
        ),
        name="normed_rows",
    )(first, second, incoming, gain.reshape(1, width))


def project_kernel(choices, place_ref, first_ref, a_ref, *refs):
    count = sum(sum(options) for options in choices)
    weights = list(refs[:count])
    give_ref, keep_ref, held, sems = refs[count:]
    half, block = len(choices) // 2, held.shape[2]
    whole = weights[0]

    def fetch(slot, pieces):
        row = 0
        for piece in pieces:
            rows = pl.ds(row, piece.shape[0])
            pltpu.make_async_copy(piece, held.at[slot, rows], sems.at[slot]).start()
            row += piece.shape[0]

    for slot, options in enumerate(choices):
        for option, pieces in enumerate(options):
            taken, weights = weights[:pieces], weights[pieces:]
            if len(options) == 1:
                fetch(slot, taken)
            else:
                pl.when(first_ref[slot] == 1 - option)(functools.partial(fetch, slot, taken))
    for slot in range(len(choices)):
        pltpu.make_async_copy(whole, held.at[slot], sems.at[slot]).wait()
        product = mxu(a_ref[...], held[slot]).astype(BF16)
        place = place_ref[slot]

        @pl.when(place < half)
        def _():
            give_ref[:, pl.ds(pl.multiple_of(place * block, block), block)] = product

        @pl.when(place >= half)
        def _():
            keep_ref[:, pl.ds(pl.multiple_of((place - half) * block, block), block)] = product


def project(places, first, rows, weights):
    tokens, depth = rows.shape
    count = len(weights)
    block = weights[0][0][0].shape[1]
    choices = tuple(tuple(len(pieces) for pieces in options) for options in weights)
    flat = [piece for options in weights for pieces in options for piece in pieces]
    half = pl.BlockSpec(memory_space=pltpu.VMEM)
    shape = jax.ShapeDtypeStruct((tokens, count // 2 * block), BF16)
    return pl.pallas_call(
        functools.partial(project_kernel, choices),
        in_specs=[pl.BlockSpec(memory_space=pltpu.SMEM)] * 2
        + [half]
        + [pl.BlockSpec(memory_space=pl.ANY)] * len(flat),
        out_specs=[half, half],
        out_shape=[shape, shape],
        scratch_shapes=[
            pltpu.VMEM((count, depth, block), BF16),
            pltpu.SemaphoreType.DMA((count,)),
        ],
        compiler_params=pltpu.CompilerParams(vmem_limit_bytes=48 * 1024 * 1024),
        cost_estimate=pl.CostEstimate(
            flops=2 * tokens * depth * block * count,
            bytes_accessed=2 * (tokens * depth + (tokens + depth) * block * count),
            transcendentals=0,
        ),
        name="project",
    )(places, first, rows, *flat)


def halving_order(count):
    order = [0]
    bit = count // 2
    while bit >= 1:
        order = [m | bit for m in order] + order
        bit //= 2
    return order


def head_sum(give, keep, pieces):
    count = lax.axis_size("head")
    bit = 1
    while bit * 2 < count:
        got = lax.ppermute(give, "head", [(i, i ^ bit) for i in range(count)])
        total = keep.astype(F32) + got.astype(F32)
        half = total.shape[1] // 2
        give, keep = total[:, :half].astype(BF16), total[:, half:]
        bit *= 2
    result = []
    for sent, kept in zip(jnp.split(give, pieces), jnp.split(keep, pieces)):
        got = lax.ppermute(sent, "head", [(i, i ^ bit) for i in range(count)])
        if result:
            kept, result[-1] = tied(kept, result[-1])
        result.append((kept.astype(F32) + got.astype(F32)).astype(BF16))
    return result


def send(value, axis, pairs):
    return lax.ppermute(value, axis, pairs)


def per_device(queries, keys, values, beta, gain, w_out):
    tokens, width = queries.shape
    heads = width // DK
    ctx, head = lax.axis_size("ctx"), lax.axis_size("head")
    here, side = lax.axis_index("ctx"), lax.axis_index("groups")
    beta_rows = beta.transpose(2, 0, 1).reshape(tokens * REFL, heads)
    half_cols = w_out.shape[1] // 2
    own = lax.dynamic_slice_in_dim(w_out, side * half_cols, half_cols, 1)
    ring = ctx == head and ctx == 4
    up, down = {0: own}, {0: own}

    def pass_up(step):
        up[step] = send(up[step - 1], "ctx", [(i, i + 1) for i in range(step - 1, ctx - 1)])

    def pass_down(step):
        down[step] = send(down[step - 1], "ctx", [(i + 1, i) for i in range(ctx - step)])

    if ring:
        pass_up(1)
        pass_down(1)
    swap = [(0, 1), (1, 0)]
    steps = tokens * REFL // CHUNK
    early = steps * 3 // 4
    near, middle = local_part(queries, keys, values, beta_rows, 0, early)
    if ring:
        up[1], down[1], middle = tied(up[1], down[1], middle)
        pass_up(2)
        pass_down(2)
    near_other = send(near, "groups", swap)
    far, state_end, total_end = local_part(
        queries, keys, values, beta_rows, early, steps - early, middle
    )
    far_other = send(far, "groups", swap)

    incoming = jnp.zeros((heads, DK, DK), BF16)
    outgoing = state_end.astype(BF16)
    for hop in range(ctx - 1):
        if hop == 1 and ring:
            up[2], down[2], outgoing = tied(up[2], down[2], outgoing)
            ahead = up[2].shape[0] // 4
            last = [(i, i + 1) for i in range(2, ctx - 1)]
            up_first = send(up[2][:ahead], "ctx", last)
        if hop == 2 and ring:
            up_first, near_other, outgoing = tied(up_first, near_other, outgoing)
        incoming = incoming + send(outgoing, "ctx", [(hop, hop + 1)])
        outgoing = (
            jnp.einsum("hde,hef->hdf", total_end, incoming, preferred_element_type=F32) + state_end
        ).astype(BF16)
    if ring:
        pass_down(3)
        up_rest, incoming = tied(up[2][ahead:], incoming)
        up[3] = [up_first, send(up_rest, "ctx", last)]
        weights = [([own],), ([up[1]], [down[3]]), ([up[2]], [down[2]]), (up[3], [down[1]])]
        targets = lax.rem(here + ctx - jnp.arange(ctx), ctx)
        first = (here >= jnp.arange(ctx)).astype(jnp.int32)
    else:
        whole = lax.all_gather(own, "ctx", axis=1, tiled=True)
        weights = [([w],) for w in jnp.split(whole, head, axis=1)]
        targets = jnp.arange(head)
        first = jnp.ones((head,), jnp.int32)
    incoming_other = send(incoming, "groups", swap)
    mine = normed_rows(near, far, incoming, gain)
    other = normed_rows(near_other, far_other, incoming_other, gain)
    distance = targets ^ lax.axis_index("head")
    order = jnp.asarray(halving_order(head), jnp.int32)
    places = jnp.argmax(distance[:, None] == order[None, :], axis=1).astype(jnp.int32)
    mine, other = tied(mine, other)
    other_sums = head_sum(*project(places, first, other, weights), 2)
    (mine_sum,) = head_sum(*project(places, first, mine, weights), 1)
    back = jnp.concatenate([send(piece, "groups", swap) for piece in other_sums], axis=0)
    blocks = mine_sum.shape[1] // half_cols
    if blocks == 1:
        return jnp.where(
            side == 0,
            jnp.concatenate([mine_sum, back], axis=1),
            jnp.concatenate([back, mine_sum], axis=1),
        )
    mine_sum = mine_sum.reshape(tokens, blocks, 1, half_cols)
    back = back.reshape(tokens, blocks, 1, half_cols)
    mixed = jnp.where(
        side == 0,
        jnp.concatenate([mine_sum, back], axis=2),
        jnp.concatenate([back, mine_sum], axis=2),
    )
    return mixed.reshape(tokens, blocks * 2 * half_cols)


def solution(mesh):
    in_specs = (
        P(("groups", "ctx"), "head"),
        P(("groups", "ctx"), None, "head"),
        P(("groups", "ctx"), None, "head"),
        P(None, "head", ("groups", "ctx")),
        P("head"),
        P("head", "ctx"),
    )
    out_specs = P(("groups", "ctx"), "head")
    return jax.shard_map(
        per_device, mesh=mesh, in_specs=in_specs, out_specs=out_specs, check_vma=False
    )
```

```python
import functools

import jax
import jax.numpy as jnp
from jax import lax
from jax.experimental import pallas as pl
from jax.experimental.pallas import tpu as pltpu
from jax.sharding import PartitionSpec as P

DK = 128
REFL = 2
TINY = 1e-06
CHUNK = 128
BASE = 8
F32 = jnp.float32
BF16 = jnp.bfloat16


def tied(*values):
    return lax.optimization_barrier(values)


def mxu(left, right):
    return jnp.dot(left, right, preferred_element_type=F32)


def mxu_nt(left, right):
    return lax.dot_general(left, right, (((1,), (1,)), ((), ())), preferred_element_type=F32)


def split(value):
    high = value.astype(BF16)
    return high, (value - high.astype(F32)).astype(BF16)


def mxu3(left, right):
    (left_high, left_low), (right_high, right_low) = left, right
    wide = jnp.concatenate([left_high, left_high], axis=1)
    tall = jnp.concatenate([right_high, right_low], axis=0)
    return mxu(wide, tall) + mxu(left_low, right_high)


def each(function, *columns):
    return [function(*row) for row in zip(*columns)]


def unit_lower_inverse(lowers):
    size = lowers[0].shape[0]
    lane = lax.broadcasted_iota(jnp.int32, (BASE, size), 1)
    sub = lax.broadcasted_iota(jnp.int32, (BASE, size), 0)
    block_of = lane // BASE
    blocks = range(size // BASE)

    def compacted(lower):
        compact = jnp.zeros((BASE, size), F32)
        for block in blocks:
            rows = lower[block * BASE : (block + 1) * BASE, :]
            compact = jnp.where(block_of == block, rows, compact)
        return compact

    compacts = each(compacted, lowers)
    inverses = [jnp.where(lane % BASE == sub, 1.0, 0.0).astype(F32) for _ in lowers]
    for step in range(BASE - 1):
        factors = each(
            lambda compact: jnp.take_along_axis(compact, block_of * BASE + step, axis=1), compacts
        )
        inverses = each(lambda inv, factor: inv - factor * inv[step : step + 1, :], inverses, factors)
    rows_of = each(lambda inv: [jnp.where(block_of == block, inv, 0.0) for block in blocks], inverses)
    width = BASE
    while width < size:
        pairs = range(size // (2 * width))
        per = width // BASE
        lane_w = lax.broadcasted_iota(jnp.int32, (width, size), 1) // width
        empty = jnp.zeros((width, size), F32)

        def picked(lower):
            return jnp.concatenate(
                [
                    jnp.where(
                        lane_w == 2 * p, lower[(2 * p + 1) * width : (2 * p + 2) * width, :], 0.0
                    )
                    for p in pairs
                ],
                axis=0,
            )

        def spread(inner):
            return jnp.concatenate(
                [x for p in pairs for x in (empty, inner[p * width : (p + 1) * width, :])], axis=0
            )

        halves = each(lambda rows: split(jnp.concatenate(rows, axis=0)), rows_of)
        picks = each(lambda lower: split(picked(lower)), lowers)
        inners = each(mxu3, picks, halves)
        belows = each(
            lambda rows: jnp.concatenate(
                [rows[(2 * p + 1) * per + i] for p in pairs for i in range(per)], axis=0
            ),
            rows_of,
        )
        joins = each(
            lambda below, inner: below - mxu3(split(below), split(spread(inner))), belows, inners
        )

        def placed(rows, joined):
            rows = list(rows)
            for p in pairs:
                for i in range(per):
                    at = (p * per + i) * BASE
                    rows[(2 * p + 1) * per + i] = joined[at : at + BASE, :]
            return rows

        rows_of = each(placed, rows_of, joins)
        width *= 2
    return each(lambda rows: split(jnp.concatenate(rows, axis=0)), rows_of)


def chunk_kernel(group, first, q_ref, k_ref, v_ref, b_ref, *refs):
    if first:
        oe_ref, end_ref, state = refs
    else:
        start_ref, oe_ref, s_ref, sent_ref, p_ref, state = refs
    chunk = pl.program_id(0)
    tokens = CHUNK // REFL

    @pl.when(chunk == 0)
    def _():
        lane = lax.broadcasted_iota(jnp.int32, (DK, 2 * DK), 1)
        sub = lax.broadcasted_iota(jnp.int32, (DK, 2 * DK), 0)
        start = jnp.where(lane == sub + DK, 1.0, 0.0).astype(F32)
        for head in range(group):
            state[head] = start if first else start_ref[head]

    below = lax.broadcasted_iota(jnp.int32, (CHUNK, CHUNK), 0) > lax.broadcasted_iota(
        jnp.int32, (CHUNK, CHUNK), 1
    )
    reach = REFL * lax.broadcasted_iota(jnp.int32, (tokens, CHUNK), 0) + (
        REFL - 1
    ) >= lax.broadcasted_iota(jnp.int32, (tokens, CHUNK), 1)
    heads = range(group)
    cols = [slice(head * DK, (head + 1) * DK) for head in heads]
    ks = [k_ref[:, :, c].reshape(CHUNK, DK) for c in cols]
    qs = [q_ref[:, c] for c in cols]

    def inverse_norm(rows):
        rows = rows.astype(F32)
        return lax.rsqrt(jnp.sum(rows * rows, axis=-1, keepdims=True) + TINY)

    k_scales = each(inverse_norm, ks)
    q_scales = each(inverse_norm, qs)
    rates = [b_ref[:, head : head + 1] * k_scales[head] for head in heads]
    rates2 = each(lambda rate, scale: rate * scale, rates, k_scales)
    kqs = each(lambda k, q: jnp.concatenate([k, q], axis=0), ks, qs)
    grams = each(mxu_nt, kqs, ks)
    lowers = each(lambda rate, gram: jnp.where(below, rate * gram[:CHUNK], 0.0), rates2, grams)
    scores = each(lambda gram: jnp.where(reach, gram[CHUNK:], 0.0).astype(BF16), grams)
    inverses = unit_lower_inverse(lowers)
    nows = [state[head] for head in heads]
    seens = each(
        lambda kq, now: mxu(
            jnp.concatenate([kq, kq], axis=1), jnp.concatenate(split(now), axis=0)
        ),
        kqs,
        nows,
    )

    def right_side(head):
        scaled = rates2[head] * seens[head][:CHUNK]
        own = rates[head] * v_ref[:, :, cols[head]].reshape(CHUNK, DK).astype(F32)
        return split(jnp.concatenate([own - scaled[:, :DK], -scaled[:, DK:]], axis=1))

    rights = each(right_side, heads)
    deltas = each(lambda inverse, right: split(mxu3(inverse, right)), inverses, rights)

    def stepped(k, now, delta):
        k_t = k.astype(F32).T.astype(BF16)
        return now + mxu(jnp.concatenate([k_t, k_t], axis=1), jnp.concatenate(delta, axis=0))

    nexts = each(stepped, ks, nows, deltas)
    outs = each(
        lambda scale, seen, score, delta: scale * (seen[CHUNK:] + mxu(score, delta[0])),
        q_scales,
        seens,
        scores,
        deltas,
    )
    for head in heads:
        state[head] = nexts[head]
        oe_ref[:, cols[head]] = outs[head][:, :DK].astype(BF16)
        oe_ref[:, slice((group + head) * DK, (group + head + 1) * DK)] = outs[head][:, DK:].astype(
            BF16
        )

    @pl.when(chunk == pl.num_programs(0) - 1)
    def _():
        for head in heads:
            if first:
                end_ref[head] = nexts[head]
            else:
                s_ref[head] = nexts[head][:, :DK]
                sent_ref[head] = nexts[head][:, :DK].astype(BF16)
                p_ref[head] = nexts[head][:, DK:].astype(BF16)


def local_part(queries, keys, values, beta, skip, steps, start=None):
    tokens, width = queries.shape
    group = width // DK
    tile = CHUNK // REFL
    first = start is None
    refl = pl.BlockSpec((tile, REFL, width), lambda c: (c + skip, 0, 0))
    whole = pl.BlockSpec((group, DK, 2 * DK), lambda c: (0, 0, 0))
    square = pl.BlockSpec((group, DK, DK), lambda c: (0, 0, 0))
    rows = jax.ShapeDtypeStruct((steps * tile, 2 * width), BF16)
    return pl.pallas_call(
        functools.partial(chunk_kernel, group, first),
        grid=(steps,),
        in_specs=[
            pl.BlockSpec((tile, width), lambda c: (c + skip, 0)),
            refl,
            refl,
            pl.BlockSpec((CHUNK, group), lambda c: (c + skip, 0)),
        ]
        + ([] if first else [whole]),
        out_specs=[pl.BlockSpec((tile, 2 * width), lambda c: (c, 0))]
        + ([whole] if first else [square] * 3),
        out_shape=[rows]
        + (
            [jax.ShapeDtypeStruct((group, DK, 2 * DK), F32)]
            if first
            else [
                jax.ShapeDtypeStruct((group, DK, DK), F32),
                jax.ShapeDtypeStruct((group, DK, DK), BF16),
                jax.ShapeDtypeStruct((group, DK, DK), BF16),
            ]
        ),
        scratch_shapes=[pltpu.VMEM((group, DK, 2 * DK), F32)],
        compiler_params=pltpu.CompilerParams(vmem_limit_bytes=56 * 1024 * 1024),
        cost_estimate=pl.CostEstimate(
            flops=400 * steps * tile * width * DK, bytes_accessed=16 * steps * tile * width, transcendentals=0
        ),
        name="local_part",
    )(queries, keys, values, beta, *([] if first else [start]))


def norm_kernel(first_ref, second_ref, s_ref, g_ref, out_ref):
    group = s_ref.shape[0]
    heads = range(group)
    cols = [slice(head * DK, (head + 1) * DK) for head in heads]
    for half, oe_ref in enumerate((first_ref, second_ref)):
        tile = oe_ref.shape[0] // 2
        for at in range(0, oe_ref.shape[0], tile):
            rows = slice(at, at + tile)
            to = slice(half * first_ref.shape[0] + at, half * first_ref.shape[0] + at + tile)
            seen = [
                mxu(oe_ref[rows, (group + head) * DK : (group + head + 1) * DK], s_ref[head])
                for head in heads
            ]
            readouts = [oe_ref[rows, cols[head]].astype(F32) + seen[head] for head in heads]
            scales = each(
                lambda x: lax.rsqrt(jnp.mean(x * x, axis=-1, keepdims=True) + TINY), readouts
            )
            for head in heads:
                out_ref[to, cols[head]] = (
                    readouts[head] * scales[head] * g_ref[:, cols[head]]
                ).astype(BF16)


def normed_rows(first, second, incoming, gain):
    width = gain.shape[0]
    tokens = first.shape[0] + second.shape[0]
    return pl.pallas_call(
        norm_kernel,
        in_specs=[pl.BlockSpec(memory_space=pltpu.VMEM)] * 4,
        out_specs=pl.BlockSpec(memory_space=pltpu.VMEM),
        out_shape=jax.ShapeDtypeStruct((tokens, width), BF16),
        cost_estimate=pl.CostEstimate(
            flops=2 * tokens * width * DK, bytes_accessed=6 * tokens * width, transcendentals=0
        ),
        name="normed_rows",
    )(first, second, incoming, gain.reshape(1, width))


def project_kernel(choices, place_ref, first_ref, a_ref, *refs):
    count = sum(sum(options) for options in choices)
    weights = list(refs[:count])
    give_ref, keep_ref, held, sems = refs[count:]
    half, block = len(choices) // 2, held.shape[2]
    whole = weights[0]

    def fetch(slot, pieces):
        row = 0
        for piece in pieces:
            rows = pl.ds(row, piece.shape[0])
            pltpu.make_async_copy(piece, held.at[slot, rows], sems.at[slot]).start()
            row += piece.shape[0]

    for slot, options in enumerate(choices):
        for option, pieces in enumerate(options):
            taken, weights = weights[:pieces], weights[pieces:]
            if len(options) == 1:
                fetch(slot, taken)
            else:
                pl.when(first_ref[slot] == 1 - option)(functools.partial(fetch, slot, taken))
    for slot in range(len(choices)):
        pltpu.make_async_copy(whole, held.at[slot], sems.at[slot]).wait()
        product = mxu(a_ref[...], held[slot]).astype(BF16)
        place = place_ref[slot]

        @pl.when(place < half)
        def _():
            give_ref[:, pl.ds(pl.multiple_of(place * block, block), block)] = product

        @pl.when(place >= half)
        def _():
            keep_ref[:, pl.ds(pl.multiple_of((place - half) * block, block), block)] = product


def project(places, first, rows, weights):
    tokens, depth = rows.shape
    count = len(weights)
    block = weights[0][0][0].shape[1]
    choices = tuple(tuple(len(pieces) for pieces in options) for options in weights)
    flat = [piece for options in weights for pieces in options for piece in pieces]
    half = pl.BlockSpec(memory_space=pltpu.VMEM)
    shape = jax.ShapeDtypeStruct((tokens, count // 2 * block), BF16)
    return pl.pallas_call(
        functools.partial(project_kernel, choices),
        in_specs=[pl.BlockSpec(memory_space=pltpu.SMEM)] * 2
        + [half]
        + [pl.BlockSpec(memory_space=pl.ANY)] * len(flat),
        out_specs=[half, half],
        out_shape=[shape, shape],
        scratch_shapes=[
            pltpu.VMEM((count, depth, block), BF16),
            pltpu.SemaphoreType.DMA((count,)),
        ],
        compiler_params=pltpu.CompilerParams(vmem_limit_bytes=48 * 1024 * 1024),
        cost_estimate=pl.CostEstimate(
            flops=2 * tokens * depth * block * count,
            bytes_accessed=2 * (tokens * depth + (tokens + depth) * block * count),
            transcendentals=0,
        ),
        name="project",
    )(places, first, rows, *flat)


def halving_order(count):
    order = [0]
    bit = count // 2
    while bit >= 1:
        order = [m | bit for m in order] + order
        bit //= 2
    return order


def head_pairs(bit):
    return [(i, i ^ bit) for i in range(lax.axis_size("head"))]


def head_halved(give, keep):
    bit = 1
    while bit * 2 < lax.axis_size("head"):
        got = lax.ppermute(give, "head", head_pairs(bit))
        total = keep.astype(F32) + got.astype(F32)
        half = total.shape[1] // 2
        give, keep = total[:, :half].astype(BF16), total[:, half:]
        bit *= 2
    return give, keep


def summed(keep, got):
    return (keep.astype(F32) + got.astype(F32)).astype(BF16)


def send(value, axis, pairs):
    return lax.ppermute(value, axis, pairs)


def per_device(queries, keys, values, beta, gain, w_out):
    tokens, width = queries.shape
    heads = width // DK
    ctx, head = lax.axis_size("ctx"), lax.axis_size("head")
    here, side = lax.axis_index("ctx"), lax.axis_index("groups")
    beta_rows = beta.transpose(2, 0, 1).reshape(tokens * REFL, heads)
    half_cols = w_out.shape[1] // 2
    own = lax.dynamic_slice_in_dim(w_out, side * half_cols, half_cols, 1)
    ring = ctx == head and ctx == 4
    up, down = {0: own}, {0: own}

    def pass_up(step):
        up[step] = send(up[step - 1], "ctx", [(i, i + 1) for i in range(step - 1, ctx - 1)])

    def pass_down(step):
        down[step] = send(down[step - 1], "ctx", [(i + 1, i) for i in range(ctx - step)])

    if ring:
        pass_up(1)
        pass_down(1)
    swap = [(0, 1), (1, 0)]
    steps = tokens * REFL // CHUNK
    early = steps * 5 // 8
    near, middle = local_part(queries, keys, values, beta_rows, 0, early)
    if ring:
        up[1], down[1], middle = tied(up[1], down[1], middle)
        pass_up(2)
        pass_down(2)
    near_other = send(near, "groups", swap)
    far, state_end, outgoing, total_end = local_part(
        queries, keys, values, beta_rows, early, steps - early, middle
    )
    far_other = send(far, "groups", swap)

    incoming = jnp.zeros((heads, DK, DK), BF16)
    for hop in range(ctx - 1):
        if hop == 1 and ring:
            up[2], down[2], outgoing = tied(up[2], down[2], outgoing)
            ahead = up[2].shape[0] // 4
            last = [(i, i + 1) for i in range(2, ctx - 1)]
            up_first = send(up[2][:ahead], "ctx", last)
        if hop == 2 and ring:
            up_first, near_other, outgoing = tied(up_first, near_other, outgoing)
        incoming = incoming + send(outgoing, "ctx", [(hop, hop + 1)])
        outgoing = (
            jnp.einsum("hde,hef->hdf", total_end, incoming, preferred_element_type=F32) + state_end
        ).astype(BF16)
    if ring:
        pass_down(3)
        up_rest, incoming = tied(up[2][ahead:], incoming)
        up[3] = [up_first, send(up_rest, "ctx", last)]
        weights = [([own],), ([up[1]], [down[3]]), ([up[2]], [down[2]]), (up[3], [down[1]])]
        targets = lax.rem(here + ctx - jnp.arange(ctx), ctx)
        first = (here >= jnp.arange(ctx)).astype(jnp.int32)
    else:
        whole = lax.all_gather(own, "ctx", axis=1, tiled=True)
        weights = [([w],) for w in jnp.split(whole, head, axis=1)]
        targets = jnp.arange(head)
        first = jnp.ones((head,), jnp.int32)
    far_other, incoming = tied(far_other, incoming)
    incoming_other = send(incoming, "groups", swap)
    mine = normed_rows(near, far, incoming, gain)
    other = normed_rows(near_other, far_other, incoming_other, gain)
    distance = targets ^ lax.axis_index("head")
    order = jnp.asarray(halving_order(head), jnp.int32)
    places = jnp.argmax(distance[:, None] == order[None, :], axis=1).astype(jnp.int32)
    mine, other = tied(mine, other)
    give, keep = head_halved(*project(places, first, other, weights))
    own_give, own_keep = head_halved(*project(places, first, mine, weights))
    last_pairs = head_pairs(head // 2)
    give_a, give_b = jnp.split(give, 2)
    keep_a, keep_b = jnp.split(keep, 2)
    got_a = send(give_a, "head", last_pairs)
    got_b = send(give_b, "head", last_pairs)
    got_a, own_give = tied(got_a, own_give)
    back_a = send(summed(keep_a, got_a), "groups", swap)
    own_got = send(own_give, "head", last_pairs)
    back_a, got_b, keep_b = tied(back_a, got_b, keep_b)
    back_b = send(summed(keep_b, got_b), "groups", swap)
    mine_sum = summed(own_keep, own_got)
    back = jnp.concatenate([back_a, back_b], axis=0)
    blocks = mine_sum.shape[1] // half_cols
    if blocks == 1:
        return jnp.where(
            side == 0,
            jnp.concatenate([mine_sum, back], axis=1),
            jnp.concatenate([back, mine_sum], axis=1),
        )
    mine_sum = mine_sum.reshape(tokens, blocks, 1, half_cols)
    back = back.reshape(tokens, blocks, 1, half_cols)
    mixed = jnp.where(
        side == 0,
        jnp.concatenate([mine_sum, back], axis=2),
        jnp.concatenate([back, mine_sum], axis=2),
    )
    return mixed.reshape(tokens, blocks * 2 * half_cols)


def solution(mesh):
    in_specs = (
        P(("groups", "ctx"), "head"),
        P(("groups", "ctx"), None, "head"),
        P(("groups", "ctx"), None, "head"),
        P(None, "head", ("groups", "ctx")),
        P("head"),
        P("head", "ctx"),
    )
    out_specs = P(("groups", "ctx"), "head")
    return jax.shard_map(
        per_device, mesh=mesh, in_specs=in_specs, out_specs=out_specs, check_vma=False
    )
```

```python
import functools

import jax
import jax.numpy as jnp
from jax import lax
from jax.experimental import pallas as pl
from jax.experimental.pallas import tpu as pltpu
from jax.sharding import PartitionSpec as P

DK = 128
REFL = 2
TINY = 1e-06
CHUNK = 128
BASE = 8
F32 = jnp.float32
BF16 = jnp.bfloat16


def tied(*values):
    return lax.optimization_barrier(values)


def mxu(left, right):
    return jnp.dot(left, right, preferred_element_type=F32)


def mxu_nt(left, right):
    return lax.dot_general(left, right, (((1,), (1,)), ((), ())), preferred_element_type=F32)


def split(value):
    high = value.astype(BF16)
    return high, (value - high.astype(F32)).astype(BF16)


def mxu3(left, right):
    (left_high, left_low), (right_high, right_low) = left, right
    wide = jnp.concatenate([left_high, left_high], axis=1)
    tall = jnp.concatenate([right_high, right_low], axis=0)
    return mxu(wide, tall) + mxu(left_low, right_high)


def each(function, *columns):
    return [function(*row) for row in zip(*columns)]


def unit_lower_inverse(lowers):
    size = lowers[0].shape[0]
    lane = lax.broadcasted_iota(jnp.int32, (BASE, size), 1)
    sub = lax.broadcasted_iota(jnp.int32, (BASE, size), 0)
    block_of = lane // BASE
    blocks = range(size // BASE)

    def compacted(lower):
        compact = jnp.zeros((BASE, size), F32)
        for block in blocks:
            rows = lower[block * BASE : (block + 1) * BASE, :]
            compact = jnp.where(block_of == block, rows, compact)
        return compact

    compacts = each(compacted, lowers)
    inverses = [jnp.where(lane % BASE == sub, 1.0, 0.0).astype(F32) for _ in lowers]
    for step in range(BASE - 1):
        factors = each(
            lambda compact: jnp.take_along_axis(compact, block_of * BASE + step, axis=1), compacts
        )
        inverses = each(lambda inv, factor: inv - factor * inv[step : step + 1, :], inverses, factors)
    rows_of = each(lambda inv: [jnp.where(block_of == block, inv, 0.0) for block in blocks], inverses)
    width = BASE
    while width < size:
        pairs = range(size // (2 * width))
        per = width // BASE
        lane_w = lax.broadcasted_iota(jnp.int32, (width, size), 1) // width
        empty = jnp.zeros((width, size), F32)

        def picked(lower):
            return jnp.concatenate(
                [
                    jnp.where(
                        lane_w == 2 * p, lower[(2 * p + 1) * width : (2 * p + 2) * width, :], 0.0
                    )
                    for p in pairs
                ],
                axis=0,
            )

        def spread(inner):
            return jnp.concatenate(
                [x for p in pairs for x in (empty, inner[p * width : (p + 1) * width, :])], axis=0
            )

        halves = each(lambda rows: split(jnp.concatenate(rows, axis=0)), rows_of)
        picks = each(lambda lower: split(picked(lower)), lowers)
        inners = each(mxu3, picks, halves)
        belows = each(
            lambda rows: jnp.concatenate(
                [rows[(2 * p + 1) * per + i] for p in pairs for i in range(per)], axis=0
            ),
            rows_of,
        )
        joins = each(
            lambda below, inner: below - mxu3(split(below), split(spread(inner))), belows, inners
        )

        def placed(rows, joined):
            rows = list(rows)
            for p in pairs:
                for i in range(per):
                    at = (p * per + i) * BASE
                    rows[(2 * p + 1) * per + i] = joined[at : at + BASE, :]
            return rows

        rows_of = each(placed, rows_of, joins)
        width *= 2
    return each(lambda rows: split(jnp.concatenate(rows, axis=0)), rows_of)


def chunk_kernel(group, first, q_ref, k_ref, v_ref, b_ref, *refs):
    if first:
        oe_ref, end_ref, state = refs
    else:
        start_ref, oe_ref, s_ref, sent_ref, p_ref, state = refs
    chunk = pl.program_id(0)
    tokens = CHUNK // REFL

    @pl.when(chunk == 0)
    def _():
        lane = lax.broadcasted_iota(jnp.int32, (DK, 2 * DK), 1)
        sub = lax.broadcasted_iota(jnp.int32, (DK, 2 * DK), 0)
        start = jnp.where(lane == sub + DK, 1.0, 0.0).astype(F32)
        for head in range(group):
            state[head] = start if first else start_ref[head]

    below = lax.broadcasted_iota(jnp.int32, (CHUNK, CHUNK), 0) > lax.broadcasted_iota(
        jnp.int32, (CHUNK, CHUNK), 1
    )
    reach = REFL * lax.broadcasted_iota(jnp.int32, (tokens, CHUNK), 0) + (
        REFL - 1
    ) >= lax.broadcasted_iota(jnp.int32, (tokens, CHUNK), 1)
    heads = range(group)
    cols = [slice(head * DK, (head + 1) * DK) for head in heads]
    ks = [k_ref[:, :, c].reshape(CHUNK, DK) for c in cols]
    qs = [q_ref[:, c] for c in cols]

    def inverse_norm(rows):
        rows = rows.astype(F32)
        return lax.rsqrt(jnp.sum(rows * rows, axis=-1, keepdims=True) + TINY)

    k_scales = each(inverse_norm, ks)
    q_scales = each(inverse_norm, qs)
    rates = [b_ref[:, head : head + 1] * k_scales[head] for head in heads]
    rates2 = each(lambda rate, scale: rate * scale, rates, k_scales)
    kqs = each(lambda k, q: jnp.concatenate([k, q], axis=0), ks, qs)
    grams = each(mxu_nt, kqs, ks)
    lowers = each(lambda rate, gram: jnp.where(below, rate * gram[:CHUNK], 0.0), rates2, grams)
    scores = each(lambda gram: jnp.where(reach, gram[CHUNK:], 0.0).astype(BF16), grams)
    inverses = unit_lower_inverse(lowers)
    nows = [state[head] for head in heads]
    seens = each(
        lambda kq, now: mxu(
            jnp.concatenate([kq, kq], axis=1), jnp.concatenate(split(now), axis=0)
        ),
        kqs,
        nows,
    )

    def right_side(head):
        scaled = rates2[head] * seens[head][:CHUNK]
        own = rates[head] * v_ref[:, :, cols[head]].reshape(CHUNK, DK).astype(F32)
        return split(jnp.concatenate([own - scaled[:, :DK], -scaled[:, DK:]], axis=1))

    rights = each(right_side, heads)
    deltas = each(lambda inverse, right: split(mxu3(inverse, right)), inverses, rights)

    def stepped(k, now, delta):
        k_t = k.astype(F32).T.astype(BF16)
        return now + mxu(jnp.concatenate([k_t, k_t], axis=1), jnp.concatenate(delta, axis=0))

    nexts = each(stepped, ks, nows, deltas)
    outs = each(
        lambda scale, seen, score, delta: scale * (seen[CHUNK:] + mxu(score, delta[0])),
        q_scales,
        seens,
        scores,
        deltas,
    )
    for head in heads:
        state[head] = nexts[head]
        oe_ref[:, cols[head]] = outs[head][:, :DK].astype(BF16)
        oe_ref[:, slice((group + head) * DK, (group + head + 1) * DK)] = outs[head][:, DK:].astype(
            BF16
        )

    @pl.when(chunk == pl.num_programs(0) - 1)
    def _():
        for head in heads:
            if first:
                end_ref[head] = nexts[head]
            else:
                s_ref[head] = nexts[head][:, :DK]
                sent_ref[head] = nexts[head][:, :DK].astype(BF16)
                p_ref[head] = nexts[head][:, DK:].astype(BF16)


def local_part(queries, keys, values, beta, skip, steps, start=None):
    tokens, width = queries.shape
    group = width // DK
    tile = CHUNK // REFL
    first = start is None
    refl = pl.BlockSpec((tile, REFL, width), lambda c: (c + skip, 0, 0))
    whole = pl.BlockSpec((group, DK, 2 * DK), lambda c: (0, 0, 0))
    square = pl.BlockSpec((group, DK, DK), lambda c: (0, 0, 0))
    rows = jax.ShapeDtypeStruct((steps * tile, 2 * width), BF16)
    return pl.pallas_call(
        functools.partial(chunk_kernel, group, first),
        grid=(steps,),
        in_specs=[
            pl.BlockSpec((tile, width), lambda c: (c + skip, 0)),
            refl,
            refl,
            pl.BlockSpec((CHUNK, group), lambda c: (c + skip, 0)),
        ]
        + ([] if first else [whole]),
        out_specs=[pl.BlockSpec((tile, 2 * width), lambda c: (c, 0))]
        + ([whole] if first else [square] * 3),
        out_shape=[rows]
        + (
            [jax.ShapeDtypeStruct((group, DK, 2 * DK), F32)]
            if first
            else [
                jax.ShapeDtypeStruct((group, DK, DK), F32),
                jax.ShapeDtypeStruct((group, DK, DK), BF16),
                jax.ShapeDtypeStruct((group, DK, DK), BF16),
            ]
        ),
        scratch_shapes=[pltpu.VMEM((group, DK, 2 * DK), F32)],
        compiler_params=pltpu.CompilerParams(vmem_limit_bytes=56 * 1024 * 1024),
        cost_estimate=pl.CostEstimate(
            flops=400 * steps * tile * width * DK, bytes_accessed=16 * steps * tile * width, transcendentals=0
        ),
        name="local_part",
    )(queries, keys, values, beta, *([] if first else [start]))


def norm_kernel(first_ref, second_ref, s_ref, g_ref, out_ref):
    group = s_ref.shape[0]
    heads = range(group)
    cols = [slice(head * DK, (head + 1) * DK) for head in heads]
    for half, oe_ref in enumerate((first_ref, second_ref)):
        tile = oe_ref.shape[0] // 2
        for at in range(0, oe_ref.shape[0], tile):
            rows = slice(at, at + tile)
            to = slice(half * first_ref.shape[0] + at, half * first_ref.shape[0] + at + tile)
            seen = [
                mxu(oe_ref[rows, (group + head) * DK : (group + head + 1) * DK], s_ref[head])
                for head in heads
            ]
            readouts = [oe_ref[rows, cols[head]].astype(F32) + seen[head] for head in heads]
            scales = each(
                lambda x: lax.rsqrt(jnp.mean(x * x, axis=-1, keepdims=True) + TINY), readouts
            )
            for head in heads:
                out_ref[to, cols[head]] = (
                    readouts[head] * scales[head] * g_ref[:, cols[head]]
                ).astype(BF16)


def normed_rows(first, second, incoming, gain):
    width = gain.shape[0]
    tokens = first.shape[0] + second.shape[0]
    return pl.pallas_call(
        norm_kernel,
        in_specs=[pl.BlockSpec(memory_space=pltpu.VMEM)] * 4,
        out_specs=pl.BlockSpec(memory_space=pltpu.VMEM),
        out_shape=jax.ShapeDtypeStruct((tokens, width), BF16),
        cost_estimate=pl.CostEstimate(
            flops=2 * tokens * width * DK, bytes_accessed=6 * tokens * width, transcendentals=0
        ),
        name="normed_rows",
    )(first, second, incoming, gain.reshape(1, width))


def project_kernel(choices, place_ref, first_ref, a_ref, *refs):
    count = sum(sum(options) for options in choices)
    weights = list(refs[:count])
    give_ref, keep_ref, held, sems = refs[count:]
    half, block = len(choices) // 2, held.shape[2]
    whole = weights[0]

    def fetch(slot, pieces):
        row = 0
        for piece in pieces:
            rows = pl.ds(row, piece.shape[0])
            pltpu.make_async_copy(piece, held.at[slot, rows], sems.at[slot]).start()
            row += piece.shape[0]

    for slot, options in enumerate(choices):
        for option, pieces in enumerate(options):
            taken, weights = weights[:pieces], weights[pieces:]
            if len(options) == 1:
                fetch(slot, taken)
            else:
                pl.when(first_ref[slot] == 1 - option)(functools.partial(fetch, slot, taken))
    for slot in range(len(choices)):
        pltpu.make_async_copy(whole, held.at[slot], sems.at[slot]).wait()
        product = mxu(a_ref[...], held[slot]).astype(BF16)
        place = place_ref[slot]

        @pl.when(place < half)
        def _():
            give_ref[:, pl.ds(pl.multiple_of(place * block, block), block)] = product

        @pl.when(place >= half)
        def _():
            keep_ref[:, pl.ds(pl.multiple_of((place - half) * block, block), block)] = product


def project(places, first, rows, weights):
    tokens, depth = rows.shape
    count = len(weights)
    block = weights[0][0][0].shape[1]
    choices = tuple(tuple(len(pieces) for pieces in options) for options in weights)
    flat = [piece for options in weights for pieces in options for piece in pieces]
    half = pl.BlockSpec(memory_space=pltpu.VMEM)
    shape = jax.ShapeDtypeStruct((tokens, count // 2 * block), BF16)
    return pl.pallas_call(
        functools.partial(project_kernel, choices),
        in_specs=[pl.BlockSpec(memory_space=pltpu.SMEM)] * 2
        + [half]
        + [pl.BlockSpec(memory_space=pl.ANY)] * len(flat),
        out_specs=[half, half],
        out_shape=[shape, shape],
        scratch_shapes=[
            pltpu.VMEM((count, depth, block), BF16),
            pltpu.SemaphoreType.DMA((count,)),
        ],
        compiler_params=pltpu.CompilerParams(vmem_limit_bytes=48 * 1024 * 1024),
        cost_estimate=pl.CostEstimate(
            flops=2 * tokens * depth * block * count,
            bytes_accessed=2 * (tokens * depth + (tokens + depth) * block * count),
            transcendentals=0,
        ),
        name="project",
    )(places, first, rows, *flat)


def halving_order(count):
    order = [0]
    bit = count // 2
    while bit >= 1:
        order = [m | bit for m in order] + order
        bit //= 2
    return order


def head_pairs(bit):
    return [(i, i ^ bit) for i in range(lax.axis_size("head"))]


def head_halved(give, keep):
    bit = 1
    while bit * 2 < lax.axis_size("head"):
        got = lax.ppermute(give, "head", head_pairs(bit))
        total = keep.astype(F32) + got.astype(F32)
        half = total.shape[1] // 2
        give, keep = total[:, :half].astype(BF16), total[:, half:]
        bit *= 2
    return give, keep


def summed(keep, got):
    return (keep.astype(F32) + got.astype(F32)).astype(BF16)


def send(value, axis, pairs):
    return lax.ppermute(value, axis, pairs)


def per_device(queries, keys, values, beta, gain, w_out):
    tokens, width = queries.shape
    heads = width // DK
    ctx, head = lax.axis_size("ctx"), lax.axis_size("head")
    here, side = lax.axis_index("ctx"), lax.axis_index("groups")
    beta_rows = beta.transpose(2, 0, 1).reshape(tokens * REFL, heads)
    half_cols = w_out.shape[1] // 2
    own = lax.dynamic_slice_in_dim(w_out, side * half_cols, half_cols, 1)
    ring = ctx == head and ctx == 4
    up, down = {0: own}, {0: own}

    def pass_up(step):
        up[step] = send(up[step - 1], "ctx", [(i, i + 1) for i in range(step - 1, ctx - 1)])

    def pass_down(step):
        down[step] = send(down[step - 1], "ctx", [(i + 1, i) for i in range(ctx - step)])

    if ring:
        pass_up(1)
        pass_down(1)
    swap = [(0, 1), (1, 0)]
    steps = tokens * REFL // CHUNK
    early = steps * 5 // 8
    near, middle = local_part(queries, keys, values, beta_rows, 0, early)
    if ring:
        up[1], down[1], middle = tied(up[1], down[1], middle)
        pass_up(2)
        pass_down(2)
    near_other = send(near, "groups", swap)
    far, state_end, outgoing, total_end = local_part(
        queries, keys, values, beta_rows, early, steps - early, middle
    )
    far_other = send(far, "groups", swap)

    incoming = jnp.zeros((heads, DK, DK), BF16)
    for hop in range(ctx - 1):
        if hop == 1 and ring:
            ahead = up[2].shape[0] // 4
            last = [(i, i + 1) for i in range(2, ctx - 1)]
            up_first = send(up[2][:ahead], "ctx", last)
        if hop == 2 and ring:
            up_first, down[2], near_other, outgoing = tied(up_first, down[2], near_other, outgoing)
        incoming = incoming + send(outgoing, "ctx", [(hop, hop + 1)])
        outgoing = (
            jnp.einsum("hde,hef->hdf", total_end, incoming, preferred_element_type=F32) + state_end
        ).astype(BF16)
    if ring:
        pass_down(3)
        up_rest, incoming = tied(up[2][ahead:], incoming)
        up[3] = [up_first, send(up_rest, "ctx", last)]
        weights = [([own],), ([up[1]], [down[3]]), ([up[2]], [down[2]]), (up[3], [down[1]])]
        targets = lax.rem(here + ctx - jnp.arange(ctx), ctx)
        first = (here >= jnp.arange(ctx)).astype(jnp.int32)
    else:
        whole = lax.all_gather(own, "ctx", axis=1, tiled=True)
        weights = [([w],) for w in jnp.split(whole, head, axis=1)]
        targets = jnp.arange(head)
        first = jnp.ones((head,), jnp.int32)
    far_other, incoming = tied(far_other, incoming)
    incoming_other = send(incoming, "groups", swap)
    mine = normed_rows(near, far, incoming, gain)
    other = normed_rows(near_other, far_other, incoming_other, gain)
    distance = targets ^ lax.axis_index("head")
    order = jnp.asarray(halving_order(head), jnp.int32)
    places = jnp.argmax(distance[:, None] == order[None, :], axis=1).astype(jnp.int32)
    mine, other = tied(mine, other)
    give, keep = head_halved(*project(places, first, other, weights))
    own_give, own_keep = head_halved(*project(places, first, mine, weights))
    last_pairs = head_pairs(head // 2)
    give_a, give_b = jnp.split(give, 2)
    keep_a, keep_b = jnp.split(keep, 2)
    got_a = send(give_a, "head", last_pairs)
    give_b, own_give = tied(give_b, own_give)
    got_b = send(give_b, "head", last_pairs)
    got_a, own_give = tied(got_a, own_give)
    back_a = send(summed(keep_a, got_a), "groups", swap)
    own_got = send(own_give, "head", last_pairs)
    back_a, got_b, keep_b = tied(back_a, got_b, keep_b)
    back_b = send(summed(keep_b, got_b), "groups", swap)
    mine_sum = summed(own_keep, own_got)
    back = jnp.concatenate([back_a, back_b], axis=0)
    blocks = mine_sum.shape[1] // half_cols
    if blocks == 1:
        return jnp.where(
            side == 0,
            jnp.concatenate([mine_sum, back], axis=1),
            jnp.concatenate([back, mine_sum], axis=1),
        )
    mine_sum = mine_sum.reshape(tokens, blocks, 1, half_cols)
    back = back.reshape(tokens, blocks, 1, half_cols)
    mixed = jnp.where(
        side == 0,
        jnp.concatenate([mine_sum, back], axis=2),
        jnp.concatenate([back, mine_sum], axis=2),
    )
    return mixed.reshape(tokens, blocks * 2 * half_cols)


def solution(mesh):
    in_specs = (
        P(("groups", "ctx"), "head"),
        P(("groups", "ctx"), None, "head"),
        P(("groups", "ctx"), None, "head"),
        P(None, "head", ("groups", "ctx")),
        P("head"),
        P("head", "ctx"),
    )
    out_specs = P(("groups", "ctx"), "head")
    return jax.shard_map(
        per_device, mesh=mesh, in_specs=in_specs, out_specs=out_specs, check_vma=False
    )
```

```python
import functools

import jax
import jax.numpy as jnp
from jax import lax
from jax.experimental import pallas as pl
from jax.experimental.pallas import tpu as pltpu
from jax.sharding import PartitionSpec as P

DK = 128
REFL = 2
TINY = 1e-06
CHUNK = 128
BASE = 8
F32 = jnp.float32
BF16 = jnp.bfloat16


def tied(*values):
    return lax.optimization_barrier(values)


def mxu(left, right):
    return jnp.dot(left, right, preferred_element_type=F32)


def mxu_nt(left, right):
    return lax.dot_general(left, right, (((1,), (1,)), ((), ())), preferred_element_type=F32)


def split(value):
    high = value.astype(BF16)
    return high, (value - high.astype(F32)).astype(BF16)


def mxu3(left, right):
    (left_high, left_low), (right_high, right_low) = left, right
    wide = jnp.concatenate([left_high, left_high], axis=1)
    tall = jnp.concatenate([right_high, right_low], axis=0)
    return mxu(wide, tall) + mxu(left_low, right_high)


def each(function, *columns):
    return [function(*row) for row in zip(*columns)]


def unit_lower_inverse(lowers):
    size = lowers[0].shape[0]
    lane = lax.broadcasted_iota(jnp.int32, (BASE, size), 1)
    sub = lax.broadcasted_iota(jnp.int32, (BASE, size), 0)
    block_of = lane // BASE
    blocks = range(size // BASE)

    def compacted(lower):
        compact = jnp.zeros((BASE, size), F32)
        for block in blocks:
            rows = lower[block * BASE : (block + 1) * BASE, :]
            compact = jnp.where(block_of == block, rows, compact)
        return compact

    compacts = each(compacted, lowers)
    inverses = [jnp.where(lane % BASE == sub, 1.0, 0.0).astype(F32) for _ in lowers]
    for step in range(BASE - 1):
        factors = each(
            lambda compact: jnp.take_along_axis(compact, block_of * BASE + step, axis=1), compacts
        )
        inverses = each(lambda inv, factor: inv - factor * inv[step : step + 1, :], inverses, factors)
    rows_of = each(lambda inv: [jnp.where(block_of == block, inv, 0.0) for block in blocks], inverses)
    width = BASE
    while width < size:
        pairs = range(size // (2 * width))
        per = width // BASE
        lane_w = lax.broadcasted_iota(jnp.int32, (width, size), 1) // width
        empty = jnp.zeros((width, size), F32)

        def picked(lower):
            return jnp.concatenate(
                [
                    jnp.where(
                        lane_w == 2 * p, lower[(2 * p + 1) * width : (2 * p + 2) * width, :], 0.0
                    )
                    for p in pairs
                ],
                axis=0,
            )

        def spread(inner):
            return jnp.concatenate(
                [x for p in pairs for x in (empty, inner[p * width : (p + 1) * width, :])], axis=0
            )

        halves = each(lambda rows: split(jnp.concatenate(rows, axis=0)), rows_of)
        picks = each(lambda lower: split(picked(lower)), lowers)
        inners = each(mxu3, picks, halves)
        belows = each(
            lambda rows: jnp.concatenate(
                [rows[(2 * p + 1) * per + i] for p in pairs for i in range(per)], axis=0
            ),
            rows_of,
        )
        joins = each(
            lambda below, inner: below - mxu3(split(below), split(spread(inner))), belows, inners
        )

        def placed(rows, joined):
            rows = list(rows)
            for p in pairs:
                for i in range(per):
                    at = (p * per + i) * BASE
                    rows[(2 * p + 1) * per + i] = joined[at : at + BASE, :]
            return rows

        rows_of = each(placed, rows_of, joins)
        width *= 2
    return each(lambda rows: split(jnp.concatenate(rows, axis=0)), rows_of)


def chunk_kernel(group, first, q_ref, k_ref, v_ref, b_ref, *refs):
    if first:
        oe_ref, end_ref, state = refs
    else:
        start_ref, oe_ref, s_ref, sent_ref, p_ref, state = refs
    chunk = pl.program_id(0)
    tokens = CHUNK // REFL

    @pl.when(chunk == 0)
    def _():
        lane = lax.broadcasted_iota(jnp.int32, (DK, 2 * DK), 1)
        sub = lax.broadcasted_iota(jnp.int32, (DK, 2 * DK), 0)
        start = jnp.where(lane == sub + DK, 1.0, 0.0).astype(F32)
        for head in range(group):
            state[head] = start if first else start_ref[head]

    below = lax.broadcasted_iota(jnp.int32, (CHUNK, CHUNK), 0) > lax.broadcasted_iota(
        jnp.int32, (CHUNK, CHUNK), 1
    )
    reach = REFL * lax.broadcasted_iota(jnp.int32, (tokens, CHUNK), 0) + (
        REFL - 1
    ) >= lax.broadcasted_iota(jnp.int32, (tokens, CHUNK), 1)
    heads = range(group)
    cols = [slice(head * DK, (head + 1) * DK) for head in heads]
    ks = [k_ref[:, :, c].reshape(CHUNK, DK) for c in cols]
    qs = [q_ref[:, c] for c in cols]

    def inverse_norm(rows):
        rows = rows.astype(F32)
        return lax.rsqrt(jnp.sum(rows * rows, axis=-1, keepdims=True) + TINY)

    k_scales = each(inverse_norm, ks)
    q_scales = each(inverse_norm, qs)
    rates = [b_ref[:, head : head + 1] * k_scales[head] for head in heads]
    rates2 = each(lambda rate, scale: rate * scale, rates, k_scales)
    kqs = each(lambda k, q: jnp.concatenate([k, q], axis=0), ks, qs)
    grams = each(mxu_nt, kqs, ks)
    lowers = each(lambda rate, gram: jnp.where(below, rate * gram[:CHUNK], 0.0), rates2, grams)
    scores = each(lambda gram: jnp.where(reach, gram[CHUNK:], 0.0).astype(BF16), grams)
    inverses = unit_lower_inverse(lowers)
    nows = [state[head] for head in heads]
    seens = each(
        lambda kq, now: mxu(
            jnp.concatenate([kq, kq], axis=1), jnp.concatenate(split(now), axis=0)
        ),
        kqs,
        nows,
    )

    def right_side(head):
        scaled = rates2[head] * seens[head][:CHUNK]
        own = rates[head] * v_ref[:, :, cols[head]].reshape(CHUNK, DK).astype(F32)
        return split(jnp.concatenate([own - scaled[:, :DK], -scaled[:, DK:]], axis=1))

    rights = each(right_side, heads)
    deltas = each(lambda inverse, right: split(mxu3(inverse, right)), inverses, rights)

    def stepped(k, now, delta):
        k_t = k.astype(F32).T.astype(BF16)
        return now + mxu(jnp.concatenate([k_t, k_t], axis=1), jnp.concatenate(delta, axis=0))

    nexts = each(stepped, ks, nows, deltas)
    outs = each(
        lambda scale, seen, score, delta: scale * (seen[CHUNK:] + mxu(score, delta[0])),
        q_scales,
        seens,
        scores,
        deltas,
    )
    for head in heads:
        state[head] = nexts[head]
        oe_ref[:, cols[head]] = outs[head][:, :DK].astype(BF16)
        oe_ref[:, slice((group + head) * DK, (group + head + 1) * DK)] = outs[head][:, DK:].astype(
            BF16
        )

    @pl.when(chunk == pl.num_programs(0) - 1)
    def _():
        for head in heads:
            if first:
                end_ref[head] = nexts[head]
            else:
                s_ref[head] = nexts[head][:, :DK]
                sent_ref[head] = nexts[head][:, :DK].astype(BF16)
                p_ref[head] = nexts[head][:, DK:].astype(BF16)


def local_part(queries, keys, values, beta, skip, steps, start=None):
    tokens, width = queries.shape
    group = width // DK
    tile = CHUNK // REFL
    first = start is None
    refl = pl.BlockSpec((tile, REFL, width), lambda c: (c + skip, 0, 0))
    whole = pl.BlockSpec((group, DK, 2 * DK), lambda c: (0, 0, 0))
    square = pl.BlockSpec((group, DK, DK), lambda c: (0, 0, 0))
    rows = jax.ShapeDtypeStruct((steps * tile, 2 * width), BF16)
    return pl.pallas_call(
        functools.partial(chunk_kernel, group, first),
        grid=(steps,),
        in_specs=[
            pl.BlockSpec((tile, width), lambda c: (c + skip, 0)),
            refl,
            refl,
            pl.BlockSpec((CHUNK, group), lambda c: (c + skip, 0)),
        ]
        + ([] if first else [whole]),
        out_specs=[pl.BlockSpec((tile, 2 * width), lambda c: (c, 0))]
        + ([whole] if first else [square] * 3),
        out_shape=[rows]
        + (
            [jax.ShapeDtypeStruct((group, DK, 2 * DK), F32)]
            if first
            else [
                jax.ShapeDtypeStruct((group, DK, DK), F32),
                jax.ShapeDtypeStruct((group, DK, DK), BF16),
                jax.ShapeDtypeStruct((group, DK, DK), BF16),
            ]
        ),
        scratch_shapes=[pltpu.VMEM((group, DK, 2 * DK), F32)],
        compiler_params=pltpu.CompilerParams(vmem_limit_bytes=56 * 1024 * 1024),
        cost_estimate=pl.CostEstimate(
            flops=400 * steps * tile * width * DK, bytes_accessed=16 * steps * tile * width, transcendentals=0
        ),
        name="local_part",
    )(queries, keys, values, beta, *([] if first else [start]))


def norm_kernel(first_ref, second_ref, s_ref, g_ref, out_ref):
    group = s_ref.shape[0]
    heads = range(group)
    cols = [slice(head * DK, (head + 1) * DK) for head in heads]
    for half, oe_ref in enumerate((first_ref, second_ref)):
        tile = oe_ref.shape[0] // 2
        for at in range(0, oe_ref.shape[0], tile):
            rows = slice(at, at + tile)
            to = slice(half * first_ref.shape[0] + at, half * first_ref.shape[0] + at + tile)
            seen = [
                mxu(oe_ref[rows, (group + head) * DK : (group + head + 1) * DK], s_ref[head])
                for head in heads
            ]
            readouts = [oe_ref[rows, cols[head]].astype(F32) + seen[head] for head in heads]
            scales = each(
                lambda x: lax.rsqrt(jnp.mean(x * x, axis=-1, keepdims=True) + TINY), readouts
            )
            for head in heads:
                out_ref[to, cols[head]] = (
                    readouts[head] * scales[head] * g_ref[:, cols[head]]
                ).astype(BF16)


def normed_rows(first, second, incoming, gain):
    width = gain.shape[0]
    tokens = first.shape[0] + second.shape[0]
    return pl.pallas_call(
        norm_kernel,
        in_specs=[pl.BlockSpec(memory_space=pltpu.VMEM)] * 4,
        out_specs=pl.BlockSpec(memory_space=pltpu.VMEM),
        out_shape=jax.ShapeDtypeStruct((tokens, width), BF16),
        cost_estimate=pl.CostEstimate(
            flops=2 * tokens * width * DK, bytes_accessed=6 * tokens * width, transcendentals=0
        ),
        name="normed_rows",
    )(first, second, incoming, gain.reshape(1, width))


def project_kernel(choices, place_ref, first_ref, a_ref, *refs):
    count = sum(sum(options) for options in choices)
    weights = list(refs[:count])
    *done, give_ref, keep_ref, held, sems = refs[count:]
    done_ref = done[0] if done else None
    block = held.shape[2]
    half = give_ref.shape[1] // block
    whole = weights[0]

    def fetch(slot, pieces):
        row = 0
        for piece in pieces:
            rows = pl.ds(row, piece.shape[0])
            pltpu.make_async_copy(piece, held.at[slot, rows], sems.at[slot]).start()
            row += piece.shape[0]

    for slot, options in enumerate(choices):
        for option, pieces in enumerate(options):
            taken, weights = weights[:pieces], weights[pieces:]
            if len(options) == 1:
                fetch(slot, taken)
            else:
                pl.when(first_ref[slot] == 1 - option)(functools.partial(fetch, slot, taken))
    def put(place, product):
        @pl.when(place < half)
        def _():
            give_ref[:, pl.ds(pl.multiple_of(place * block, block), block)] = product

        @pl.when(place >= half)
        def _():
            keep_ref[:, pl.ds(pl.multiple_of((place - half) * block, block), block)] = product

    if done_ref is not None:
        for slot in range(done_ref.shape[1] // block):
            put(place_ref[len(choices) + slot], done_ref[:, slot * block : (slot + 1) * block])
    for slot in range(len(choices)):
        pltpu.make_async_copy(whole, held.at[slot], sems.at[slot]).wait()
        put(place_ref[slot], mxu(a_ref[...], held[slot]).astype(BF16))


def product_kernel(a_ref, *refs):
    weights, out_ref = refs[:-1], refs[-1]
    block = weights[0].shape[1]
    for slot, weight in enumerate(weights):
        out_ref[:, slot * block : (slot + 1) * block] = mxu(a_ref[...], weight[...]).astype(BF16)


def products(rows, weights):
    tokens, block = rows.shape[0], weights[0].shape[1]
    vmem = pl.BlockSpec(memory_space=pltpu.VMEM)
    return pl.pallas_call(
        product_kernel,
        in_specs=[vmem] * (1 + len(weights)),
        out_specs=vmem,
        out_shape=jax.ShapeDtypeStruct((tokens, block * len(weights)), BF16),
        compiler_params=pltpu.CompilerParams(vmem_limit_bytes=32 * 1024 * 1024),
        name="products",
    )(rows, *weights)


def project(places, first, rows, weights, done=None):
    tokens, depth = rows.shape
    count = len(weights)
    block = weights[0][0][0].shape[1]
    choices = tuple(tuple(len(pieces) for pieces in options) for options in weights)
    flat = [piece for options in weights for pieces in options for piece in pieces]
    vmem = pl.BlockSpec(memory_space=pltpu.VMEM)
    extra = [] if done is None else [done]
    total = count + sum(array.shape[1] // block for array in extra)
    shape = jax.ShapeDtypeStruct((tokens, total // 2 * block), BF16)
    return pl.pallas_call(
        functools.partial(project_kernel, choices),
        in_specs=[pl.BlockSpec(memory_space=pltpu.SMEM)] * 2
        + [vmem]
        + [pl.BlockSpec(memory_space=pl.ANY)] * len(flat)
        + [vmem] * len(extra),
        out_specs=[vmem, vmem],
        out_shape=[shape, shape],
        scratch_shapes=[
            pltpu.VMEM((count, depth, block), BF16),
            pltpu.SemaphoreType.DMA((count,)),
        ],
        compiler_params=pltpu.CompilerParams(vmem_limit_bytes=48 * 1024 * 1024),
        cost_estimate=pl.CostEstimate(
            flops=2 * tokens * depth * block * count,
            bytes_accessed=2 * (tokens * depth + (tokens + depth) * block * count),
            transcendentals=0,
        ),
        name="project",
    )(places, first, rows, *flat, *extra)


def halving_order(count):
    order = [0]
    bit = count // 2
    while bit >= 1:
        order = [m | bit for m in order] + order
        bit //= 2
    return order


def head_pairs(bit):
    return [(i, i ^ bit) for i in range(lax.axis_size("head"))]


def head_halved(give, keep):
    bit = 1
    while bit * 2 < lax.axis_size("head"):
        got = lax.ppermute(give, "head", head_pairs(bit))
        total = keep.astype(F32) + got.astype(F32)
        half = total.shape[1] // 2
        give, keep = total[:, :half].astype(BF16), total[:, half:]
        bit *= 2
    return give, keep


def summed(keep, got):
    return (keep.astype(F32) + got.astype(F32)).astype(BF16)


def send(value, axis, pairs):
    return lax.ppermute(value, axis, pairs)


def per_device(queries, keys, values, beta, gain, w_out):
    tokens, width = queries.shape
    heads = width // DK
    ctx, head = lax.axis_size("ctx"), lax.axis_size("head")
    here, side = lax.axis_index("ctx"), lax.axis_index("groups")
    beta_rows = beta.transpose(2, 0, 1).reshape(tokens * REFL, heads)
    half_cols = w_out.shape[1] // 2
    own = lax.dynamic_slice_in_dim(w_out, side * half_cols, half_cols, 1)
    ring = ctx == head and ctx == 4
    up, down = {0: own}, {0: own}

    def pass_up(step):
        up[step] = send(up[step - 1], "ctx", [(i, i + 1) for i in range(step - 1, ctx - 1)])

    def pass_down(step):
        down[step] = send(down[step - 1], "ctx", [(i + 1, i) for i in range(ctx - step)])

    if ring:
        pass_up(1)
        down[0], beta_rows = tied(own, beta_rows)
        pass_down(1)
    swap = [(0, 1), (1, 0)]
    steps = tokens * REFL // CHUNK
    cut = steps * 5 // 8
    near, middle = local_part(queries, keys, values, beta_rows, 0, cut)
    if ring:
        up[1], down[1], middle = tied(up[1], down[1], middle)
        pass_up(2)
        pass_down(2)
    near_other = send(near, "groups", swap)
    far, state_end, outgoing, total_end = local_part(
        queries, keys, values, beta_rows, cut, steps - cut, middle
    )
    far_other = send(far, "groups", swap)

    incoming = jnp.zeros((heads, DK, DK), BF16)
    for hop in range(ctx - 1):
        if hop == 1 and ring:
            ahead = up[2].shape[0] * 3 // 8
            last = [(i, i + 1) for i in range(2, ctx - 1)]
            up_first = send(up[2][:ahead], "ctx", last)
        if hop == 2 and ring:
            up_first, down[2], near_other, outgoing = tied(up_first, down[2], near_other, outgoing)
        incoming = incoming + send(outgoing, "ctx", [(hop, hop + 1)])
        outgoing = (
            jnp.einsum("hde,hef->hdf", total_end, incoming, preferred_element_type=F32) + state_end
        ).astype(BF16)
    if ring:
        pass_down(3)
        up_rest, incoming = tied(up[2][ahead:], incoming)
        up[3] = [up_first, send(up_rest, "ctx", last)]
        weights = [(up[3], [down[1]]), ([up[1]], [down[3]])]
        slots = jnp.asarray([3, 1, 0, 2], jnp.int32)
        targets = lax.rem(here + ctx - slots, ctx)
        first = (here >= slots).astype(jnp.int32)
        early = [own, jnp.where(here >= 2, up[2], down[2])]
    else:
        whole = lax.all_gather(own, "ctx", axis=1, tiled=True)
        weights = [([w],) for w in jnp.split(whole, head, axis=1)]
        targets = jnp.arange(head)
        first = jnp.ones((head,), jnp.int32)
        early = []
    far_other, incoming = tied(far_other, incoming)
    incoming_other = send(incoming, "groups", swap)
    mine = normed_rows(near, far, incoming, gain)
    other = normed_rows(near_other, far_other, incoming_other, gain)
    distance = targets ^ lax.axis_index("head")
    order = jnp.asarray(halving_order(head), jnp.int32)
    places = jnp.argmax(distance[:, None] == order[None, :], axis=1).astype(jnp.int32)
    done = products(mine, early) if early else None
    other_done = products(other, early) if early else None
    if early:
        done, other_done = tied(done, other_done)
    give, keep = head_halved(*project(places, first, other, weights, other_done))
    own_give, own_keep = head_halved(*project(places, first, mine, weights, done))
    last_pairs = head_pairs(head // 2)
    give_a, give_b = jnp.split(give, 2)
    keep_a, keep_b = jnp.split(keep, 2)
    got_a = send(give_a, "head", last_pairs)
    give_b, own_give = tied(give_b, own_give)
    got_b = send(give_b, "head", last_pairs)
    got_a, own_give = tied(got_a, own_give)
    back_a = send(summed(keep_a, got_a), "groups", swap)
    own_got = send(own_give, "head", last_pairs)
    back_a, got_b, keep_b = tied(back_a, got_b, keep_b)
    back_b = send(summed(keep_b, got_b), "groups", swap)
    mine_sum = summed(own_keep, own_got)
    back = jnp.concatenate([back_a, back_b], axis=0)
    blocks = mine_sum.shape[1] // half_cols
    if blocks == 1:
        return jnp.where(
            side == 0,
            jnp.concatenate([mine_sum, back], axis=1),
            jnp.concatenate([back, mine_sum], axis=1),
        )
    mine_sum = mine_sum.reshape(tokens, blocks, 1, half_cols)
    back = back.reshape(tokens, blocks, 1, half_cols)
    mixed = jnp.where(
        side == 0,
        jnp.concatenate([mine_sum, back], axis=2),
        jnp.concatenate([back, mine_sum], axis=2),
    )
    return mixed.reshape(tokens, blocks * 2 * half_cols)


def solution(mesh):
    in_specs = (
        P(("groups", "ctx"), "head"),
        P(("groups", "ctx"), None, "head"),
        P(("groups", "ctx"), None, "head"),
        P(None, "head", ("groups", "ctx")),
        P("head"),
        P("head", "ctx"),
    )
    out_specs = P(("groups", "ctx"), "head")
    return jax.shard_map(
        per_device, mesh=mesh, in_specs=in_specs, out_specs=out_specs, check_vma=False
    )
```

```python
import functools

import jax
import jax.numpy as jnp
from jax import lax
from jax.experimental import pallas as pl
from jax.experimental.pallas import tpu as pltpu
from jax.sharding import PartitionSpec as P

DK = 128
REFL = 2
TINY = 1e-06
CHUNK = 128
BASE = 8
F32 = jnp.float32
BF16 = jnp.bfloat16


def tied(*values):
    return lax.optimization_barrier(values)


def mxu(left, right):
    return jnp.dot(left, right, preferred_element_type=F32)


def mxu_nt(left, right):
    return lax.dot_general(left, right, (((1,), (1,)), ((), ())), preferred_element_type=F32)


def split(value):
    high = value.astype(BF16)
    return high, (value - high.astype(F32)).astype(BF16)


def mxu3(left, right):
    (left_high, left_low), (right_high, right_low) = left, right
    wide = jnp.concatenate([left_high, left_high], axis=1)
    tall = jnp.concatenate([right_high, right_low], axis=0)
    return mxu(wide, tall) + mxu(left_low, right_high)


def each(function, *columns):
    return [function(*row) for row in zip(*columns)]


def unit_lower_inverse(lowers):
    size = lowers[0].shape[0]
    lane = lax.broadcasted_iota(jnp.int32, (BASE, size), 1)
    sub = lax.broadcasted_iota(jnp.int32, (BASE, size), 0)
    block_of = lane // BASE
    blocks = range(size // BASE)

    def compacted(lower):
        compact = jnp.zeros((BASE, size), F32)
        for block in blocks:
            rows = lower[block * BASE : (block + 1) * BASE, :]
            compact = jnp.where(block_of == block, rows, compact)
        return compact

    compacts = each(compacted, lowers)
    inverses = [jnp.where(lane % BASE == sub, 1.0, 0.0).astype(F32) for _ in lowers]
    for step in range(BASE - 1):
        factors = each(
            lambda compact: jnp.take_along_axis(compact, block_of * BASE + step, axis=1), compacts
        )
        inverses = each(lambda inv, factor: inv - factor * inv[step : step + 1, :], inverses, factors)
    rows_of = each(lambda inv: [jnp.where(block_of == block, inv, 0.0) for block in blocks], inverses)
    width = BASE
    while width < size:
        pairs = range(size // (2 * width))
        per = width // BASE
        lane_w = lax.broadcasted_iota(jnp.int32, (width, size), 1) // width
        empty = jnp.zeros((width, size), F32)

        def picked(lower):
            return jnp.concatenate(
                [
                    jnp.where(
                        lane_w == 2 * p, lower[(2 * p + 1) * width : (2 * p + 2) * width, :], 0.0
                    )
                    for p in pairs
                ],
                axis=0,
            )

        def spread(inner):
            return jnp.concatenate(
                [x for p in pairs for x in (empty, inner[p * width : (p + 1) * width, :])], axis=0
            )

        halves = each(lambda rows: split(jnp.concatenate(rows, axis=0)), rows_of)
        picks = each(lambda lower: split(picked(lower)), lowers)
        inners = each(mxu3, picks, halves)
        belows = each(
            lambda rows: jnp.concatenate(
                [rows[(2 * p + 1) * per + i] for p in pairs for i in range(per)], axis=0
            ),
            rows_of,
        )
        joins = each(
            lambda below, inner: below - mxu3(split(below), split(spread(inner))), belows, inners
        )

        def placed(rows, joined):
            rows = list(rows)
            for p in pairs:
                for i in range(per):
                    at = (p * per + i) * BASE
                    rows[(2 * p + 1) * per + i] = joined[at : at + BASE, :]
            return rows

        rows_of = each(placed, rows_of, joins)
        width *= 2
    return each(lambda rows: split(jnp.concatenate(rows, axis=0)), rows_of)


def chunk_kernel(group, first, q_ref, k_ref, v_ref, b_ref, *refs):
    if first:
        oe_ref, end_ref, state = refs
    else:
        start_ref, oe_ref, s_ref, sent_ref, p_ref, state = refs
    chunk = pl.program_id(0)
    tokens = CHUNK // REFL

    @pl.when(chunk == 0)
    def _():
        lane = lax.broadcasted_iota(jnp.int32, (DK, 2 * DK), 1)
        sub = lax.broadcasted_iota(jnp.int32, (DK, 2 * DK), 0)
        start = jnp.where(lane == sub + DK, 1.0, 0.0).astype(F32)
        for head in range(group):
            state[head] = start if first else start_ref[head]

    below = lax.broadcasted_iota(jnp.int32, (CHUNK, CHUNK), 0) > lax.broadcasted_iota(
        jnp.int32, (CHUNK, CHUNK), 1
    )
    reach = REFL * lax.broadcasted_iota(jnp.int32, (tokens, CHUNK), 0) + (
        REFL - 1
    ) >= lax.broadcasted_iota(jnp.int32, (tokens, CHUNK), 1)
    heads = range(group)
    cols = [slice(head * DK, (head + 1) * DK) for head in heads]
    ks = [k_ref[:, :, c].reshape(CHUNK, DK) for c in cols]
    qs = [q_ref[:, c] for c in cols]

    def inverse_norm(rows):
        rows = rows.astype(F32)
        return lax.rsqrt(jnp.sum(rows * rows, axis=-1, keepdims=True) + TINY)

    k_scales = each(inverse_norm, ks)
    q_scales = each(inverse_norm, qs)
    rates = [b_ref[:, head : head + 1] * k_scales[head] for head in heads]
    rates2 = each(lambda rate, scale: rate * scale, rates, k_scales)
    kqs = each(lambda k, q: jnp.concatenate([k, q], axis=0), ks, qs)
    grams = each(mxu_nt, kqs, ks)
    lowers = each(lambda rate, gram: jnp.where(below, rate * gram[:CHUNK], 0.0), rates2, grams)
    scores = each(lambda gram: jnp.where(reach, gram[CHUNK:], 0.0).astype(BF16), grams)
    inverses = unit_lower_inverse(lowers)
    nows = [state[head] for head in heads]
    seens = each(
        lambda kq, now: mxu(
            jnp.concatenate([kq, kq], axis=1), jnp.concatenate(split(now), axis=0)
        ),
        kqs,
        nows,
    )

    def right_side(head):
        scaled = rates2[head] * seens[head][:CHUNK]
        own = rates[head] * v_ref[:, :, cols[head]].reshape(CHUNK, DK).astype(F32)
        return split(jnp.concatenate([own - scaled[:, :DK], -scaled[:, DK:]], axis=1))

    rights = each(right_side, heads)
    deltas = each(lambda inverse, right: split(mxu3(inverse, right)), inverses, rights)

    def stepped(k, now, delta):
        k_t = k.astype(F32).T.astype(BF16)
        return now + mxu(jnp.concatenate([k_t, k_t], axis=1), jnp.concatenate(delta, axis=0))

    nexts = each(stepped, ks, nows, deltas)
    outs = each(
        lambda scale, seen, score, delta: scale * (seen[CHUNK:] + mxu(score, delta[0])),
        q_scales,
        seens,
        scores,
        deltas,
    )
    for head in heads:
        state[head] = nexts[head]
        oe_ref[:, cols[head]] = outs[head][:, :DK].astype(BF16)
        oe_ref[:, slice((group + head) * DK, (group + head + 1) * DK)] = outs[head][:, DK:].astype(
            BF16
        )

    @pl.when(chunk == pl.num_programs(0) - 1)
    def _():
        for head in heads:
            if first:
                end_ref[head] = nexts[head]
            else:
                s_ref[head] = nexts[head][:, :DK]
                sent_ref[head] = nexts[head][:, :DK].astype(BF16)
                p_ref[head] = nexts[head][:, DK:].astype(BF16)


def local_part(queries, keys, values, beta, skip, steps, start=None):
    tokens, width = queries.shape
    group = width // DK
    tile = CHUNK // REFL
    first = start is None
    refl = pl.BlockSpec((tile, REFL, width), lambda c: (c + skip, 0, 0))
    whole = pl.BlockSpec((group, DK, 2 * DK), lambda c: (0, 0, 0))
    square = pl.BlockSpec((group, DK, DK), lambda c: (0, 0, 0))
    rows = jax.ShapeDtypeStruct((steps * tile, 2 * width), BF16)
    return pl.pallas_call(
        functools.partial(chunk_kernel, group, first),
        grid=(steps,),
        in_specs=[
            pl.BlockSpec((tile, width), lambda c: (c + skip, 0)),
            refl,
            refl,
            pl.BlockSpec((CHUNK, group), lambda c: (c + skip, 0)),
        ]
        + ([] if first else [whole]),
        out_specs=[pl.BlockSpec((tile, 2 * width), lambda c: (c, 0))]
        + ([whole] if first else [square] * 3),
        out_shape=[rows]
        + (
            [jax.ShapeDtypeStruct((group, DK, 2 * DK), F32)]
            if first
            else [
                jax.ShapeDtypeStruct((group, DK, DK), F32),
                jax.ShapeDtypeStruct((group, DK, DK), BF16),
                jax.ShapeDtypeStruct((group, DK, DK), BF16),
            ]
        ),
        scratch_shapes=[pltpu.VMEM((group, DK, 2 * DK), F32)],
        compiler_params=pltpu.CompilerParams(vmem_limit_bytes=56 * 1024 * 1024),
        cost_estimate=pl.CostEstimate(
            flops=400 * steps * tile * width * DK, bytes_accessed=16 * steps * tile * width, transcendentals=0
        ),
        name="local_part",
    )(queries, keys, values, beta, *([] if first else [start]))


def norm_kernel(first_ref, second_ref, s_ref, g_ref, out_ref):
    group = s_ref.shape[0]
    heads = range(group)
    cols = [slice(head * DK, (head + 1) * DK) for head in heads]
    for half, oe_ref in enumerate((first_ref, second_ref)):
        tile = oe_ref.shape[0] // 2
        for at in range(0, oe_ref.shape[0], tile):
            rows = slice(at, at + tile)
            to = slice(half * first_ref.shape[0] + at, half * first_ref.shape[0] + at + tile)
            seen = [
                mxu(oe_ref[rows, (group + head) * DK : (group + head + 1) * DK], s_ref[head])
                for head in heads
            ]
            readouts = [oe_ref[rows, cols[head]].astype(F32) + seen[head] for head in heads]
            scales = each(
                lambda x: lax.rsqrt(jnp.mean(x * x, axis=-1, keepdims=True) + TINY), readouts
            )
            for head in heads:
                out_ref[to, cols[head]] = (
                    readouts[head] * scales[head] * g_ref[:, cols[head]]
                ).astype(BF16)


def normed_rows(first, second, incoming, gain):
    width = gain.shape[0]
    tokens = first.shape[0] + second.shape[0]
    return pl.pallas_call(
        norm_kernel,
        in_specs=[pl.BlockSpec(memory_space=pltpu.VMEM)] * 4,
        out_specs=pl.BlockSpec(memory_space=pltpu.VMEM),
        out_shape=jax.ShapeDtypeStruct((tokens, width), BF16),
        cost_estimate=pl.CostEstimate(
            flops=2 * tokens * width * DK, bytes_accessed=6 * tokens * width, transcendentals=0
        ),
        name="normed_rows",
    )(first, second, incoming, gain.reshape(1, width))


def project_kernel(options, pick_ref, a_ref, *refs):
    count = sum(options)
    weights, (*outs, rows, rows_sem, held, sems) = refs[:count], refs[count:]
    copy_rows = pltpu.make_async_copy(a_ref, rows, rows_sem)
    copy_rows.start()

    def fetch(place, pieces):
        at = 0
        for piece in pieces:
            to = held.at[place, pl.ds(at, piece.shape[0])]
            pltpu.make_async_copy(piece, to, sems.at[place]).start()
            at += piece.shape[0]

    for place in range(len(outs)):
        at = 0
        for option, pieces in enumerate(options):
            taken = weights[at : at + pieces]
            at += pieces
            pl.when(pick_ref[place] == option)(functools.partial(fetch, place, taken))
    copy_rows.wait()
    for place, out in enumerate(outs):
        pltpu.make_async_copy(weights[0], held.at[place], sems.at[place]).wait()
        out[...] = mxu(rows[...], held[place]).astype(BF16)


def project(picks, rows, weights):
    tokens, depth = rows.shape
    count = picks.shape[0]
    block = weights[0][0].shape[1]
    flat = [piece for pieces in weights for piece in pieces]
    return pl.pallas_call(
        functools.partial(project_kernel, tuple(len(pieces) for pieces in weights)),
        in_specs=[pl.BlockSpec(memory_space=pltpu.SMEM)]
        + [pl.BlockSpec(memory_space=pl.ANY)] * (1 + len(flat)),
        out_specs=[pl.BlockSpec(memory_space=pltpu.VMEM)] * count,
        out_shape=[jax.ShapeDtypeStruct((tokens, block), BF16)] * count,
        scratch_shapes=[
            pltpu.VMEM((tokens, depth), BF16),
            pltpu.SemaphoreType.DMA,
            pltpu.VMEM((count, depth, block), BF16),
            pltpu.SemaphoreType.DMA((count,)),
        ],
        compiler_params=pltpu.CompilerParams(vmem_limit_bytes=16 * 1024 * 1024),
        cost_estimate=pl.CostEstimate(
            flops=2 * tokens * depth * block * count,
            bytes_accessed=2 * (tokens * depth + (tokens + depth) * block * count),
            transcendentals=0,
        ),
        name="project",
    )(picks, rows, *flat)


def halving_order(count):
    order = [0]
    bit = count // 2
    while bit >= 1:
        order = [m | bit for m in order] + order
        bit //= 2
    return order


def head_pairs(bit):
    return [(i, i ^ bit) for i in range(lax.axis_size("head"))]


def head_halved(give, keep):
    bit = 1
    while bit * 2 < lax.axis_size("head"):
        got = lax.ppermute(give, "head", head_pairs(bit))
        total = keep.astype(F32) + got.astype(F32)
        half = total.shape[1] // 2
        give, keep = total[:, :half].astype(BF16), total[:, half:]
        bit *= 2
    return give, keep


def summed(keep, got):
    return (keep.astype(F32) + got.astype(F32)).astype(BF16)


def send(value, axis, pairs):
    return lax.ppermute(value, axis, pairs)


def per_device(queries, keys, values, beta, gain, w_out):
    tokens, width = queries.shape
    heads = width // DK
    ctx, head = lax.axis_size("ctx"), lax.axis_size("head")
    here, side = lax.axis_index("ctx"), lax.axis_index("groups")
    beta_rows = beta.transpose(2, 0, 1).reshape(tokens * REFL, heads)
    half_cols = w_out.shape[1] // 2
    own = lax.dynamic_slice_in_dim(w_out, side * half_cols, half_cols, 1)
    ring = ctx == head and ctx == 4
    up, down = {0: own}, {0: own}

    def pass_up(step):
        up[step] = send(up[step - 1], "ctx", [(i, i + 1) for i in range(step - 1, ctx - 1)])

    def pass_down(step):
        down[step] = send(down[step - 1], "ctx", [(i + 1, i) for i in range(ctx - step)])

    if ring:
        pass_up(1)
        pass_down(1)
    swap = [(0, 1), (1, 0)]
    steps = tokens * REFL // CHUNK
    early = steps * 5 // 8
    near, middle = local_part(queries, keys, values, beta_rows, 0, early)
    if ring:
        up[1], down[1], middle = tied(up[1], down[1], middle)
        pass_up(2)
        pass_down(2)
    near_other = send(near, "groups", swap)
    far, state_end, outgoing, total_end = local_part(
        queries, keys, values, beta_rows, early, steps - early, middle
    )
    far_other = send(far, "groups", swap)

    incoming = jnp.zeros((heads, DK, DK), BF16)
    for hop in range(ctx - 1):
        if hop == 1 and ring:
            ahead = up[2].shape[0] // 4
            last = [(i, i + 1) for i in range(2, ctx - 1)]
            up_first = send(up[2][:ahead], "ctx", last)
        if hop == 2 and ring:
            up_first, down[2], near_other, outgoing = tied(up_first, down[2], near_other, outgoing)
        incoming = incoming + send(outgoing, "ctx", [(hop, hop + 1)])
        outgoing = (
            jnp.einsum("hde,hef->hdf", total_end, incoming, preferred_element_type=F32) + state_end
        ).astype(BF16)
    if ring:
        pass_down(3)
        up_rest, incoming = tied(up[2][ahead:], incoming)
        up[3] = [up_first, send(up_rest, "ctx", last)]
        weights = [[own], [up[1]], [down[3]], [up[2]], [down[2]], up[3], [down[1]]]
        slots = lax.rem(here + ctx - jnp.arange(ctx), ctx)
        block_of = jnp.where(slots == 0, 0, 2 * slots - (here >= slots).astype(jnp.int32))
    else:
        whole = lax.all_gather(own, "ctx", axis=1, tiled=True)
        weights = [[w] for w in jnp.split(whole, head, axis=1)]
        block_of = jnp.arange(head)
    far_other, incoming = tied(far_other, incoming)
    incoming_other = send(incoming, "groups", swap)
    mine = normed_rows(near, far, incoming, gain)
    other = normed_rows(near_other, far_other, incoming_other, gain)
    mine, other = tied(mine, other)
    order = lax.axis_index("head") ^ jnp.asarray(halving_order(head), jnp.int32)
    picks = jnp.sum(
        jnp.where(order[:, None] == jnp.arange(head)[None, :], block_of[None, :], 0), axis=1
    ).astype(jnp.int32)
    if head == 4:
        near_pairs, last_pairs = head_pairs(1), head_pairs(2)
        sent, kept = project(picks[0::2], other, weights)
        own_sent, own_kept = project(picks[0::2], mine, weights)
        sent, own_sent = send(sent, "head", near_pairs), send(own_sent, "head", near_pairs)
        give_a, give_b = jnp.split(summed(kept, sent), 2)
        own_give = summed(own_kept, own_sent)
        got_a = send(give_a, "head", last_pairs)
        give_b, own_give = tied(give_b, own_give)
        got_b = send(give_b, "head", last_pairs)
        other, mine, got_a = tied(other, mine, got_a)
        sent, kept = project(picks[1::2], other, weights)
        own_sent, own_kept = project(picks[1::2], mine, weights)
        keep = kept.astype(F32) + send(sent, "head", near_pairs).astype(F32)
        own_keep = own_kept.astype(F32) + send(own_sent, "head", near_pairs).astype(F32)
    else:
        last_pairs = head_pairs(head // 2)
        sides = []
        for rows in (other, mine):
            parts = project(picks, rows, weights)
            give, keep = parts[: head // 2], parts[head // 2 :]
            sides += head_halved(jnp.concatenate(give, axis=1), jnp.concatenate(keep, axis=1))
        give, keep, own_give, own_keep = sides
        give_a, give_b = jnp.split(give, 2)
        got_a = send(give_a, "head", last_pairs)
        got_b = send(give_b, "head", last_pairs)
    keep_a, keep_b = jnp.split(keep, 2)
    got_a, own_give = tied(got_a, own_give)
    back_a = send(summed(keep_a, got_a), "groups", swap)
    own_got = send(own_give, "head", last_pairs)
    back_a, got_b, keep_b = tied(back_a, got_b, keep_b)
    back_b = send(summed(keep_b, got_b), "groups", swap)
    mine_sum = summed(own_keep, own_got)
    back = jnp.concatenate([back_a, back_b], axis=0)
    blocks = mine_sum.shape[1] // half_cols
    if blocks == 1:
        return jnp.where(
            side == 0,
            jnp.concatenate([mine_sum, back], axis=1),
            jnp.concatenate([back, mine_sum], axis=1),
        )
    mine_sum = mine_sum.reshape(tokens, blocks, 1, half_cols)
    back = back.reshape(tokens, blocks, 1, half_cols)
    mixed = jnp.where(
        side == 0,
        jnp.concatenate([mine_sum, back], axis=2),
        jnp.concatenate([back, mine_sum], axis=2),
    )
    return mixed.reshape(tokens, blocks * 2 * half_cols)


def solution(mesh):
    in_specs = (
        P(("groups", "ctx"), "head"),
        P(("groups", "ctx"), None, "head"),
        P(("groups", "ctx"), None, "head"),
        P(None, "head", ("groups", "ctx")),
        P("head"),
        P("head", "ctx"),
    )
    out_specs = P(("groups", "ctx"), "head")
    return jax.shard_map(
        per_device, mesh=mesh, in_specs=in_specs, out_specs=out_specs, check_vma=False
    )
```

```python
import functools

import jax
import jax.numpy as jnp
from jax import lax
from jax.experimental import pallas as pl
from jax.experimental.pallas import tpu as pltpu
from jax.sharding import PartitionSpec as P

DK = 128
REFL = 2
TINY = 1e-06
CHUNK = 128
BASE = 8
F32 = jnp.float32
BF16 = jnp.bfloat16


def tied(*values):
    return lax.optimization_barrier(values)


def mxu(left, right):
    return jnp.dot(left, right, preferred_element_type=F32)


def mxu_nt(left, right):
    return lax.dot_general(left, right, (((1,), (1,)), ((), ())), preferred_element_type=F32)


def split(value):
    high = value.astype(BF16)
    return high, (value - high.astype(F32)).astype(BF16)


def mxu3(left, right):
    (left_high, left_low), (right_high, right_low) = left, right
    wide = jnp.concatenate([left_high, left_high], axis=1)
    tall = jnp.concatenate([right_high, right_low], axis=0)
    return mxu(wide, tall) + mxu(left_low, right_high)


def each(function, *columns):
    return [function(*row) for row in zip(*columns)]


def unit_lower_inverse(lowers):
    size = lowers[0].shape[0]
    lane = lax.broadcasted_iota(jnp.int32, (BASE, size), 1)
    sub = lax.broadcasted_iota(jnp.int32, (BASE, size), 0)
    block_of = lane // BASE
    blocks = range(size // BASE)

    def compacted(lower):
        compact = jnp.zeros((BASE, size), F32)
        for block in blocks:
            rows = lower[block * BASE : (block + 1) * BASE, :]
            compact = jnp.where(block_of == block, rows, compact)
        return compact

    compacts = each(compacted, lowers)
    inverses = [jnp.where(lane % BASE == sub, 1.0, 0.0).astype(F32) for _ in lowers]
    for step in range(BASE - 1):
        factors = each(
            lambda compact: jnp.take_along_axis(compact, block_of * BASE + step, axis=1), compacts
        )
        inverses = each(lambda inv, factor: inv - factor * inv[step : step + 1, :], inverses, factors)
    rows_of = each(lambda inv: [jnp.where(block_of == block, inv, 0.0) for block in blocks], inverses)
    width = BASE
    while width < size:
        pairs = range(size // (2 * width))
        per = width // BASE
        lane_w = lax.broadcasted_iota(jnp.int32, (width, size), 1) // width
        empty = jnp.zeros((width, size), F32)

        def picked(lower):
            return jnp.concatenate(
                [
                    jnp.where(
                        lane_w == 2 * p, lower[(2 * p + 1) * width : (2 * p + 2) * width, :], 0.0
                    )
                    for p in pairs
                ],
                axis=0,
            )

        def spread(inner):
            return jnp.concatenate(
                [x for p in pairs for x in (empty, inner[p * width : (p + 1) * width, :])], axis=0
            )

        halves = each(lambda rows: split(jnp.concatenate(rows, axis=0)), rows_of)
        picks = each(lambda lower: split(picked(lower)), lowers)
        inners = each(mxu3, picks, halves)
        belows = each(
            lambda rows: jnp.concatenate(
                [rows[(2 * p + 1) * per + i] for p in pairs for i in range(per)], axis=0
            ),
            rows_of,
        )
        joins = each(
            lambda below, inner: below - mxu3(split(below), split(spread(inner))), belows, inners
        )

        def placed(rows, joined):
            rows = list(rows)
            for p in pairs:
                for i in range(per):
                    at = (p * per + i) * BASE
                    rows[(2 * p + 1) * per + i] = joined[at : at + BASE, :]
            return rows

        rows_of = each(placed, rows_of, joins)
        width *= 2
    return each(lambda rows: split(jnp.concatenate(rows, axis=0)), rows_of)


def chunk_kernel(group, first, q_ref, k_ref, v_ref, b_ref, *refs):
    if first:
        oe_ref, end_ref, state = refs
    else:
        start_ref, oe_ref, s_ref, sent_ref, p_ref, state = refs
    chunk = pl.program_id(0)
    tokens = CHUNK // REFL

    @pl.when(chunk == 0)
    def _():
        lane = lax.broadcasted_iota(jnp.int32, (DK, 2 * DK), 1)
        sub = lax.broadcasted_iota(jnp.int32, (DK, 2 * DK), 0)
        start = jnp.where(lane == sub + DK, 1.0, 0.0).astype(F32)
        for head in range(group):
            state[head] = start if first else start_ref[head]

    below = lax.broadcasted_iota(jnp.int32, (CHUNK, CHUNK), 0) > lax.broadcasted_iota(
        jnp.int32, (CHUNK, CHUNK), 1
    )
    reach = REFL * lax.broadcasted_iota(jnp.int32, (tokens, CHUNK), 0) + (
        REFL - 1
    ) >= lax.broadcasted_iota(jnp.int32, (tokens, CHUNK), 1)
    heads = range(group)
    cols = [slice(head * DK, (head + 1) * DK) for head in heads]
    ks = [k_ref[:, :, c].reshape(CHUNK, DK) for c in cols]
    qs = [q_ref[:, c] for c in cols]

    def inverse_norm(rows):
        rows = rows.astype(F32)
        return lax.rsqrt(jnp.sum(rows * rows, axis=-1, keepdims=True) + TINY)

    k_scales = each(inverse_norm, ks)
    q_scales = each(inverse_norm, qs)
    rates = [b_ref[:, head : head + 1] * k_scales[head] for head in heads]
    rates2 = each(lambda rate, scale: rate * scale, rates, k_scales)
    kqs = each(lambda k, q: jnp.concatenate([k, q], axis=0), ks, qs)
    grams = each(mxu_nt, kqs, ks)
    lowers = each(lambda rate, gram: jnp.where(below, rate * gram[:CHUNK], 0.0), rates2, grams)
    scores = each(lambda gram: jnp.where(reach, gram[CHUNK:], 0.0).astype(BF16), grams)
    inverses = unit_lower_inverse(lowers)
    nows = [state[head] for head in heads]
    seens = each(
        lambda kq, now: mxu(
            jnp.concatenate([kq, kq], axis=1), jnp.concatenate(split(now), axis=0)
        ),
        kqs,
        nows,
    )

    def right_side(head):
        scaled = rates2[head] * seens[head][:CHUNK]
        own = rates[head] * v_ref[:, :, cols[head]].reshape(CHUNK, DK).astype(F32)
        return split(jnp.concatenate([own - scaled[:, :DK], -scaled[:, DK:]], axis=1))

    rights = each(right_side, heads)
    deltas = each(lambda inverse, right: split(mxu3(inverse, right)), inverses, rights)

    def stepped(k, now, delta):
        k_t = k.astype(F32).T.astype(BF16)
        return now + mxu(jnp.concatenate([k_t, k_t], axis=1), jnp.concatenate(delta, axis=0))

    nexts = each(stepped, ks, nows, deltas)
    outs = each(
        lambda scale, seen, score, delta: scale * (seen[CHUNK:] + mxu(score, delta[0])),
        q_scales,
        seens,
        scores,
        deltas,
    )
    for head in heads:
        state[head] = nexts[head]
        oe_ref[:, cols[head]] = outs[head][:, :DK].astype(BF16)
        oe_ref[:, slice((group + head) * DK, (group + head + 1) * DK)] = outs[head][:, DK:].astype(
            BF16
        )

    @pl.when(chunk == pl.num_programs(0) - 1)
    def _():
        for head in heads:
            if first:
                end_ref[head] = nexts[head]
            else:
                s_ref[head] = nexts[head][:, :DK]
                sent_ref[head] = nexts[head][:, :DK].astype(BF16)
                p_ref[head] = nexts[head][:, DK:].astype(BF16)


def local_part(queries, keys, values, beta, skip, steps, start=None):
    tokens, width = queries.shape
    group = width // DK
    tile = CHUNK // REFL
    first = start is None
    refl = pl.BlockSpec((tile, REFL, width), lambda c: (c + skip, 0, 0))
    whole = pl.BlockSpec((group, DK, 2 * DK), lambda c: (0, 0, 0))
    square = pl.BlockSpec((group, DK, DK), lambda c: (0, 0, 0))
    rows = jax.ShapeDtypeStruct((steps * tile, 2 * width), BF16)
    return pl.pallas_call(
        functools.partial(chunk_kernel, group, first),
        grid=(steps,),
        in_specs=[
            pl.BlockSpec((tile, width), lambda c: (c + skip, 0)),
            refl,
            refl,
            pl.BlockSpec((CHUNK, group), lambda c: (c + skip, 0)),
        ]
        + ([] if first else [whole]),
        out_specs=[pl.BlockSpec((tile, 2 * width), lambda c: (c, 0))]
        + ([whole] if first else [square] * 3),
        out_shape=[rows]
        + (
            [jax.ShapeDtypeStruct((group, DK, 2 * DK), F32)]
            if first
            else [
                jax.ShapeDtypeStruct((group, DK, DK), F32),
                jax.ShapeDtypeStruct((group, DK, DK), BF16),
                jax.ShapeDtypeStruct((group, DK, DK), BF16),
            ]
        ),
        scratch_shapes=[pltpu.VMEM((group, DK, 2 * DK), F32)],
        compiler_params=pltpu.CompilerParams(vmem_limit_bytes=56 * 1024 * 1024),
        cost_estimate=pl.CostEstimate(
            flops=400 * steps * tile * width * DK, bytes_accessed=16 * steps * tile * width, transcendentals=0
        ),
        name="local_part",
    )(queries, keys, values, beta, *([] if first else [start]))


def norm_kernel(first_ref, second_ref, s_ref, g_ref, out_ref):
    group = s_ref.shape[0]
    heads = range(group)
    cols = [slice(head * DK, (head + 1) * DK) for head in heads]
    for half, oe_ref in enumerate((first_ref, second_ref)):
        tile = oe_ref.shape[0] // 2
        for at in range(0, oe_ref.shape[0], tile):
            rows = slice(at, at + tile)
            to = slice(half * first_ref.shape[0] + at, half * first_ref.shape[0] + at + tile)
            seen = [
                mxu(oe_ref[rows, (group + head) * DK : (group + head + 1) * DK], s_ref[head])
                for head in heads
            ]
            readouts = [oe_ref[rows, cols[head]].astype(F32) + seen[head] for head in heads]
            scales = each(
                lambda x: lax.rsqrt(jnp.mean(x * x, axis=-1, keepdims=True) + TINY), readouts
            )
            for head in heads:
                out_ref[to, cols[head]] = (
                    readouts[head] * scales[head] * g_ref[:, cols[head]]
                ).astype(BF16)


def normed_rows(first, second, incoming, gain):
    width = gain.shape[0]
    tokens = first.shape[0] + second.shape[0]
    return pl.pallas_call(
        norm_kernel,
        in_specs=[pl.BlockSpec(memory_space=pltpu.VMEM)] * 4,
        out_specs=pl.BlockSpec(memory_space=pltpu.VMEM),
        out_shape=jax.ShapeDtypeStruct((tokens, width), BF16),
        cost_estimate=pl.CostEstimate(
            flops=2 * tokens * width * DK, bytes_accessed=6 * tokens * width, transcendentals=0
        ),
        name="normed_rows",
    )(first, second, incoming, gain.reshape(1, width))


def project_kernel(options, pick_ref, a_ref, *refs):
    count = sum(options)
    weights, (give_ref, keep_ref, rows, rows_sem, held, sems) = refs[:count], refs[count:]
    places, block = held.shape[0], held.shape[2]
    copy_rows = pltpu.make_async_copy(a_ref, rows, rows_sem)
    copy_rows.start()

    def fetch(place, pieces):
        at = 0
        for piece in pieces:
            to = held.at[place, pl.ds(at, piece.shape[0])]
            pltpu.make_async_copy(piece, to, sems.at[place]).start()
            at += piece.shape[0]

    for place in range(places):
        at = 0
        for option, pieces in enumerate(options):
            taken = weights[at : at + pieces]
            at += pieces
            pl.when(pick_ref[place] == option)(functools.partial(fetch, place, taken))
    copy_rows.wait()
    for place in range(places):
        pltpu.make_async_copy(weights[0], held.at[place], sems.at[place]).wait()
        out, at = divmod(place, places // 2)
        (give_ref, keep_ref)[out][:, at * block : (at + 1) * block] = mxu(
            rows[...], held[place]
        ).astype(BF16)


def project(picks, rows, weights):
    tokens, depth = rows.shape
    count = picks.shape[0]
    block = weights[0][0].shape[1]
    flat = [piece for pieces in weights for piece in pieces]
    return pl.pallas_call(
        functools.partial(project_kernel, tuple(len(pieces) for pieces in weights)),
        in_specs=[pl.BlockSpec(memory_space=pltpu.SMEM)]
        + [pl.BlockSpec(memory_space=pl.ANY)] * (1 + len(flat)),
        out_specs=[pl.BlockSpec(memory_space=pltpu.VMEM)] * 2,
        out_shape=[jax.ShapeDtypeStruct((tokens, count // 2 * block), BF16)] * 2,
        scratch_shapes=[
            pltpu.VMEM((tokens, depth), BF16),
            pltpu.SemaphoreType.DMA,
            pltpu.VMEM((count, depth, block), BF16),
            pltpu.SemaphoreType.DMA((count,)),
        ],
        compiler_params=pltpu.CompilerParams(vmem_limit_bytes=58 * 1024 * 1024),
        cost_estimate=pl.CostEstimate(
            flops=2 * tokens * depth * block * count,
            bytes_accessed=2 * (tokens * depth + (tokens + depth) * block * count),
            transcendentals=0,
        ),
        name="project",
    )(picks, rows, *flat)


def halving_order(count):
    order = [0]
    bit = count // 2
    while bit >= 1:
        order = [m | bit for m in order] + order
        bit //= 2
    return order


def head_pairs(bit):
    return [(i, i ^ bit) for i in range(lax.axis_size("head"))]


def head_halved(give, keep):
    bit = 1
    while bit * 2 < lax.axis_size("head"):
        got = lax.ppermute(give, "head", head_pairs(bit))
        total = keep.astype(F32) + got.astype(F32)
        half = total.shape[1] // 2
        give, keep = total[:, :half].astype(BF16), total[:, half:]
        bit *= 2
    return give, keep


def summed(keep, got):
    return (keep.astype(F32) + got.astype(F32)).astype(BF16)


def send(value, axis, pairs):
    return lax.ppermute(value, axis, pairs)


def per_device(queries, keys, values, beta, gain, w_out):
    tokens, width = queries.shape
    heads = width // DK
    ctx, head = lax.axis_size("ctx"), lax.axis_size("head")
    here, side = lax.axis_index("ctx"), lax.axis_index("groups")
    beta_rows = beta.transpose(2, 0, 1).reshape(tokens * REFL, heads)
    half_cols = w_out.shape[1] // 2
    own = lax.dynamic_slice_in_dim(w_out, side * half_cols, half_cols, 1)
    ring = ctx == head and ctx == 4
    up, down = {0: own}, {0: own}

    def pass_up(step):
        up[step] = send(up[step - 1], "ctx", [(i, i + 1) for i in range(step - 1, ctx - 1)])

    def pass_down(step):
        down[step] = send(down[step - 1], "ctx", [(i + 1, i) for i in range(ctx - step)])

    if ring:
        pass_up(1)
        pass_down(1)
    swap = [(0, 1), (1, 0)]
    steps = tokens * REFL // CHUNK
    early = steps * 5 // 8
    near, middle = local_part(queries, keys, values, beta_rows, 0, early)
    if ring:
        up[1], down[1], middle = tied(up[1], down[1], middle)
        pass_up(2)
        pass_down(2)
    near_other = send(near, "groups", swap)
    far, state_end, outgoing, total_end = local_part(
        queries, keys, values, beta_rows, early, steps - early, middle
    )
    far_other = send(far, "groups", swap)

    incoming = jnp.zeros((heads, DK, DK), BF16)
    for hop in range(ctx - 1):
        if hop == 1 and ring:
            ahead = up[2].shape[0] // 4
            last = [(i, i + 1) for i in range(2, ctx - 1)]
            up_first = send(up[2][:ahead], "ctx", last)
        if hop == 2 and ring:
            up_first, down[2], near_other, outgoing = tied(up_first, down[2], near_other, outgoing)
        incoming = incoming + send(outgoing, "ctx", [(hop, hop + 1)])
        outgoing = (
            jnp.einsum("hde,hef->hdf", total_end, incoming, preferred_element_type=F32) + state_end
        ).astype(BF16)
    if ring:
        pass_down(3)
        up_rest, incoming = tied(up[2][ahead:], incoming)
        up[3] = [up_first, send(up_rest, "ctx", last)]
        weights = [[own], [up[1]], [down[3]], [up[2]], [down[2]], up[3], [down[1]]]
        slots = lax.rem(here + ctx - jnp.arange(ctx), ctx)
        block_of = jnp.where(slots == 0, 0, 2 * slots - (here >= slots).astype(jnp.int32))
    else:
        whole = lax.all_gather(own, "ctx", axis=1, tiled=True)
        weights = [[w] for w in jnp.split(whole, head, axis=1)]
        block_of = jnp.arange(head)
    far_other, incoming = tied(far_other, incoming)
    incoming_other = send(incoming, "groups", swap)
    mine = normed_rows(near, far, incoming, gain)
    other = normed_rows(near_other, far_other, incoming_other, gain)
    mine, other = tied(mine, other)
    order = lax.axis_index("head") ^ jnp.asarray(halving_order(head), jnp.int32)
    picks = jnp.sum(
        jnp.where(order[:, None] == jnp.arange(head)[None, :], block_of[None, :], 0), axis=1
    ).astype(jnp.int32)
    give, keep = head_halved(*project(picks, other, weights))
    own_give, own_keep = head_halved(*project(picks, mine, weights))
    last_pairs = head_pairs(head // 2)
    give_a, give_b = jnp.split(give, 2)
    keep_a, keep_b = jnp.split(keep, 2)
    got_a = send(give_a, "head", last_pairs)
    give_b, own_give = tied(give_b, own_give)
    got_b = send(give_b, "head", last_pairs)
    got_a, own_give = tied(got_a, own_give)
    back_a = send(summed(keep_a, got_a), "groups", swap)
    own_got = send(own_give, "head", last_pairs)
    back_a, got_b, keep_b = tied(back_a, got_b, keep_b)
    back_b = send(summed(keep_b, got_b), "groups", swap)
    mine_sum = summed(own_keep, own_got)
    back = jnp.concatenate([back_a, back_b], axis=0)
    blocks = mine_sum.shape[1] // half_cols
    if blocks == 1:
        return jnp.where(
            side == 0,
            jnp.concatenate([mine_sum, back], axis=1),
            jnp.concatenate([back, mine_sum], axis=1),
        )
    mine_sum = mine_sum.reshape(tokens, blocks, 1, half_cols)
    back = back.reshape(tokens, blocks, 1, half_cols)
    mixed = jnp.where(
        side == 0,
        jnp.concatenate([mine_sum, back], axis=2),
        jnp.concatenate([back, mine_sum], axis=2),
    )
    return mixed.reshape(tokens, blocks * 2 * half_cols)


def solution(mesh):
    in_specs = (
        P(("groups", "ctx"), "head"),
        P(("groups", "ctx"), None, "head"),
        P(("groups", "ctx"), None, "head"),
        P(None, "head", ("groups", "ctx")),
        P("head"),
        P("head", "ctx"),
    )
    out_specs = P(("groups", "ctx"), "head")
    return jax.shard_map(
        per_device, mesh=mesh, in_specs=in_specs, out_specs=out_specs, check_vma=False
    )
```

```python
import functools

import jax
import jax.numpy as jnp
from jax import lax
from jax.experimental import pallas as pl
from jax.experimental.pallas import tpu as pltpu
from jax.sharding import PartitionSpec as P

DK = 128
REFL = 2
TINY = 1e-06
GRANT = 24 * 1024 * 1024
CHUNK = 128
BASE = 8
F32 = jnp.float32
BF16 = jnp.bfloat16


def tied(*values):
    return lax.optimization_barrier(values)


def mxu(left, right):
    return jnp.dot(left, right, preferred_element_type=F32)


def mxu_nt(left, right):
    return lax.dot_general(left, right, (((1,), (1,)), ((), ())), preferred_element_type=F32)


def split(value):
    high = value.astype(BF16)
    return high, (value - high.astype(F32)).astype(BF16)


def mxu3(left, right):
    (left_high, left_low), (right_high, right_low) = left, right
    wide = jnp.concatenate([left_high, left_high], axis=1)
    tall = jnp.concatenate([right_high, right_low], axis=0)
    return mxu(wide, tall) + mxu(left_low, right_high)


def each(function, *columns):
    return [function(*row) for row in zip(*columns)]


def unit_lower_inverse(lowers):
    size = lowers[0].shape[0]
    lane = lax.broadcasted_iota(jnp.int32, (BASE, size), 1)
    sub = lax.broadcasted_iota(jnp.int32, (BASE, size), 0)
    block_of = lane // BASE
    blocks = range(size // BASE)

    def compacted(lower):
        compact = jnp.zeros((BASE, size), F32)
        for block in blocks:
            rows = lower[block * BASE : (block + 1) * BASE, :]
            compact = jnp.where(block_of == block, rows, compact)
        return compact

    compacts = each(compacted, lowers)
    inverses = [jnp.where(lane % BASE == sub, 1.0, 0.0).astype(F32) for _ in lowers]
    for step in range(BASE - 1):
        factors = each(
            lambda compact: jnp.take_along_axis(compact, block_of * BASE + step, axis=1), compacts
        )
        inverses = each(lambda inv, factor: inv - factor * inv[step : step + 1, :], inverses, factors)
    rows_of = each(lambda inv: [jnp.where(block_of == block, inv, 0.0) for block in blocks], inverses)
    width = BASE
    while width < size:
        pairs = range(size // (2 * width))
        per = width // BASE
        lane_w = lax.broadcasted_iota(jnp.int32, (width, size), 1) // width
        empty = jnp.zeros((width, size), F32)

        def picked(lower):
            return jnp.concatenate(
                [
                    jnp.where(
                        lane_w == 2 * p, lower[(2 * p + 1) * width : (2 * p + 2) * width, :], 0.0
                    )
                    for p in pairs
                ],
                axis=0,
            )

        def spread(inner):
            return jnp.concatenate(
                [x for p in pairs for x in (empty, inner[p * width : (p + 1) * width, :])], axis=0
            )

        halves = each(lambda rows: split(jnp.concatenate(rows, axis=0)), rows_of)
        picks = each(lambda lower: split(picked(lower)), lowers)
        inners = each(mxu3, picks, halves)
        belows = each(
            lambda rows: jnp.concatenate(
                [rows[(2 * p + 1) * per + i] for p in pairs for i in range(per)], axis=0
            ),
            rows_of,
        )
        joins = each(
            lambda below, inner: below - mxu3(split(below), split(spread(inner))), belows, inners
        )

        def placed(rows, joined):
            rows = list(rows)
            for p in pairs:
                for i in range(per):
                    at = (p * per + i) * BASE
                    rows[(2 * p + 1) * per + i] = joined[at : at + BASE, :]
            return rows

        rows_of = each(placed, rows_of, joins)
        width *= 2
    return each(lambda rows: split(jnp.concatenate(rows, axis=0)), rows_of)


def chunk_kernel(group, first, q_ref, k_ref, v_ref, b_ref, *refs):
    if first:
        oe_ref, end_ref, state = refs
    else:
        start_ref, oe_ref, s_ref, sent_ref, p_ref, state = refs
    chunk = pl.program_id(0)
    tokens = CHUNK // REFL

    @pl.when(chunk == 0)
    def _():
        lane = lax.broadcasted_iota(jnp.int32, (DK, 2 * DK), 1)
        sub = lax.broadcasted_iota(jnp.int32, (DK, 2 * DK), 0)
        start = jnp.where(lane == sub + DK, 1.0, 0.0).astype(F32)
        for head in range(group):
            state[head] = start if first else start_ref[head]

    below = lax.broadcasted_iota(jnp.int32, (CHUNK, CHUNK), 0) > lax.broadcasted_iota(
        jnp.int32, (CHUNK, CHUNK), 1
    )
    reach = REFL * lax.broadcasted_iota(jnp.int32, (tokens, CHUNK), 0) + (
        REFL - 1
    ) >= lax.broadcasted_iota(jnp.int32, (tokens, CHUNK), 1)
    heads = range(group)
    cols = [slice(head * DK, (head + 1) * DK) for head in heads]
    ks = [k_ref[:, :, c].reshape(CHUNK, DK) for c in cols]
    qs = [q_ref[:, c] for c in cols]

    def inverse_norm(rows):
        rows = rows.astype(F32)
        return lax.rsqrt(jnp.sum(rows * rows, axis=-1, keepdims=True) + TINY)

    k_scales = each(inverse_norm, ks)
    q_scales = each(inverse_norm, qs)
    rates = [b_ref[:, head : head + 1] * k_scales[head] for head in heads]
    rates2 = each(lambda rate, scale: rate * scale, rates, k_scales)
    kqs = each(lambda k, q: jnp.concatenate([k, q], axis=0), ks, qs)
    grams = each(mxu_nt, kqs, ks)
    lowers = each(lambda rate, gram: jnp.where(below, rate * gram[:CHUNK], 0.0), rates2, grams)
    scores = each(lambda gram: jnp.where(reach, gram[CHUNK:], 0.0).astype(BF16), grams)
    inverses = unit_lower_inverse(lowers)
    nows = [state[head] for head in heads]
    seens = each(
        lambda kq, now: mxu(
            jnp.concatenate([kq, kq], axis=1), jnp.concatenate(split(now), axis=0)
        ),
        kqs,
        nows,
    )

    def right_side(head):
        scaled = rates2[head] * seens[head][:CHUNK]
        own = rates[head] * v_ref[:, :, cols[head]].reshape(CHUNK, DK).astype(F32)
        return split(jnp.concatenate([own - scaled[:, :DK], -scaled[:, DK:]], axis=1))

    rights = each(right_side, heads)
    deltas = each(lambda inverse, right: split(mxu3(inverse, right)), inverses, rights)

    def stepped(k, now, delta):
        k_t = k.astype(F32).T.astype(BF16)
        return now + mxu(jnp.concatenate([k_t, k_t], axis=1), jnp.concatenate(delta, axis=0))

    nexts = each(stepped, ks, nows, deltas)
    outs = each(
        lambda scale, seen, score, delta: scale * (seen[CHUNK:] + mxu(score, delta[0])),
        q_scales,
        seens,
        scores,
        deltas,
    )
    for head in heads:
        state[head] = nexts[head]
        oe_ref[:, cols[head]] = outs[head][:, :DK].astype(BF16)
        oe_ref[:, slice((group + head) * DK, (group + head + 1) * DK)] = outs[head][:, DK:].astype(
            BF16
        )

    @pl.when(chunk == pl.num_programs(0) - 1)
    def _():
        for head in heads:
            if first:
                end_ref[head] = nexts[head]
            else:
                s_ref[head] = nexts[head][:, :DK]
                sent_ref[head] = nexts[head][:, :DK].astype(BF16)
                p_ref[head] = nexts[head][:, DK:].astype(BF16)


def local_part(queries, keys, values, beta, skip, steps, start=None):
    tokens, width = queries.shape
    group = width // DK
    tile = CHUNK // REFL
    first = start is None
    refl = pl.BlockSpec((tile, REFL, width), lambda c: (c + skip, 0, 0))
    whole = pl.BlockSpec((group, DK, 2 * DK), lambda c: (0, 0, 0))
    square = pl.BlockSpec((group, DK, DK), lambda c: (0, 0, 0))
    rows = jax.ShapeDtypeStruct((steps * tile, 2 * width), BF16)
    return pl.pallas_call(
        functools.partial(chunk_kernel, group, first),
        grid=(steps,),
        in_specs=[
            pl.BlockSpec((tile, width), lambda c: (c + skip, 0)),
            refl,
            refl,
            pl.BlockSpec((CHUNK, group), lambda c: (c + skip, 0)),
        ]
        + ([] if first else [whole]),
        out_specs=[pl.BlockSpec((tile, 2 * width), lambda c: (c, 0))]
        + ([whole] if first else [square] * 3),
        out_shape=[rows]
        + (
            [jax.ShapeDtypeStruct((group, DK, 2 * DK), F32)]
            if first
            else [
                jax.ShapeDtypeStruct((group, DK, DK), F32),
                jax.ShapeDtypeStruct((group, DK, DK), BF16),
                jax.ShapeDtypeStruct((group, DK, DK), BF16),
            ]
        ),
        scratch_shapes=[pltpu.VMEM((group, DK, 2 * DK), F32)],
        compiler_params=pltpu.CompilerParams(vmem_limit_bytes=56 * 1024 * 1024),
        cost_estimate=pl.CostEstimate(
            flops=400 * steps * tile * width * DK, bytes_accessed=16 * steps * tile * width, transcendentals=0
        ),
        name="local_part",
    )(queries, keys, values, beta, *([] if first else [start]))


def norm_kernel(first_ref, second_ref, s_ref, g_ref, out_ref):
    group = s_ref.shape[0]
    heads = range(group)
    cols = [slice(head * DK, (head + 1) * DK) for head in heads]
    for half, oe_ref in enumerate((first_ref, second_ref)):
        tile = oe_ref.shape[0] // 2
        for at in range(0, oe_ref.shape[0], tile):
            rows = slice(at, at + tile)
            to = slice(half * first_ref.shape[0] + at, half * first_ref.shape[0] + at + tile)
            seen = [
                mxu(oe_ref[rows, (group + head) * DK : (group + head + 1) * DK], s_ref[head])
                for head in heads
            ]
            readouts = [oe_ref[rows, cols[head]].astype(F32) + seen[head] for head in heads]
            scales = each(
                lambda x: lax.rsqrt(jnp.mean(x * x, axis=-1, keepdims=True) + TINY), readouts
            )
            for head in heads:
                out_ref[to, cols[head]] = (
                    readouts[head] * scales[head] * g_ref[:, cols[head]]
                ).astype(BF16)


def normed_rows(first, second, incoming, gain):
    width = gain.shape[0]
    tokens = first.shape[0] + second.shape[0]
    return pl.pallas_call(
        norm_kernel,
        in_specs=[pl.BlockSpec(memory_space=pltpu.VMEM)] * 4,
        out_specs=pl.BlockSpec(memory_space=pltpu.VMEM),
        out_shape=jax.ShapeDtypeStruct((tokens, width), BF16),
        compiler_params=pltpu.CompilerParams(vmem_limit_bytes=GRANT),
        name="normed_rows",
    )(first, second, incoming, gain.reshape(1, width))


def project_kernel(options, place_ref, first_ref, a_ref, *refs):
    weights, out_ref = list(refs[:-1]), refs[-1]

    def put(slot, pieces):
        at, product = 0, None
        for piece in pieces:
            part = mxu(a_ref[:, at : at + piece.shape[0]], piece[...])
            product = part if product is None else product + part
            at += piece.shape[0]
        out_ref[place_ref[slot]] = product.astype(BF16)

    for slot, counts in enumerate(options):
        for option, pieces in enumerate(counts):
            taken, weights = weights[:pieces], weights[pieces:]
            if len(counts) == 1:
                put(slot, taken)
            else:
                pl.when(first_ref[slot] == 1 - option)(functools.partial(put, slot, taken))


def project(places, first, rows, weights):
    tokens = rows.shape[0]
    block = weights[0][0][0].shape[1]
    count = len(weights)
    flat = [piece for options in weights for pieces in options for piece in pieces]
    return pl.pallas_call(
        functools.partial(
            project_kernel, tuple(tuple(len(pieces) for pieces in options) for options in weights)
        ),
        in_specs=[pl.BlockSpec(memory_space=pltpu.SMEM)] * 2
        + [pl.BlockSpec(memory_space=pltpu.VMEM)] * (1 + len(flat)),
        out_specs=pl.BlockSpec(memory_space=pltpu.VMEM),
        out_shape=jax.ShapeDtypeStruct((count, tokens, block), BF16),
        compiler_params=pltpu.CompilerParams(vmem_limit_bytes=GRANT),
        name="project",
    )(places, first, rows, *flat)


def halving_order(count):
    order = [0]
    bit = count // 2
    while bit >= 1:
        order = [m | bit for m in order] + order
        bit //= 2
    return order


def head_pairs(bit):
    return [(i, i ^ bit) for i in range(lax.axis_size("head"))]


def head_halved(parts):
    bit, give, keep = 1, parts[: parts.shape[0] // 2], parts[parts.shape[0] // 2 :]
    while bit * 2 < lax.axis_size("head"):
        got = lax.ppermute(give, "head", head_pairs(bit))
        half = keep.shape[0] // 2
        give = summed(keep[:half], got[:half])
        keep = keep[half:].astype(F32) + got[half:].astype(F32)
        bit *= 2
    return give[0], keep[0]


def summed(keep, got):
    return (keep.astype(F32) + got.astype(F32)).astype(BF16)


def send(value, axis, pairs):
    return lax.ppermute(value, axis, pairs)


def per_device(queries, keys, values, beta, gain, w_out):
    tokens, width = queries.shape
    heads = width // DK
    ctx, head = lax.axis_size("ctx"), lax.axis_size("head")
    here, side = lax.axis_index("ctx"), lax.axis_index("groups")
    beta_rows = beta.transpose(2, 0, 1).reshape(tokens * REFL, heads)
    half_cols = w_out.shape[1] // 2
    own = lax.dynamic_slice_in_dim(w_out, side * half_cols, half_cols, 1)
    ring = ctx == head and ctx == 4
    up, down = {0: own}, {0: own}

    def pass_up(step):
        up[step] = send(up[step - 1], "ctx", [(i, i + 1) for i in range(step - 1, ctx - 1)])

    def pass_down(step):
        down[step] = send(down[step - 1], "ctx", [(i + 1, i) for i in range(ctx - step)])

    if ring:
        pass_up(1)
        pass_down(1)
    swap = [(0, 1), (1, 0)]
    steps = tokens * REFL // CHUNK
    early = steps * 5 // 8
    near, middle = local_part(queries, keys, values, beta_rows, 0, early)
    if ring:
        up[1], down[1], middle = tied(up[1], down[1], middle)
        pass_up(2)
        pass_down(2)
    near_other = send(near, "groups", swap)
    far, state_end, outgoing, total_end = local_part(
        queries, keys, values, beta_rows, early, steps - early, middle
    )
    far_other = send(far, "groups", swap)

    incoming = jnp.zeros((heads, DK, DK), BF16)
    for hop in range(ctx - 1):
        if hop == 1 and ring:
            ahead = up[2].shape[0] // 4
            last = [(i, i + 1) for i in range(2, ctx - 1)]
            up_first = send(up[2][:ahead], "ctx", last)
        if hop == 2 and ring:
            up_first, down[2], near_other, outgoing = tied(up_first, down[2], near_other, outgoing)
        incoming = incoming + send(outgoing, "ctx", [(hop, hop + 1)])
        outgoing = (
            jnp.einsum("hde,hef->hdf", total_end, incoming, preferred_element_type=F32) + state_end
        ).astype(BF16)
    if ring:
        pass_down(3)
        up_rest, incoming = tied(up[2][ahead:], incoming)
        up[3] = [up_first, send(up_rest, "ctx", last)]
        weights = [([own],), ([up[1]], [down[3]]), ([up[2]], [down[2]]), (up[3], [down[1]])]
        targets = lax.rem(here + ctx - jnp.arange(ctx), ctx)
        first = (here >= jnp.arange(ctx)).astype(jnp.int32)
    else:
        whole = lax.all_gather(own, "ctx", axis=1, tiled=True)
        weights = [([w],) for w in jnp.split(whole, head, axis=1)]
        targets = jnp.arange(head)
        first = jnp.ones((head,), jnp.int32)
    far_other, incoming = tied(far_other, incoming)
    incoming_other = send(incoming, "groups", swap)
    mine = normed_rows(near, far, incoming, gain)
    other = normed_rows(near_other, far_other, incoming_other, gain)
    distance = targets ^ lax.axis_index("head")
    order = jnp.asarray(halving_order(head), jnp.int32)
    places = jnp.argmax(distance[:, None] == order[None, :], axis=1).astype(jnp.int32)
    mine, other = tied(mine, other)
    give, keep = head_halved(project(places, first, other, weights))
    own_give, own_keep = head_halved(project(places, first, mine, weights))
    last_pairs = head_pairs(head // 2)
    give_a, give_b = jnp.split(give, 2)
    keep_a, keep_b = jnp.split(keep, 2)
    got_a = send(give_a, "head", last_pairs)
    give_b, own_give = tied(give_b, own_give)
    got_b = send(give_b, "head", last_pairs)
    got_a, own_give = tied(got_a, own_give)
    back_a = send(summed(keep_a, got_a), "groups", swap)
    own_got = send(own_give, "head", last_pairs)
    back_a, got_b, keep_b = tied(back_a, got_b, keep_b)
    back_b = send(summed(keep_b, got_b), "groups", swap)
    mine_sum = summed(own_keep, own_got)
    back = jnp.concatenate([back_a, back_b], axis=0)
    blocks = mine_sum.shape[1] // half_cols
    if blocks == 1:
        return jnp.where(
            side == 0,
            jnp.concatenate([mine_sum, back], axis=1),
            jnp.concatenate([back, mine_sum], axis=1),
        )
    mine_sum = mine_sum.reshape(tokens, blocks, 1, half_cols)
    back = back.reshape(tokens, blocks, 1, half_cols)
    mixed = jnp.where(
        side == 0,
        jnp.concatenate([mine_sum, back], axis=2),
        jnp.concatenate([back, mine_sum], axis=2),
    )
    return mixed.reshape(tokens, blocks * 2 * half_cols)


def solution(mesh):
    in_specs = (
        P(("groups", "ctx"), "head"),
        P(("groups", "ctx"), None, "head"),
        P(("groups", "ctx"), None, "head"),
        P(None, "head", ("groups", "ctx")),
        P("head"),
        P("head", "ctx"),
    )
    out_specs = P(("groups", "ctx"), "head")
    return jax.shard_map(
        per_device, mesh=mesh, in_specs=in_specs, out_specs=out_specs, check_vma=False
    )
```

```python
import functools

import jax
import jax.numpy as jnp
from jax import lax
from jax.experimental import pallas as pl
from jax.experimental.pallas import tpu as pltpu
from jax.sharding import PartitionSpec as P

DK = 128
REFL = 2
TINY = 1e-06
GRANT = 24 * 1024 * 1024
CHUNK = 128
BASE = 8
F32 = jnp.float32
BF16 = jnp.bfloat16


def tied(*values):
    return lax.optimization_barrier(values)


def mxu(left, right):
    return jnp.dot(left, right, preferred_element_type=F32)


def mxu_nt(left, right):
    return lax.dot_general(left, right, (((1,), (1,)), ((), ())), preferred_element_type=F32)


def split(value):
    high = value.astype(BF16)
    return high, (value - high.astype(F32)).astype(BF16)


def mxu3(left, right):
    (left_high, left_low), (right_high, right_low) = left, right
    wide = jnp.concatenate([left_high, left_high], axis=1)
    tall = jnp.concatenate([right_high, right_low], axis=0)
    return mxu(wide, tall) + mxu(left_low, right_high)


def each(function, *columns):
    return [function(*row) for row in zip(*columns)]


def unit_lower_inverse(lowers):
    size = lowers[0].shape[0]
    lane = lax.broadcasted_iota(jnp.int32, (BASE, size), 1)
    sub = lax.broadcasted_iota(jnp.int32, (BASE, size), 0)
    block_of = lane // BASE
    blocks = range(size // BASE)

    def compacted(lower):
        compact = jnp.zeros((BASE, size), F32)
        for block in blocks:
            rows = lower[block * BASE : (block + 1) * BASE, :]
            compact = jnp.where(block_of == block, rows, compact)
        return compact

    compacts = each(compacted, lowers)
    inverses = [jnp.where(lane % BASE == sub, 1.0, 0.0).astype(F32) for _ in lowers]
    for step in range(BASE - 1):
        factors = each(
            lambda compact: jnp.take_along_axis(compact, block_of * BASE + step, axis=1), compacts
        )
        inverses = each(lambda inv, factor: inv - factor * inv[step : step + 1, :], inverses, factors)
    rows_of = each(lambda inv: [jnp.where(block_of == block, inv, 0.0) for block in blocks], inverses)
    width = BASE
    while width < size:
        pairs = range(size // (2 * width))
        per = width // BASE
        lane_w = lax.broadcasted_iota(jnp.int32, (width, size), 1) // width
        empty = jnp.zeros((width, size), F32)

        def picked(lower):
            return jnp.concatenate(
                [
                    jnp.where(
                        lane_w == 2 * p, lower[(2 * p + 1) * width : (2 * p + 2) * width, :], 0.0
                    )
                    for p in pairs
                ],
                axis=0,
            )

        def spread(inner):
            return jnp.concatenate(
                [x for p in pairs for x in (empty, inner[p * width : (p + 1) * width, :])], axis=0
            )

        halves = each(lambda rows: split(jnp.concatenate(rows, axis=0)), rows_of)
        picks = each(lambda lower: split(picked(lower)), lowers)
        inners = each(mxu3, picks, halves)
        belows = each(
            lambda rows: jnp.concatenate(
                [rows[(2 * p + 1) * per + i] for p in pairs for i in range(per)], axis=0
            ),
            rows_of,
        )
        joins = each(
            lambda below, inner: below - mxu3(split(below), split(spread(inner))), belows, inners
        )

        def placed(rows, joined):
            rows = list(rows)
            for p in pairs:
                for i in range(per):
                    at = (p * per + i) * BASE
                    rows[(2 * p + 1) * per + i] = joined[at : at + BASE, :]
            return rows

        rows_of = each(placed, rows_of, joins)
        width *= 2
    return each(lambda rows: split(jnp.concatenate(rows, axis=0)), rows_of)


def chunk_kernel(group, first, q_ref, k_ref, v_ref, b_ref, *refs):
    if first:
        oe_ref, end_ref, state = refs
    else:
        start_ref, oe_ref, s_ref, sent_ref, p_ref, state = refs
    chunk = pl.program_id(0)
    tokens = CHUNK // REFL

    @pl.when(chunk == 0)
    def _():
        lane = lax.broadcasted_iota(jnp.int32, (DK, 2 * DK), 1)
        sub = lax.broadcasted_iota(jnp.int32, (DK, 2 * DK), 0)
        start = jnp.where(lane == sub + DK, 1.0, 0.0).astype(F32)
        for head in range(group):
            state[head] = start if first else start_ref[head]

    below = lax.broadcasted_iota(jnp.int32, (CHUNK, CHUNK), 0) > lax.broadcasted_iota(
        jnp.int32, (CHUNK, CHUNK), 1
    )
    reach = REFL * lax.broadcasted_iota(jnp.int32, (tokens, CHUNK), 0) + (
        REFL - 1
    ) >= lax.broadcasted_iota(jnp.int32, (tokens, CHUNK), 1)
    heads = range(group)
    cols = [slice(head * DK, (head + 1) * DK) for head in heads]
    ks = [k_ref[:, :, c].reshape(CHUNK, DK) for c in cols]
    qs = [q_ref[:, c] for c in cols]

    def inverse_norm(rows):
        rows = rows.astype(F32)
        return lax.rsqrt(jnp.sum(rows * rows, axis=-1, keepdims=True) + TINY)

    k_scales = each(inverse_norm, ks)
    q_scales = each(inverse_norm, qs)
    rates = [b_ref[:, head : head + 1] * k_scales[head] for head in heads]
    rates2 = each(lambda rate, scale: rate * scale, rates, k_scales)
    kqs = each(lambda k, q: jnp.concatenate([k, q], axis=0), ks, qs)
    grams = each(mxu_nt, kqs, ks)
    lowers = each(lambda rate, gram: jnp.where(below, rate * gram[:CHUNK], 0.0), rates2, grams)
    scores = each(lambda gram: jnp.where(reach, gram[CHUNK:], 0.0).astype(BF16), grams)
    inverses = unit_lower_inverse(lowers)
    nows = [state[head] for head in heads]
    seens = each(
        lambda kq, now: mxu(
            jnp.concatenate([kq, kq], axis=1), jnp.concatenate(split(now), axis=0)
        ),
        kqs,
        nows,
    )

    def right_side(head):
        scaled = rates2[head] * seens[head][:CHUNK]
        own = rates[head] * v_ref[:, :, cols[head]].reshape(CHUNK, DK).astype(F32)
        return split(jnp.concatenate([own - scaled[:, :DK], -scaled[:, DK:]], axis=1))

    rights = each(right_side, heads)
    deltas = each(lambda inverse, right: split(mxu3(inverse, right)), inverses, rights)

    def stepped(k, now, delta):
        k_t = k.astype(F32).T.astype(BF16)
        return now + mxu(jnp.concatenate([k_t, k_t], axis=1), jnp.concatenate(delta, axis=0))

    nexts = each(stepped, ks, nows, deltas)
    outs = each(
        lambda scale, seen, score, delta: scale * (seen[CHUNK:] + mxu(score, delta[0])),
        q_scales,
        seens,
        scores,
        deltas,
    )
    for head in heads:
        state[head] = nexts[head]
        oe_ref[:, cols[head]] = outs[head][:, :DK].astype(BF16)
        oe_ref[:, slice((group + head) * DK, (group + head + 1) * DK)] = outs[head][:, DK:].astype(
            BF16
        )

    @pl.when(chunk == pl.num_programs(0) - 1)
    def _():
        for head in heads:
            if first:
                end_ref[head] = nexts[head]
            else:
                s_ref[head] = nexts[head][:, :DK]
                sent_ref[head] = nexts[head][:, :DK].astype(BF16)
                p_ref[head] = nexts[head][:, DK:].astype(BF16)


def local_part(queries, keys, values, beta, skip, steps, start=None):
    tokens, width = queries.shape
    group = width // DK
    tile = CHUNK // REFL
    first = start is None
    refl = pl.BlockSpec((tile, REFL, width), lambda c: (c + skip, 0, 0))
    whole = pl.BlockSpec((group, DK, 2 * DK), lambda c: (0, 0, 0))
    square = pl.BlockSpec((group, DK, DK), lambda c: (0, 0, 0))
    rows = jax.ShapeDtypeStruct((steps * tile, 2 * width), BF16)
    return pl.pallas_call(
        functools.partial(chunk_kernel, group, first),
        grid=(steps,),
        in_specs=[
            pl.BlockSpec((tile, width), lambda c: (c + skip, 0)),
            refl,
            refl,
            pl.BlockSpec((CHUNK, group), lambda c: (c + skip, 0)),
        ]
        + ([] if first else [whole]),
        out_specs=[pl.BlockSpec((tile, 2 * width), lambda c: (c, 0))]
        + ([whole] if first else [square] * 3),
        out_shape=[rows]
        + (
            [jax.ShapeDtypeStruct((group, DK, 2 * DK), F32)]
            if first
            else [
                jax.ShapeDtypeStruct((group, DK, DK), F32),
                jax.ShapeDtypeStruct((group, DK, DK), BF16),
                jax.ShapeDtypeStruct((group, DK, DK), BF16),
            ]
        ),
        scratch_shapes=[pltpu.VMEM((group, DK, 2 * DK), F32)],
        compiler_params=pltpu.CompilerParams(vmem_limit_bytes=56 * 1024 * 1024),
        cost_estimate=pl.CostEstimate(
            flops=400 * steps * tile * width * DK, bytes_accessed=16 * steps * tile * width, transcendentals=0
        ),
        name="local_part",
    )(queries, keys, values, beta, *([] if first else [start]))


def norm_kernel(first_ref, second_ref, s_ref, g_ref, out_ref):
    group = s_ref.shape[0]
    heads = range(group)
    cols = [slice(head * DK, (head + 1) * DK) for head in heads]
    for half, oe_ref in enumerate((first_ref, second_ref)):
        tile = oe_ref.shape[0] // 2
        for at in range(0, oe_ref.shape[0], tile):
            rows = slice(at, at + tile)
            to = slice(half * first_ref.shape[0] + at, half * first_ref.shape[0] + at + tile)
            seen = [
                mxu(oe_ref[rows, (group + head) * DK : (group + head + 1) * DK], s_ref[head])
                for head in heads
            ]
            readouts = [oe_ref[rows, cols[head]].astype(F32) + seen[head] for head in heads]
            scales = each(
                lambda x: lax.rsqrt(jnp.mean(x * x, axis=-1, keepdims=True) + TINY), readouts
            )
            for head in heads:
                out_ref[to, cols[head]] = (
                    readouts[head] * scales[head] * g_ref[:, cols[head]]
                ).astype(BF16)


def normed_rows(first, second, incoming, gain):
    width = gain.shape[0]
    tokens = first.shape[0] + second.shape[0]
    return pl.pallas_call(
        norm_kernel,
        in_specs=[pl.BlockSpec(memory_space=pltpu.VMEM)] * 4,
        out_specs=pl.BlockSpec(memory_space=pltpu.VMEM),
        out_shape=jax.ShapeDtypeStruct((tokens, width), BF16),
        compiler_params=pltpu.CompilerParams(vmem_limit_bytes=GRANT),
        name="normed_rows",
    )(first, second, incoming, gain.reshape(1, width))


def project_kernel(options, rows_count, place_ref, first_ref, *refs):
    rows, refs = refs[:rows_count], refs[rows_count:]
    *weights, held, sems = refs[: -2 - rows_count] + refs[-2:]
    outs = refs[-2 - rows_count : -2]
    whole = weights[0]

    def fetch(slot, pieces):
        at = 0
        for piece in pieces:
            to = held.at[slot, pl.ds(at, piece.shape[0])]
            pltpu.make_async_copy(piece, to, sems.at[slot]).start()
            at += piece.shape[0]

    for slot, counts in enumerate(options):
        for option, pieces in enumerate(counts):
            taken, weights = weights[:pieces], weights[pieces:]
            if len(counts) == 1:
                fetch(slot, taken)
            else:
                pl.when(first_ref[slot] == 1 - option)(functools.partial(fetch, slot, taken))
    for slot in range(len(options)):
        pltpu.make_async_copy(whole, held.at[slot], sems.at[slot]).wait()
        for row, out in zip(rows, outs):
            out[place_ref[slot]] = mxu(row[...], held[slot]).astype(BF16)


def project(places, first, rows, weights):
    tokens, depth = rows[0].shape
    block = weights[0][0][0].shape[1]
    count = len(weights)
    flat = [piece for options in weights for pieces in options for piece in pieces]
    vmem = pl.BlockSpec(memory_space=pltpu.VMEM)
    return pl.pallas_call(
        functools.partial(
            project_kernel,
            tuple(tuple(len(pieces) for pieces in options) for options in weights),
            len(rows),
        ),
        in_specs=[pl.BlockSpec(memory_space=pltpu.SMEM)] * 2
        + [vmem] * len(rows)
        + [pl.BlockSpec(memory_space=pl.ANY)] * len(flat),
        out_specs=[vmem] * len(rows),
        out_shape=[jax.ShapeDtypeStruct((count, tokens, block), BF16)] * len(rows),
        scratch_shapes=[
            pltpu.VMEM((count, depth, block), BF16),
            pltpu.SemaphoreType.DMA((count,)),
        ],
        compiler_params=pltpu.CompilerParams(vmem_limit_bytes=2 * GRANT),
        name="project",
    )(places, first, *rows, *flat)


def halving_order(count):
    order = [0]
    bit = count // 2
    while bit >= 1:
        order = [m | bit for m in order] + order
        bit //= 2
    return order


def head_pairs(bit):
    return [(i, i ^ bit) for i in range(lax.axis_size("head"))]


def head_halved(parts):
    bit, give, keep = 1, parts[: parts.shape[0] // 2], parts[parts.shape[0] // 2 :]
    while bit * 2 < lax.axis_size("head"):
        got = lax.ppermute(give, "head", head_pairs(bit))
        half = keep.shape[0] // 2
        give = summed(keep[:half], got[:half])
        keep = keep[half:].astype(F32) + got[half:].astype(F32)
        bit *= 2
    return give[0], keep[0]


def summed(keep, got):
    return (keep.astype(F32) + got.astype(F32)).astype(BF16)


def send(value, axis, pairs):
    return lax.ppermute(value, axis, pairs)


def per_device(queries, keys, values, beta, gain, w_out):
    tokens, width = queries.shape
    heads = width // DK
    ctx, head = lax.axis_size("ctx"), lax.axis_size("head")
    here, side = lax.axis_index("ctx"), lax.axis_index("groups")
    beta_rows = beta.transpose(2, 0, 1).reshape(tokens * REFL, heads)
    half_cols = w_out.shape[1] // 2
    own = lax.dynamic_slice_in_dim(w_out, side * half_cols, half_cols, 1)
    ring = ctx == head and ctx == 4
    up, down = {0: own}, {0: own}

    def pass_up(step):
        up[step] = send(up[step - 1], "ctx", [(i, i + 1) for i in range(step - 1, ctx - 1)])

    def pass_down(step):
        down[step] = send(down[step - 1], "ctx", [(i + 1, i) for i in range(ctx - step)])

    if ring:
        pass_up(1)
        pass_down(1)
    swap = [(0, 1), (1, 0)]
    steps = tokens * REFL // CHUNK
    early = steps * 5 // 8
    near, middle = local_part(queries, keys, values, beta_rows, 0, early)
    if ring:
        up[1], down[1], middle = tied(up[1], down[1], middle)
        pass_up(2)
        pass_down(2)
    near_other = send(near, "groups", swap)
    far, state_end, outgoing, total_end = local_part(
        queries, keys, values, beta_rows, early, steps - early, middle
    )
    far_other = send(far, "groups", swap)

    incoming = jnp.zeros((heads, DK, DK), BF16)
    for hop in range(ctx - 1):
        if hop == 1 and ring:
            ahead = up[2].shape[0] // 4
            last = [(i, i + 1) for i in range(2, ctx - 1)]
            up_first = send(up[2][:ahead], "ctx", last)
        if hop == 2 and ring:
            up_first, down[2], near_other, outgoing = tied(up_first, down[2], near_other, outgoing)
        incoming = incoming + send(outgoing, "ctx", [(hop, hop + 1)])
        outgoing = (
            jnp.einsum("hde,hef->hdf", total_end, incoming, preferred_element_type=F32) + state_end
        ).astype(BF16)
    if ring:
        pass_down(3)
        up_rest, incoming = tied(up[2][ahead:], incoming)
        up[3] = [up_first, send(up_rest, "ctx", last)]
        weights = [([up[1]], [down[3]]), ([down[1]], up[3]), ([own],), ([up[2]], [down[2]])]
        slots = jnp.asarray([1, 3, 0, 2], jnp.int32)
        targets = lax.rem(here + ctx - slots, ctx)
        first = jnp.where(slots == 3, here < 3, here >= slots).astype(jnp.int32)
    else:
        whole = lax.all_gather(own, "ctx", axis=1, tiled=True)
        weights = [([w],) for w in jnp.split(whole, head, axis=1)]
        targets = jnp.arange(head)
        first = jnp.ones((head,), jnp.int32)
    far_other, incoming = tied(far_other, incoming)
    incoming_other = send(incoming, "groups", swap)
    mine = normed_rows(near, far, incoming, gain)
    other = normed_rows(near_other, far_other, incoming_other, gain)
    distance = targets ^ lax.axis_index("head")
    if ring:
        places = jnp.where((distance & 2) == 2, 0, 1).astype(jnp.int32)
        even = (here + lax.axis_index("head")) % 2 == 0
        cells = [(z, h) for z in range(ctx) for h in range(head)]

        def cell_pairs(parity, bit):
            return [
                (z * head + h, z * head + (h ^ bit)) for z, h in cells if (z + h) % 2 == parity
            ]

        def crossing(parts, parity):
            got = lax.ppermute(parts, ("ctx", "head"), cell_pairs(1 - parity, 1))
            return summed(parts[0], got[0]), parts[1].astype(F32) + got[1].astype(F32)

        def over_x(value, parity):
            return lax.ppermute(value, ("ctx", "head"), cell_pairs(parity, 2))

        def back_over_y(value, parity):
            pairs = [
                ((g * ctx + z) * head + h, ((1 - g) * ctx + z) * head + h)
                for g in range(2)
                for z, h in cells
                if (z + h) % 2 == parity
            ]
            return lax.ppermute(value, ("groups", "ctx", "head"), pairs)

        other_parts, parts = project(places[2:], first[2:], [other, mine], weights[2:])
        give, keep = crossing(other_parts, 0)
        own_give, own_keep = crossing(parts, 0)
        got, own_got = over_x(give, 0), over_x(own_give, 0)
        other_parts, parts = project(places[:2], first[:2], [other, mine], weights[:2])
        back = back_over_y(summed(keep, got), 0)
        even_sum = summed(own_keep, own_got)
        give, keep = crossing(other_parts, 1)
        own_give, own_keep = crossing(parts, 1)
        got = over_x(give, 1)
        own_got = over_x(own_give, 1)
        back_odd = back_over_y(summed(keep, got), 1)
        mine_sum = jnp.where(even, even_sum, summed(own_keep, own_got))
        back = jnp.where(even, back, back_odd)
    else:
        order = jnp.asarray(halving_order(head), jnp.int32)
        places = jnp.argmax(distance[:, None] == order[None, :], axis=1).astype(jnp.int32)
        last_pairs = head_pairs(head // 2)
        sums = []
        for parts in project(places, first, [other, mine], weights):
            give, keep = head_halved(parts)
            sums.append(summed(keep, lax.ppermute(give, "head", last_pairs)))
        back, mine_sum = send(sums[0], "groups", swap), sums[1]
    blocks = mine_sum.shape[1] // half_cols
    if blocks == 1:
        return jnp.where(
            side == 0,
            jnp.concatenate([mine_sum, back], axis=1),
            jnp.concatenate([back, mine_sum], axis=1),
        )
    mine_sum = mine_sum.reshape(tokens, blocks, 1, half_cols)
    back = back.reshape(tokens, blocks, 1, half_cols)
    mixed = jnp.where(
        side == 0,
        jnp.concatenate([mine_sum, back], axis=2),
        jnp.concatenate([back, mine_sum], axis=2),
    )
    return mixed.reshape(tokens, blocks * 2 * half_cols)


def solution(mesh):
    in_specs = (
        P(("groups", "ctx"), "head"),
        P(("groups", "ctx"), None, "head"),
        P(("groups", "ctx"), None, "head"),
        P(None, "head", ("groups", "ctx")),
        P("head"),
        P("head", "ctx"),
    )
    out_specs = P(("groups", "ctx"), "head")
    return jax.shard_map(
        per_device, mesh=mesh, in_specs=in_specs, out_specs=out_specs, check_vma=False
    )
```

```python
import functools

import jax
import jax.numpy as jnp
from jax import lax
from jax.experimental import pallas as pl
from jax.experimental.pallas import tpu as pltpu
from jax.sharding import PartitionSpec as P

DK = 128
REFL = 2
TINY = 1e-06
GRANT = 24 * 1024 * 1024
CHUNK = 128
BASE = 8
F32 = jnp.float32
BF16 = jnp.bfloat16


def tied(*values):
    return lax.optimization_barrier(values)


def mxu(left, right):
    return jnp.dot(left, right, preferred_element_type=F32)


def mxu_nt(left, right):
    return lax.dot_general(left, right, (((1,), (1,)), ((), ())), preferred_element_type=F32)


def split(value):
    high = value.astype(BF16)
    return high, (value - high.astype(F32)).astype(BF16)


def mxu3(left, right):
    (left_high, left_low), (right_high, right_low) = left, right
    wide = jnp.concatenate([left_high, left_high], axis=1)
    tall = jnp.concatenate([right_high, right_low], axis=0)
    return mxu(wide, tall) + mxu(left_low, right_high)


def each(function, *columns):
    return [function(*row) for row in zip(*columns)]


def unit_lower_inverse(lowers):
    size = lowers[0].shape[0]
    lane = lax.broadcasted_iota(jnp.int32, (BASE, size), 1)
    sub = lax.broadcasted_iota(jnp.int32, (BASE, size), 0)
    block_of = lane // BASE
    blocks = range(size // BASE)

    def compacted(lower):
        compact = jnp.zeros((BASE, size), F32)
        for block in blocks:
            rows = lower[block * BASE : (block + 1) * BASE, :]
            compact = jnp.where(block_of == block, rows, compact)
        return compact

    compacts = each(compacted, lowers)
    inverses = [jnp.where(lane % BASE == sub, 1.0, 0.0).astype(F32) for _ in lowers]
    for step in range(BASE - 1):
        factors = each(
            lambda compact: jnp.take_along_axis(compact, block_of * BASE + step, axis=1), compacts
        )
        inverses = each(lambda inv, factor: inv - factor * inv[step : step + 1, :], inverses, factors)
    rows_of = each(lambda inv: [jnp.where(block_of == block, inv, 0.0) for block in blocks], inverses)
    width = BASE
    while width < size:
        pairs = range(size // (2 * width))
        per = width // BASE
        lane_w = lax.broadcasted_iota(jnp.int32, (width, size), 1) // width
        empty = jnp.zeros((width, size), F32)

        def picked(lower):
            return jnp.concatenate(
                [
                    jnp.where(
                        lane_w == 2 * p, lower[(2 * p + 1) * width : (2 * p + 2) * width, :], 0.0
                    )
                    for p in pairs
                ],
                axis=0,
            )

        def spread(inner):
            return jnp.concatenate(
                [x for p in pairs for x in (empty, inner[p * width : (p + 1) * width, :])], axis=0
            )

        halves = each(lambda rows: split(jnp.concatenate(rows, axis=0)), rows_of)
        picks = each(lambda lower: split(picked(lower)), lowers)
        inners = each(mxu3, picks, halves)
        belows = each(
            lambda rows: jnp.concatenate(
                [rows[(2 * p + 1) * per + i] for p in pairs for i in range(per)], axis=0
            ),
            rows_of,
        )
        joins = each(
            lambda below, inner: below - mxu3(split(below), split(spread(inner))), belows, inners
        )

        def placed(rows, joined):
            rows = list(rows)
            for p in pairs:
                for i in range(per):
                    at = (p * per + i) * BASE
                    rows[(2 * p + 1) * per + i] = joined[at : at + BASE, :]
            return rows

        rows_of = each(placed, rows_of, joins)
        width *= 2
    return each(lambda rows: split(jnp.concatenate(rows, axis=0)), rows_of)


def chunk_kernel(group, first, q_ref, k_ref, v_ref, b_ref, *refs):
    if first:
        oe_ref, end_ref, state = refs
    else:
        start_ref, oe_ref, s_ref, sent_ref, p_ref, state = refs
    chunk = pl.program_id(0)
    tokens = CHUNK // REFL

    @pl.when(chunk == 0)
    def _():
        lane = lax.broadcasted_iota(jnp.int32, (DK, 2 * DK), 1)
        sub = lax.broadcasted_iota(jnp.int32, (DK, 2 * DK), 0)
        start = jnp.where(lane == sub + DK, 1.0, 0.0).astype(F32)
        for head in range(group):
            state[head] = start if first else start_ref[head]

    below = lax.broadcasted_iota(jnp.int32, (CHUNK, CHUNK), 0) > lax.broadcasted_iota(
        jnp.int32, (CHUNK, CHUNK), 1
    )
    reach = REFL * lax.broadcasted_iota(jnp.int32, (tokens, CHUNK), 0) + (
        REFL - 1
    ) >= lax.broadcasted_iota(jnp.int32, (tokens, CHUNK), 1)
    heads = range(group)
    cols = [slice(head * DK, (head + 1) * DK) for head in heads]
    ks = [k_ref[:, :, c].reshape(CHUNK, DK) for c in cols]
    qs = [q_ref[:, c] for c in cols]

    def inverse_norm(rows):
        rows = rows.astype(F32)
        return lax.rsqrt(jnp.sum(rows * rows, axis=-1, keepdims=True) + TINY)

    k_scales = each(inverse_norm, ks)
    q_scales = each(inverse_norm, qs)
    rates = [b_ref[:, head : head + 1] * k_scales[head] for head in heads]
    rates2 = each(lambda rate, scale: rate * scale, rates, k_scales)
    kqs = each(lambda k, q: jnp.concatenate([k, q], axis=0), ks, qs)
    grams = each(mxu_nt, kqs, ks)
    lowers = each(lambda rate, gram: jnp.where(below, rate * gram[:CHUNK], 0.0), rates2, grams)
    scores = each(lambda gram: jnp.where(reach, gram[CHUNK:], 0.0).astype(BF16), grams)
    inverses = unit_lower_inverse(lowers)
    nows = [state[head] for head in heads]
    seens = each(
        lambda kq, now: mxu(
            jnp.concatenate([kq, kq], axis=1), jnp.concatenate(split(now), axis=0)
        ),
        kqs,
        nows,
    )

    def right_side(head):
        scaled = rates2[head] * seens[head][:CHUNK]
        own = rates[head] * v_ref[:, :, cols[head]].reshape(CHUNK, DK).astype(F32)
        return split(jnp.concatenate([own - scaled[:, :DK], -scaled[:, DK:]], axis=1))

    rights = each(right_side, heads)
    deltas = each(lambda inverse, right: split(mxu3(inverse, right)), inverses, rights)

    def stepped(k, now, delta):
        k_t = k.astype(F32).T.astype(BF16)
        return now + mxu(jnp.concatenate([k_t, k_t], axis=1), jnp.concatenate(delta, axis=0))

    nexts = each(stepped, ks, nows, deltas)
    outs = each(
        lambda scale, seen, score, delta: scale * (seen[CHUNK:] + mxu(score, delta[0])),
        q_scales,
        seens,
        scores,
        deltas,
    )
    for head in heads:
        state[head] = nexts[head]
        oe_ref[:, cols[head]] = outs[head][:, :DK].astype(BF16)
        oe_ref[:, slice((group + head) * DK, (group + head + 1) * DK)] = outs[head][:, DK:].astype(
            BF16
        )

    @pl.when(chunk == pl.num_programs(0) - 1)
    def _():
        for head in heads:
            if first:
                end_ref[head] = nexts[head]
            else:
                s_ref[head] = nexts[head][:, :DK]
                sent_ref[head] = nexts[head][:, :DK].astype(BF16)
                p_ref[head] = nexts[head][:, DK:].astype(BF16)


def local_part(queries, keys, values, beta, skip, steps, start=None):
    tokens, width = queries.shape
    group = width // DK
    tile = CHUNK // REFL
    first = start is None
    refl = pl.BlockSpec((tile, REFL, width), lambda c: (c + skip, 0, 0))
    whole = pl.BlockSpec((group, DK, 2 * DK), lambda c: (0, 0, 0))
    square = pl.BlockSpec((group, DK, DK), lambda c: (0, 0, 0))
    rows = jax.ShapeDtypeStruct((steps * tile, 2 * width), BF16)
    return pl.pallas_call(
        functools.partial(chunk_kernel, group, first),
        grid=(steps,),
        in_specs=[
            pl.BlockSpec((tile, width), lambda c: (c + skip, 0)),
            refl,
            refl,
            pl.BlockSpec((CHUNK, group), lambda c: (c + skip, 0)),
        ]
        + ([] if first else [whole]),
        out_specs=[pl.BlockSpec((tile, 2 * width), lambda c: (c, 0))]
        + ([whole] if first else [square] * 3),
        out_shape=[rows]
        + (
            [jax.ShapeDtypeStruct((group, DK, 2 * DK), F32)]
            if first
            else [
                jax.ShapeDtypeStruct((group, DK, DK), F32),
                jax.ShapeDtypeStruct((group, DK, DK), BF16),
                jax.ShapeDtypeStruct((group, DK, DK), BF16),
            ]
        ),
        scratch_shapes=[pltpu.VMEM((group, DK, 2 * DK), F32)],
        compiler_params=pltpu.CompilerParams(vmem_limit_bytes=56 * 1024 * 1024),
        cost_estimate=pl.CostEstimate(
            flops=400 * steps * tile * width * DK, bytes_accessed=16 * steps * tile * width, transcendentals=0
        ),
        name="local_part",
    )(queries, keys, values, beta, *([] if first else [start]))


def norm_kernel(first_ref, second_ref, s_ref, g_ref, out_ref):
    group = s_ref.shape[0]
    heads = range(group)
    cols = [slice(head * DK, (head + 1) * DK) for head in heads]
    for half, oe_ref in enumerate((first_ref, second_ref)):
        tile = oe_ref.shape[0] // 2
        for at in range(0, oe_ref.shape[0], tile):
            rows = slice(at, at + tile)
            to = slice(half * first_ref.shape[0] + at, half * first_ref.shape[0] + at + tile)
            seen = [
                mxu(oe_ref[rows, (group + head) * DK : (group + head + 1) * DK], s_ref[head])
                for head in heads
            ]
            readouts = [oe_ref[rows, cols[head]].astype(F32) + seen[head] for head in heads]
            scales = each(
                lambda x: lax.rsqrt(jnp.mean(x * x, axis=-1, keepdims=True) + TINY), readouts
            )
            for head in heads:
                out_ref[to, cols[head]] = (
                    readouts[head] * scales[head] * g_ref[:, cols[head]]
                ).astype(BF16)


def normed_rows(first, second, incoming, gain):
    width = gain.shape[0]
    tokens = first.shape[0] + second.shape[0]
    return pl.pallas_call(
        norm_kernel,
        in_specs=[pl.BlockSpec(memory_space=pltpu.VMEM)] * 4,
        out_specs=pl.BlockSpec(memory_space=pltpu.VMEM),
        out_shape=jax.ShapeDtypeStruct((tokens, width), BF16),
        compiler_params=pltpu.CompilerParams(vmem_limit_bytes=GRANT),
        name="normed_rows",
    )(first, second, incoming, gain.reshape(1, width))


def project_kernel(options, rows_count, ready, place_ref, first_ref, *refs):
    rows, refs = refs[:rows_count], refs[rows_count:]
    done, refs = refs[:ready], refs[ready:]
    *weights, held, sems = refs[: -2 - rows_count] + refs[-2:]
    outs = refs[-2 - rows_count : -2]
    whole = weights[0]

    def fetch(slot, pieces):
        at = 0
        for piece in pieces:
            to = held.at[slot, pl.ds(at, piece.shape[0])]
            pltpu.make_async_copy(piece, to, sems.at[slot]).start()
            at += piece.shape[0]

    for slot, counts in enumerate(options):
        for option, pieces in enumerate(counts):
            taken, weights = weights[:pieces], weights[pieces:]
            if len(counts) == 1:
                fetch(slot, taken)
            else:
                pl.when(first_ref[slot] == 1 - option)(functools.partial(fetch, slot, taken))
    for blocks, out in zip(done, outs):
        for block in range(blocks.shape[0]):
            out[place_ref[len(options) + block]] = blocks[block]
    for slot in range(len(options)):
        pltpu.make_async_copy(whole, held.at[slot], sems.at[slot]).wait()
        for row, out in zip(rows, outs):
            out[place_ref[slot]] = mxu(row[...], held[slot]).astype(BF16)


def project(places, first, rows, weights, done=()):
    tokens, depth = rows[0].shape
    block = weights[0][0][0].shape[1]
    count = len(weights)
    flat = [piece for options in weights for pieces in options for piece in pieces]
    vmem = pl.BlockSpec(memory_space=pltpu.VMEM)
    return pl.pallas_call(
        functools.partial(
            project_kernel,
            tuple(tuple(len(pieces) for pieces in options) for options in weights),
            len(rows),
            len(done),
        ),
        in_specs=[pl.BlockSpec(memory_space=pltpu.SMEM)] * 2
        + [vmem] * (len(rows) + len(done))
        + [pl.BlockSpec(memory_space=pl.ANY)] * len(flat),
        out_specs=[vmem] * len(rows),
        out_shape=[jax.ShapeDtypeStruct((places.shape[0], tokens, block), BF16)] * len(rows),
        scratch_shapes=[
            pltpu.VMEM((count, depth, block), BF16),
            pltpu.SemaphoreType.DMA((count,)),
        ],
        compiler_params=pltpu.CompilerParams(vmem_limit_bytes=GRANT),
        name="project",
    )(places, first, *rows, *done, *flat)


def halving_order(count):
    order = [0]
    bit = count // 2
    while bit >= 1:
        order = [m | bit for m in order] + order
        bit //= 2
    return order


def head_pairs(bit):
    return [(i, i ^ bit) for i in range(lax.axis_size("head"))]


def head_halved(parts):
    bit, give, keep = 1, parts[: parts.shape[0] // 2], parts[parts.shape[0] // 2 :]
    while bit * 2 < lax.axis_size("head"):
        got = lax.ppermute(give, "head", head_pairs(bit))
        half = keep.shape[0] // 2
        give = summed(keep[:half], got[:half])
        keep = keep[half:].astype(F32) + got[half:].astype(F32)
        bit *= 2
    return give[0], keep[0]


def summed(keep, got):
    return (keep.astype(F32) + got.astype(F32)).astype(BF16)


def send(value, axis, pairs):
    return lax.ppermute(value, axis, pairs)


def per_device(queries, keys, values, beta, gain, w_out):
    tokens, width = queries.shape
    heads = width // DK
    ctx, head = lax.axis_size("ctx"), lax.axis_size("head")
    here, side = lax.axis_index("ctx"), lax.axis_index("groups")
    beta_rows = beta.transpose(2, 0, 1).reshape(tokens * REFL, heads)
    half_cols = w_out.shape[1] // 2
    own = lax.dynamic_slice_in_dim(w_out, side * half_cols, half_cols, 1)
    ring = ctx == head and ctx == 4
    up, down = {0: own}, {0: own}

    def pass_up(step):
        up[step] = send(up[step - 1], "ctx", [(i, i + 1) for i in range(step - 1, ctx - 1)])

    def pass_down(step):
        down[step] = send(down[step - 1], "ctx", [(i + 1, i) for i in range(ctx - step)])

    if ring:
        pass_up(1)
        pass_down(1)
    swap = [(0, 1), (1, 0)]
    steps = tokens * REFL // CHUNK
    early = steps * 5 // 8
    near, middle = local_part(queries, keys, values, beta_rows, 0, early)
    if ring:
        up[1], down[1], middle = tied(up[1], down[1], middle)
        pass_up(2)
        pass_down(2)
    near_other = send(near, "groups", swap)
    far, state_end, outgoing, total_end = local_part(
        queries, keys, values, beta_rows, early, steps - early, middle
    )
    far_other = send(far, "groups", swap)

    incoming = jnp.zeros((heads, DK, DK), BF16)
    for hop in range(ctx - 1):
        if hop == 1 and ring:
            ahead = up[2].shape[0] // 4
            last = [(i, i + 1) for i in range(2, ctx - 1)]
            up_first = send(up[2][:ahead], "ctx", last)
        if hop == 2 and ring:
            up_first, down[2], near_other, outgoing = tied(up_first, down[2], near_other, outgoing)
        incoming = incoming + send(outgoing, "ctx", [(hop, hop + 1)])
        outgoing = (
            jnp.einsum("hde,hef->hdf", total_end, incoming, preferred_element_type=F32) + state_end
        ).astype(BF16)
    if ring:
        pass_down(3)
        up_rest, incoming = tied(up[2][ahead:], incoming)
        up[3] = [up_first, send(up_rest, "ctx", last)]
        weights = [([up[1]], [down[3]]), ([down[1]], up[3]), ([own],), ([up[2]], [down[2]])]
        slots = jnp.asarray([1, 3, 0, 2], jnp.int32)
        targets = lax.rem(here + ctx - slots, ctx)
        first = jnp.where(slots == 3, here < 3, here >= slots).astype(jnp.int32)
    else:
        whole = lax.all_gather(own, "ctx", axis=1, tiled=True)
        weights = [([w],) for w in jnp.split(whole, head, axis=1)]
        targets = jnp.arange(head)
        first = jnp.ones((head,), jnp.int32)
    far_other, incoming = tied(far_other, incoming)
    incoming_other = send(incoming, "groups", swap)
    mine = normed_rows(near, far, incoming, gain)
    other = normed_rows(near_other, far_other, incoming_other, gain)
    distance = targets ^ lax.axis_index("head")
    order = jnp.asarray(halving_order(head), jnp.int32)
    places = jnp.argmax(distance[:, None] == order[None, :], axis=1).astype(jnp.int32)
    mine, other = tied(mine, other)
    if ring:
        pair = jnp.arange(2, dtype=jnp.int32)
        other_done, mine_done = project(pair, first[2:], [other, mine], weights[2:])
        (other_parts,) = project(places, first[:2], [other], weights[:2], [other_done])
        (parts,) = project(places, first[:2], [mine], weights[:2], [mine_done])
    else:
        other_parts, parts = project(places, first, [other, mine], weights)
    give, keep = head_halved(other_parts)
    own_give, own_keep = head_halved(parts)
    last_pairs = head_pairs(head // 2)
    give_a, give_b = jnp.split(give, 2)
    keep_a, keep_b = jnp.split(keep, 2)
    got_a = send(give_a, "head", last_pairs)
    give_b, own_give = tied(give_b, own_give)
    got_b = send(give_b, "head", last_pairs)
    got_a, own_give = tied(got_a, own_give)
    back_a = send(summed(keep_a, got_a), "groups", swap)
    own_got = send(own_give, "head", last_pairs)
    back_a, got_b, keep_b = tied(back_a, got_b, keep_b)
    back_b = send(summed(keep_b, got_b), "groups", swap)
    mine_sum = summed(own_keep, own_got)
    back = jnp.concatenate([back_a, back_b], axis=0)
    blocks = mine_sum.shape[1] // half_cols
    if blocks == 1:
        return jnp.where(
            side == 0,
            jnp.concatenate([mine_sum, back], axis=1),
            jnp.concatenate([back, mine_sum], axis=1),
        )
    mine_sum = mine_sum.reshape(tokens, blocks, 1, half_cols)
    back = back.reshape(tokens, blocks, 1, half_cols)
    mixed = jnp.where(
        side == 0,
        jnp.concatenate([mine_sum, back], axis=2),
        jnp.concatenate([back, mine_sum], axis=2),
    )
    return mixed.reshape(tokens, blocks * 2 * half_cols)


def solution(mesh):
    in_specs = (
        P(("groups", "ctx"), "head"),
        P(("groups", "ctx"), None, "head"),
        P(("groups", "ctx"), None, "head"),
        P(None, "head", ("groups", "ctx")),
        P("head"),
        P("head", "ctx"),
    )
    out_specs = P(("groups", "ctx"), "head")
    return jax.shard_map(
        per_device, mesh=mesh, in_specs=in_specs, out_specs=out_specs, check_vma=False
    )
```
